32 devices in a mesh: dp: 8 (over z, x), fsdp: 4 (over y, core).
Axes of the slice: x: 2, y: 2, z: 4, core: 2. Of those that a mesh axis runs over, the one named last changes fastest.
Arguments:
- tokens: bfloat16 [65536, 512], P(('dp', 'fsdp')), may hold values from -6 to 6
- mask_flags: int32 [65536], P(('dp', 'fsdp')), may hold values 0 or 1
- timesteps: int32 [65536], P(('dp', 'fsdp')), may hold values from 0 to 255
- segment_ids: int32 [32, 2048], P(('dp', 'fsdp')), may hold values from 0 to 3, never falling along the last dimension, each value on 1 to 1024 neighbouring positions
- mask_embed: bfloat16 [512], P(('dp', 'fsdp')), may hold values from -6 to 6
- time_table: bfloat16 [256, 512], P(('dp', 'fsdp')), may hold values from -6 to 6
- first_gain: bfloat16 [512], P(('dp', 'fsdp')), may hold values from 0.099609375 to 1.8984375
- first_bias: bfloat16 [512], P(('dp', 'fsdp')), may hold values from -4 to 4
- input_proj: bfloat16 [512, 1536], P(('dp', 'fsdp')), may hold values from -0.25 to 0.25
- output_proj: bfloat16 [512, 512], P(('dp', 'fsdp')), may hold values from -2 to 2
- output_bias: bfloat16 [512], P(('dp', 'fsdp')), may hold values from -4 to 4
- second_gain: bfloat16 [512], P(('dp', 'fsdp')), may hold values from 0.099609375 to 1.8984375
- second_bias: bfloat16 [512], P(('dp', 'fsdp')), may hold values from -4 to 4
- hidden_weight: bfloat16 [512, 2048], P(('dp', 'fsdp')), may hold values from -0.25 to 0.25
- hidden_bias: bfloat16 [2048], P(('dp', 'fsdp')), may hold values from -6 to 6
- down_weight: bfloat16 [2048, 512], P(('dp', 'fsdp')), may hold values from -0.125 to 0.125
- down_bias: bfloat16 [512], P(('dp', 'fsdp')), may hold values from -4 to 4
- cotangent: float32 [65536, 512], P(('dp', 'fsdp')), may hold values from -6 to 6
Outputs:
- out_tokens: bfloat16 [65536, 512], P(('dp', 'fsdp'))
- grad_tokens: float32 [65536, 512], P(('dp', 'fsdp'))
- grad_mask_embed: float32 [512], P(('dp', 'fsdp'))
- grad_time_table: float32 [256, 512], P(('dp', 'fsdp'))
- grad_first_gain: float32 [512], P(('dp', 'fsdp'))
- grad_first_bias: float32 [512], P(('dp', 'fsdp'))
- grad_input_proj: float32 [512, 1536], P(('dp', 'fsdp'))
- grad_output_proj: float32 [512, 512], P(('dp', 'fsdp'))
- grad_output_bias: float32 [512], P(('dp', 'fsdp'))
- grad_second_gain: float32 [512], P(('dp', 'fsdp'))
- grad_second_bias: float32 [512], P(('dp', 'fsdp'))
- grad_hidden_weight: float32 [512, 2048], P(('dp', 'fsdp'))
- grad_hidden_bias: float32 [2048], P(('dp', 'fsdp'))
- grad_down_weight: float32 [2048, 512], P(('dp', 'fsdp'))
- grad_down_bias: float32 [512], P(('dp', 'fsdp'))
The draws below stay inside these ranges and needn't reach their ends.
Inputs may be any that keep to these rules, and one draw needn't show every extreme that they name: `segment_ids`: along each packed row the segment ids never fall, and each segment holds 1 to half of 2048 positions; one holds exactly that many.
All inputs are finite; a program needn't handle non-finite values. No bound on the sum of `mask_flags` on one device may be relied on, other than what follows from the above.
Results may differ from the reference program's by a relative error of at most 0.011.
Values may be sent and summed in bfloat16 or wider, within the bound.
A program may use at most 256 MiB of HBM per device.

```python
import math
import jax
import jax.numpy as jnp
import numpy as np
from jax import lax

D = 512
HEADS = 8
HD = 64
FF = 2048
TIMESTEPS = 256
LENGTH = 2048
SEGMENTS = 4
ROWS = 32
TOKENS = 65536


def with_ends(entries, rng, least, top_value):
    longest = entries.shape.index(max(entries.shape))
    spots = []
    for shift in (0, 1):
        where = [jax.random.randint(jax.random.fold_in(rng, axis), (), 0, length) for axis, length in enumerate(entries.shape)]
        where[longest] = (where[longest] + shift) % entries.shape[longest]
        spots.append(tuple(where))
    return entries.at[spots[0]].set(least).at[spots[1]].set(top_value)


def level_of(own_key, shape, pieces, low, high):
    level = 1.0
    for axis_at, blocks in pieces:
        steps = jax.random.uniform(jax.random.fold_in(jax.random.fold_in(own_key, 6), axis_at), (blocks,), jnp.float32, low / len(pieces), high / len(pieces))
        level = level * jnp.repeat(jnp.exp(steps), shape[axis_at] // blocks).reshape((-1,) + (1,) * (len(shape) - 1 - axis_at))
    return level


def split_up(amount, total, reach, skew):
    portions = [(1 << 20) // math.isqrt(standing ** skew) + 1 for standing in range(2, amount + 1)]
    surplus, given = total - reach - (amount - 1), [1] * (amount - 1)
    while surplus > 0:
        movable = [i for i in range(amount - 1) if given[i] < reach]
        whole, budget = sum([portions[i] for i in movable]), surplus
        for i in movable:
            more = min(reach - given[i], max(1, budget * portions[i] // whole), surplus)
            given[i] = given[i] + more
            surplus = surplus - more
    return np.array([reach] + given)


def ragged_sizes(stream_key, number_of, total, most, lean):
    if number_of == 2:
        one = jax.random.randint(stream_key, (), max(1, total - most), min(most, total - 1) + 1)
        return jnp.stack([one, total - one])
    sizes = jnp.asarray(split_up(number_of, total, most, lean), jnp.int32)
    couples = (number_of - 1) // 2
    donor, taker = sizes[1:1 + 2 * couples:2], sizes[2:2 + 2 * couples:2]
    room = jnp.minimum(donor - 1, most - taker)
    passed = jax.random.randint(jax.random.fold_in(stream_key, 1), (couples,), 0, 1 << 20) % (room + 1)
    sizes = sizes.at[1:1 + 2 * couples:2].set(donor - passed).at[2:2 + 2 * couples:2].set(taker + passed)
    return sizes[jax.random.permutation(jax.random.fold_in(stream_key, 2), number_of)]


def noise(rng, dims, scale, limit, split=(), kind=jnp.bfloat16):
    values = scale * jax.random.normal(rng, dims, jnp.float32)
    if split:
        values = values * level_of(rng, dims, split, -0.22, 0.18)
    return jnp.clip(values, -limit, limit).astype(kind)


def setup_inputs(seed: int = 0) -> dict:
    seeds = jax.random.split(jax.random.key(seed), 19)
    tokens = noise(seeds[0], (TOKENS, D), 1.0, 6.0, ((0, 32),))
    mask_flags = with_ends((jax.random.randint(seeds[1], (TOKENS,), 0, 2) < 1).astype(jnp.int32), jax.random.fold_in(seeds[1], 1), 0, 1)
    timesteps = with_ends(jax.random.randint(seeds[2], (TOKENS,), 0, TIMESTEPS), jax.random.fold_in(seeds[2], 1), 0, TIMESTEPS - 1).astype(jnp.int32)
    segment_ids = jax.vmap(lambda own: jnp.searchsorted(jnp.cumsum(ragged_sizes(own, SEGMENTS, LENGTH, LENGTH // 2, 0)), jnp.arange(LENGTH), side="right"))(jax.random.split(seeds[3], ROWS)).reshape((ROWS, LENGTH)).astype(jnp.int32)
    mask_embed = noise(seeds[4], (D,), 1.0, 6.0, ((0, 32),))
    time_table = noise(seeds[5], (TIMESTEPS, D), 0.5, 6.0, ((0, 32),))
    first_gain = jnp.clip(1.0 + 0.18 * jax.random.normal(seeds[6], (D,), jnp.float32), 0.099609375, 1.8984375).astype(jnp.bfloat16)
    first_bias = noise(seeds[7], (D,), 0.3, 4.0, ((0, 32),))
    input_proj = noise(seeds[8], (D, 3 * D), D ** -0.5, 0.25, ((0, 32),))
    output_proj = noise(seeds[9], (D, D), (D // 64) ** -0.5, 2.0, ((0, 32),))
    output_bias = noise(seeds[10], (D,), 0.3, 4.0, ((0, 32),))
    second_gain = jnp.clip(1.0 + 0.18 * jax.random.normal(seeds[11], (D,), jnp.float32), 0.099609375, 1.8984375).astype(jnp.bfloat16)
    second_bias = noise(seeds[12], (D,), 0.3, 4.0, ((0, 32),))
    hidden_weight = noise(seeds[13], (D, FF), D ** -0.5, 0.25, ((0, 32),))
    hidden_bias = noise(seeds[14], (FF,), 0.5, 6.0, ((0, 32),))
    down_weight = noise(seeds[15], (FF, D), FF ** -0.5, 0.125, ((0, 32),))
    down_bias = noise(seeds[16], (D,), 0.3, 4.0, ((0, 32),))
    cotangent = noise(seeds[17], (TOKENS, D), 1.0, 6.0, ((0, 32),), jnp.float32)
    return dict(tokens=tokens, mask_flags=mask_flags, timesteps=timesteps, segment_ids=segment_ids, mask_embed=mask_embed, time_table=time_table, first_gain=first_gain, first_bias=first_bias, input_proj=input_proj, output_proj=output_proj, output_bias=output_bias, second_gain=second_gain, second_bias=second_bias, hidden_weight=hidden_weight, hidden_bias=hidden_bias, down_weight=down_weight, down_bias=down_bias, cotangent=cotangent)


@jax.custom_vjp
def low(v):
    return lax.optimization_barrier(v.astype(jnp.bfloat16)).astype(jnp.float32)

@jax.custom_vjp
def low_back(v):
    return v

def low_keep(v):
    return (low(v), None)

def low_pass(kept, grad):
    return (grad,)

def back_keep(v):
    return (v, None)

def back_low(kept, grad):
    return (low(grad),)
low.defvjp(low_keep, low_pass)
low_back.defvjp(back_keep, back_low)
EPSILON = 1e-05

def product(left, right):
    return jnp.dot(left, right, precision=lax.Precision.HIGHEST, preferred_element_type=jnp.float32)

def layer_norm(hidden, gain, bias):
    average = lax.optimization_barrier(jnp.mean(hidden, axis=-1, keepdims=True))
    centered = hidden - average
    spread = lax.optimization_barrier(jnp.mean(centered * centered, axis=-1, keepdims=True))
    return centered * lax.rsqrt(spread + EPSILON) * gain + bias

def attend_row(inputs):
    packed_row, row_ids = inputs
    queries = packed_row[:, 0]
    key_rows = packed_row[:, 1]
    value_rows = packed_row[:, 2]
    scores = low_back(jnp.einsum('qhc,khc->hqk', queries, key_rows, precision=lax.Precision.HIGHEST) * HD ** (-0.5))
    same_doc = row_ids[:, None] == row_ids[None, :]
    scores = jnp.where(same_doc[None], scores, -1e+30)
    highest = lax.optimization_barrier(jnp.max(scores, axis=-1, keepdims=True))
    weights = jnp.exp(scores - highest)
    weights = weights / lax.optimization_barrier(jnp.sum(weights, axis=-1, keepdims=True))
    mixture = jnp.einsum('hqk,khc->qhc', low(weights), value_rows, precision=lax.Precision.HIGHEST)
    return mixture.reshape(LENGTH, HEADS * HD)

def reference(tokens, mask_flags, timesteps, segment_ids, mask_embed, time_table, first_gain, first_bias, input_proj, output_proj, output_bias, second_gain, second_bias, hidden_weight, hidden_bias, down_weight, down_bias, cotangent):
    selector = (timesteps[:, None] == jnp.arange(TIMESTEPS, dtype=jnp.int32)[None, :]).astype(jnp.float32)
    flag_column = mask_flags.astype(jnp.float32)[:, None]
    floats = tuple((member.astype(jnp.float32) for member in (tokens, mask_embed, time_table, first_gain, first_bias, input_proj, output_proj, output_bias, second_gain, second_bias, hidden_weight, hidden_bias, down_weight, down_bias)))

    def forward(tokens, mask_embed, time_table, first_gain, first_bias, input_proj, output_proj, output_bias, second_gain, second_bias, hidden_weight, hidden_bias, down_weight, down_bias):
        start = tokens + flag_column * mask_embed[None, :] + product(selector, time_table)
        normed = low(layer_norm(start, first_gain, first_bias))
        packed = low(low_back(product(normed, input_proj)))
        layered = packed.reshape(ROWS, LENGTH, 3, HEADS, HD)
        mixture = lax.map(jax.checkpoint(attend_row), (layered, segment_ids))
        mixture = low(low_back(mixture.reshape(TOKENS, HEADS * HD)))
        middle = start + low_back(product(mixture, output_proj) + output_bias[None, :])
        normed_two = low(layer_norm(middle, second_gain, second_bias))
        pre_act = low_back(product(normed_two, hidden_weight) + hidden_bias[None, :])
        activated = low(jax.nn.gelu(pre_act, approximate=False))
        return middle + low_back(product(activated, down_weight) + down_bias[None, :])
    result, pullback = jax.vjp(forward, *floats)
    gradients = pullback(cotangent.astype(jnp.float32))
    return (result.astype(jnp.bfloat16), gradients[0], gradients[1], gradients[2], gradients[3], gradients[4], gradients[5], gradients[6], gradients[7], gradients[8], gradients[9], gradients[10], gradients[11], gradients[12], gradients[13])
```

```python
import functools

import jax
import jax.numpy as jnp
from jax import lax
from jax.experimental import pallas as pl
from jax.experimental.pallas import tpu as pltpu
from jax.sharding import PartitionSpec as P

F32, BF16 = jnp.float32, jnp.bfloat16
HD = 64
SCALE = HD ** -0.5
NEG = -1e30
EPSILON = 1e-05
AXES = ("dp", "fsdp")
MESH = pl.DeviceIdType.MESH
VMEM_BYTES = 58 << 20
SMALL_ROWS = 16
TILE = 512


def dot(a, b):
    return jnp.dot(a, b, preferred_element_type=F32)


def dot_nt(a, b):
    return lax.dot_general(a, b, (((1,), (1,)), ((), ())), preferred_element_type=F32)


def dot_tn(a, b):
    return lax.dot_general(a, b, (((0,), (0,)), ((), ())), preferred_element_type=F32)


def iota(shape, dim):
    return lax.broadcasted_iota(jnp.int32, shape, dim)


def params(**more):
    return pltpu.CompilerParams(vmem_limit_bytes=VMEM_BYTES, **more)


def norm_parts(h):
    centered = h - jnp.mean(h, axis=-1, keepdims=True)
    rstd = lax.rsqrt(jnp.mean(centered * centered, axis=-1, keepdims=True) + EPSILON)
    return centered * rstd, rstd


def norm_back(n, xhat, rstd, gain):
    ng = n * gain
    first = jnp.mean(ng, axis=-1, keepdims=True)
    second = jnp.mean(ng * xhat, axis=-1, keepdims=True)
    return rstd * (ng - first - xhat * second)


def embed_kernel(tok, ids, small, w_in, start_o, normt_o, packed_o, mq_o, mk_o, vec_o, hid_o, table):
    width = tok.shape[1]
    devices = small.shape[0]
    steps = devices * 8

    @pl.when(pl.program_id(0) == 0)
    def _():
        flat = small[...].astype(F32)
        row = flat[:, 8, :].astype(BF16)
        per = width // devices
        lane = iota((devices, width), 1)
        spread = jnp.concatenate(
            [jnp.where(lane // per == i, row, jnp.zeros_like(row)) for i in range(7)], 0
        )
        same = (iota((width, width), 0) % per == iota((width, width), 1) % per).astype(BF16)
        wide = dot(spread, same).reshape(7, devices, width)
        mine = (lane // per == iota((devices, width), 0))[None]
        vecs = jnp.sum(jnp.where(mine, wide, 0.0), axis=1)
        vec_o[...] = jnp.concatenate([vecs, jnp.zeros((1, width), F32)], 0)
        hidden = hid_o.shape[1]
        part = hidden // devices
        at = iota((width, hidden), 0) - 7 * per
        pick = (at == iota((width, hidden), 1) % part).astype(BF16)
        own = iota((devices, hidden), 1) // part == iota((devices, hidden), 0)
        hid_o[...] = jnp.sum(jnp.where(own, dot(row, pick), 0.0), axis=0, keepdims=True)
        table[:steps, :] = flat[:, :8, :].reshape(steps, width).astype(BF16)
        table[steps:, :] = jnp.where(
            iota((16, width), 0) == 0, vecs[0:1], 0.0
        ).astype(BF16)

    rows = tok.shape[0]
    select = token_selector(ids, steps, rows)
    start = tok[...].astype(F32) + dot_tn(select, table[...])
    start_o[...] = start
    xhat, _ = norm_parts(start)
    normed = (xhat * vec_o[1:2, :] + vec_o[2:3, :]).astype(BF16)
    normt_o[...] = jnp.transpose(normed, (1, 0))
    packed_o[...] = dot(normed, w_in[...]).astype(BF16)
    member = jnp.transpose((ids[2:3, :] == iota((128, rows), 0)).astype(F32), (1, 0))
    mq_o[...] = member.astype(BF16)
    mk_o[...] = jnp.where(iota((rows, 128), 1) < 4, (1.0 - member) * NEG, 0.0).astype(BF16)


def token_selector(ids, steps, rows):
    stamps = (ids[0:1, :] == iota((steps, rows), 0)).astype(F32)
    flags = jnp.where(iota((16, rows), 0) == 0, ids[1:2, :].astype(F32), 0.0)
    return jnp.concatenate([stamps, flags], 0).astype(BF16)


def embed(tokens, ids, small, w_in, hidden):
    count, width = tokens.shape
    devices = small.shape[0]
    rows = min(TILE, count)
    tile = lambda w: pl.BlockSpec((rows, w), lambda i: (i, 0))
    whole = lambda a: pl.BlockSpec(a, lambda i: (0,) * len(a))
    return pl.pallas_call(
        embed_kernel,
        grid=(count // rows,),
        in_specs=[tile(width), pl.BlockSpec((8, rows), lambda i: (0, i)), whole(small.shape), whole(w_in.shape)],
        out_specs=[tile(width), pl.BlockSpec((width, rows), lambda i: (0, i)), tile(3 * width), tile(128), tile(128),
                   whole((8, width)), whole((1, hidden))],
        out_shape=[
            jax.ShapeDtypeStruct((count, width), F32),
            jax.ShapeDtypeStruct((width, count), BF16),
            jax.ShapeDtypeStruct((count, 3 * width), BF16),
            jax.ShapeDtypeStruct((count, 128), BF16),
            jax.ShapeDtypeStruct((count, 128), BF16),
            jax.ShapeDtypeStruct((8, width), F32),
            jax.ShapeDtypeStruct((1, hidden), F32),
        ],
        scratch_shapes=[pltpu.VMEM((devices * 8 + 16, width), BF16)],
        compiler_params=params(),
        name="embed_project",
    )(tokens, ids, small, w_in)


def gelu_parts(v):
    phi = 0.5 * lax.erf(v * 0.7071067811865476) + 0.5
    return v * phi, phi + v * (jnp.exp(v * v * -0.5) * 0.3989422804014327)


def feed_kernel(tiles, chunks, start, mix, cot, w_out, up, down, vec, hid,
                out_o, gmid_o, dmix_o, delta_o, gup_o, gdown_o, gout_o, gvec_o, ghid_o,
                mid, res, gn2, n2, n2t, br, brt, mixs, act0, act1, gpre0, gpre1, gup, gdt, gout):
    s = pl.program_id(0)
    t_rows = start.shape[0]
    f = act0.shape[1]
    half = tiles // 2
    middle_steps = chunks * half

    def rows_at(t):
        return pl.ds(pl.multiple_of(t * t_rows, t_rows), t_rows)

    def cols_at(c):
        return pl.ds(pl.multiple_of(c * f, f), f)

    @pl.when(s == 0)
    def _():
        for ref in (act1, gpre1, gup, gdt, gn2, gout, gvec_o, ghid_o):
            ref[...] = jnp.zeros_like(ref)

    @pl.when(s < tiles)
    def _():
        rows = rows_at(s)
        mixs[rows, :] = mix[...]
        middle = start[...] + dot(mix[...], w_out[...]) + vec[3:4, :]
        mid[rows, :] = middle
        res[rows, :] = middle + vec[6:7, :]
        xhat, _ = norm_parts(middle)
        normed = (xhat * vec[4:5, :] + vec[5:6, :]).astype(BF16)
        n2[rows, :] = normed
        n2t[:, rows] = jnp.transpose(normed, (1, 0))
        branch = cot[...].astype(BF16)
        br[rows, :] = branch
        brt[:, rows] = jnp.transpose(branch, (1, 0))
        gvec_o[3:4, :] += jnp.sum(branch.astype(F32), axis=0, keepdims=True)

    def inner(c, t, act, gpre):
        cols, rows = cols_at(c), rows_at(t)
        pre = dot(n2[rows, :], up[:, cols]) + hid[:, cols]
        grad = dot_nt(br[rows, :], down[cols, :])
        value, slope = gelu_parts(pre)
        act[...] = value.astype(BF16)
        low = (grad * slope).astype(BF16)
        gpre[...] = low
        ghid_o[:, cols] += jnp.sum(low.astype(F32), axis=0, keepdims=True)

    def outer(c, t, act, gpre):
        cols, rows = cols_at(c), rows_at(t)
        a, g = act[...], gpre[...]
        res[rows, :] += dot(a, down[cols, :])
        gn2[rows, :] += dot_nt(g, up[:, cols])
        gup[:, cols] += dot(n2t[:, rows], g)
        gdt[:, cols] += dot(brt[:, rows], a)

    @pl.when((s >= tiles) & (s < tiles + middle_steps))
    def _():
        b = s - tiles
        before = jnp.maximum(b - 1, 0)
        c, t = b // half, 2 * (b % half)
        outer(before // half, 2 * (before % half) + 1, act1, gpre1)
        inner(c, t, act0, gpre0)
        outer(c, t, act0, gpre0)
        inner(c, t + 1, act1, gpre1)

    @pl.when(s == tiles + middle_steps)
    def _():
        outer(chunks - 1, tiles - 1, act1, gpre1)
        for c in range(chunks):
            gup_o[:, c * f:(c + 1) * f] = gup[:, c * f:(c + 1) * f].astype(BF16)
            gdown_o[c * f:(c + 1) * f, :] = jnp.transpose(gdt[:, c * f:(c + 1) * f], (1, 0)).astype(BF16)

    @pl.when(s >= tiles + middle_steps)
    def _():
        rows = rows_at(s - tiles - middle_steps)
        out_o[...] = res[rows, :].astype(BF16)
        xhat, rstd = norm_parts(mid[rows, :])
        n = gn2[rows, :]
        grad = cot[...] + norm_back(n, xhat, rstd, vec[4:5, :])
        gmid_o[...] = grad
        low = grad.astype(BF16)
        gvec_o[0:1, :] += jnp.sum(low.astype(F32), axis=0, keepdims=True)
        gvec_o[1:2, :] += jnp.sum(n * xhat, axis=0, keepdims=True)
        gvec_o[2:3, :] += jnp.sum(n, axis=0, keepdims=True)
        mixed = mixs[rows, :]
        gout[...] += dot_tn(mixed, low)
        gout_o[...] = gout[...].astype(BF16)
        dmix = dot_nt(low, w_out[...]).astype(BF16)
        dmix_o[...] = dmix
        prod = dmix.astype(F32) * mixed.astype(F32)
        high = prod.astype(BF16)
        rest = (prod - high.astype(F32)).astype(BF16)
        heads = (iota((16, prod.shape[1]), 1) // HD == iota((16, prod.shape[1]), 0)).astype(BF16)
        delta_o[...] = (dot_nt(heads, high) + dot_nt(heads, rest))[:8]


def feed(start, mixture, cotangent, w_out, up, down, vec, hid):
    count, width = start.shape
    hidden = up.shape[1]
    rows = min(TILE, count)
    f = min(512, hidden)
    tiles, chunks = count // rows, hidden // f
    middle = chunks * (tiles // 2)
    first = lambda s: jnp.minimum(s, tiles - 1)
    last = lambda s: jnp.maximum(s - tiles - middle, 0)
    both = lambda s: jnp.where(s < tiles + middle, first(s), last(s))
    tile = lambda at: pl.BlockSpec((rows, width), lambda s: (at(s), 0))
    whole = lambda *a: pl.BlockSpec(a, lambda s: (0,) * len(a))
    big = lambda d: pltpu.VMEM((count, width), d)
    return pl.pallas_call(
        functools.partial(feed_kernel, tiles, chunks),
        grid=(tiles + middle + tiles,),
        in_specs=[tile(first), tile(first), tile(both), whole(width, width), whole(width, hidden), whole(hidden, width),
                  whole(8, width), whole(1, hidden)],
        out_specs=[tile(last), tile(last), tile(last), pl.BlockSpec((8, rows), lambda s: (0, last(s))),
                   whole(width, hidden), whole(hidden, width), whole(width, width), whole(8, width), whole(1, hidden)],
        out_shape=[
            jax.ShapeDtypeStruct((count, width), BF16),
            jax.ShapeDtypeStruct((count, width), F32),
            jax.ShapeDtypeStruct((count, width), BF16),
            jax.ShapeDtypeStruct((8, count), F32),
            jax.ShapeDtypeStruct((width, hidden), BF16),
            jax.ShapeDtypeStruct((hidden, width), BF16),
            jax.ShapeDtypeStruct((width, width), BF16),
            jax.ShapeDtypeStruct((8, width), F32),
            jax.ShapeDtypeStruct((1, hidden), F32),
        ],
        scratch_shapes=[big(F32), big(F32), big(F32), big(BF16), pltpu.VMEM((width, count), BF16), big(BF16),
                        pltpu.VMEM((width, count), BF16), big(BF16)]
        + [pltpu.VMEM((rows, f), BF16)] * 4
        + [pltpu.VMEM((width, hidden), F32)] * 2
        + [pltpu.VMEM((width, width), F32)],
        compiler_params=params(),
        name="feed_forward",
    )(start, mixture, cotangent, w_out, up, down, vec, hid)


def project_back_kernel(dq, dk, dv, normt, w_in, start, gmid, ids, vec, gvec2, ghid,
                        gtok_o, gin_o, gsmall_o, gtab_o, gvec_o, gin):
    width = start.shape[1]
    rows = start.shape[0]
    steps = gtab_o.shape[0] - 16

    @pl.when(pl.program_id(0) == 0)
    def _():
        for ref in (gin, gtab_o, gvec_o):
            ref[...] = jnp.zeros_like(ref)

    n = jnp.zeros((rows, width), F32)
    for i, d in enumerate((dq, dk, dv)):
        cols = slice(width * i, width * (i + 1))
        low = d[...]
        gin[:, cols] += dot(normt[...], low)
        n = n + dot_nt(low, w_in[:, cols])
    xhat, rstd = norm_parts(start[...])
    grad = gmid[...] + norm_back(n, xhat, rstd, vec[1:2, :])
    gtok_o[...] = grad
    gvec_o[0:1, :] += jnp.sum(n * xhat, axis=0, keepdims=True)
    gvec_o[1:2, :] += jnp.sum(n, axis=0, keepdims=True)
    gtab_o[...] += dot(token_selector(ids, steps, rows), grad.astype(BF16))

    @pl.when(pl.program_id(0) == pl.num_programs(0) - 1)
    def _():
        gin_o[...] = gin[...].astype(BF16)
        groups = steps // 8
        per = width // groups
        sums = [gtab_o[steps : steps + 1, :], gvec_o[0:1, :], gvec_o[1:2, :]]
        sums += [gvec2[i : i + 1, :] for i in range(4)]
        mine = iota((groups, width), 1) // per == iota((groups, width), 0)
        spread = jnp.concatenate([jnp.where(mine, v, 0.0) for v in sums], 0).astype(BF16)
        same = (iota((width, width), 0) % per == iota((width, width), 1) % per).astype(BF16)
        wide = dot(spread, same).reshape(7, groups, width)
        lane = iota((1, width), 1)
        row = jnp.zeros((groups, width), F32)
        for i in range(7):
            row = jnp.where(lane // per == i, wide[i], row)
        hidden = ghid.shape[1]
        part = hidden // groups
        own = iota((groups, hidden), 1) // part == iota((groups, hidden), 0)
        pick = (iota((hidden, width), 0) % part == iota((hidden, width), 1) - 7 * per).astype(BF16)
        row = row + dot(jnp.where(own, ghid[...], 0.0).astype(BF16), pick)
        table = gtab_o[:steps, :].reshape(groups, 8, width)
        below = jnp.where(iota((groups, 8, width), 1) == 0, row[:, None, :], 0.0)
        gsmall_o[...] = jnp.concatenate([table, below], 1).astype(BF16)


def project_back(dq, dk, dv, normt, w_in, start, gmid, ids, vec, gvec2, ghid, steps):
    count, width = start.shape
    rows = min(TILE, count)
    tile = pl.BlockSpec((rows, width), lambda i: (i, 0))
    whole = lambda *a: pl.BlockSpec(a, lambda i: (0,) * len(a))
    return pl.pallas_call(
        project_back_kernel,
        grid=(count // rows,),
        in_specs=[tile, tile, tile, pl.BlockSpec((width, rows), lambda i: (0, i)), whole(*w_in.shape), tile, tile,
                  pl.BlockSpec((8, rows), lambda i: (0, i)), whole(8, width), whole(8, width), whole(*ghid.shape)],
        out_specs=[tile, whole(width, 3 * width), whole(steps // 8, 16, width), whole(steps + 16, width), whole(8, width)],
        out_shape=[
            jax.ShapeDtypeStruct((count, width), F32),
            jax.ShapeDtypeStruct((width, 3 * width), BF16),
            jax.ShapeDtypeStruct((steps // 8, 16, width), BF16),
            jax.ShapeDtypeStruct((steps + 16, width), F32),
            jax.ShapeDtypeStruct((8, width), F32),
        ],
        scratch_shapes=[pltpu.VMEM((width, 3 * width), F32)],
        compiler_params=params(),
        name="project_back",
    )(dq, dk, dv, normt, w_in, start, gmid, ids, vec, gvec2, ghid)


FTQ, FTK, FNP = 256, 512, 2
BTQ, BTK, BNP = 256, 512, 2


def bounds(seg, length):
    def first_at_least(s):
        def step(_, lh):
            lo, hi = lh
            mid = (lo + hi) // 2
            below = seg[jnp.minimum(mid, length - 1)] < s
            live = lo < hi
            return (jnp.where(live & below, mid + 1, lo), jnp.where(live & ~below, mid, hi))
        lo, _ = lax.fori_loop(0, length.bit_length(), step, (jnp.int32(0), jnp.int32(length)))
        return lo
    return [jnp.int32(0)] + [first_at_least(s) for s in (1, 2, 3)] + [jnp.int32(length)]

def pick(vals, i):
    out = vals[0]
    for j in range(1, len(vals)):
        out = jnp.where(i == j, vals[j], out)
    return out

def key_range(seg, edges, row, rows):
    first, last = seg[row], seg[row + rows - 1]
    return pick(edges[:-1], first), pick(edges[1:], last)

def fwd_kernel(length, tq, tk, npair, seg, q_ref, k_ref, v_ref, mq_ref, mk_ref, o_ref, lse_ref, kx, vx, col):
    g = pl.program_id(0)
    steps = 4 // npair
    edges = bounds(seg, length)
    lane = lax.broadcasted_iota(jnp.int32, (1, 128), 1)
    head0 = (lane < 64)
    for i in range(npair):
        kx[i, :, :128] = k_ref[:, 128 * i:128 * i + 128]
        vx[i, :, :128] = v_ref[:, 128 * i:128 * i + 128]
    @pl.when(g == 0)
    def _():
        for i in range(npair):
            kx[i, :, 128:] = mk_ref[...]
            vx[i, :, 128:] = jnp.ones((length, 128), BF16)
    def q_tile(t, _):
        row = pl.multiple_of(t * tq, tq)
        lo, hi = key_range(seg, edges, row, tq)
        rows = pl.ds(row, tq)
        mq = mq_ref[rows, :]
        qs = []
        for i in range(npair):
            q = q_ref[rows, 128 * i:128 * i + 128].astype(F32) * SCALE
            qs += [jnp.concatenate([jnp.where(head0, q, 0.).astype(BF16), mq], 1),
                   jnp.concatenate([jnp.where(head0, 0., q).astype(BF16), mq], 1)]
        def k_tile(j, carry):
            krow = pl.ds(pl.multiple_of(j * tk, tk), tk)
            out = []
            for h in range(2 * npair):
                k = kx[h // 2, krow, :]
                v = vx[h // 2, krow, :]
                m, acc = carry[h]
                s = dot_nt(qs[h], k)
                mn = jnp.maximum(m, jnp.max(s, axis=1, keepdims=True))
                p = jnp.exp(s - mn).astype(BF16)
                out.append((mn, acc * jnp.exp(m - mn) + dot(p, v)))
            return tuple(out)
        init = tuple((jnp.full((tq, 1), -3e38, F32), jnp.zeros((tq, 256), F32)) for _ in range(2 * npair))
        res = lax.fori_loop(lo // tk, (hi + tk - 1) // tk, k_tile, init)
        old = jnp.where(g == 0, jnp.zeros((tq, 128), F32), col[rows, :])
        for i in range(npair):
            outs = []
            for h in range(2):
                m, acc = res[2 * i + h]
                total = acc[:, 128:]
                outs.append(acc[:, :128] / total)
                lse = m + jnp.log(total[:, :1])
                old = jnp.where(lane == 2 * (g * npair + i) + h, lse, old)
            o_ref[rows, 128 * i:128 * i + 128] = jnp.where(head0, outs[0], outs[1]).astype(BF16)
        col[rows, :] = old
        return 0
    lax.fori_loop(0, length // tq, q_tile, 0)
    @pl.when(g == steps - 1)
    def _():
        lse_ref[...] = jnp.transpose(col[...], (1, 0))[:8]

def attention_forward(packed, seg, mq, mk, tq=256, tk=256, npair=1):
    length = packed.shape[0]
    steps = 4 // npair
    w = 128 * npair
    col = lambda o: pl.BlockSpec((length, w), lambda g, s: (0, g + o * steps))
    whole = pl.BlockSpec((length, 128), lambda g, s: (0, 0))
    return pl.pallas_call(
        functools.partial(fwd_kernel, length, tq, tk, npair),
        grid_spec=pltpu.PrefetchScalarGridSpec(
            num_scalar_prefetch=1, grid=(steps,),
            in_specs=[col(0), col(1), col(2), whole, whole],
            out_specs=[col(0), pl.BlockSpec((8, length), lambda g, s: (0, 0))],
            scratch_shapes=[pltpu.VMEM((npair, length, 256), BF16), pltpu.VMEM((npair, length, 256), BF16), pltpu.VMEM((length, 128), F32)]),
        out_shape=[jax.ShapeDtypeStruct((length, 512), BF16), jax.ShapeDtypeStruct((8, length), F32)],
        compiler_params=params(),
        name="attend_forward",
    )(seg, packed, packed, packed, mq, mk)

def bwd_kernel(length, tq, tk, npair, seg, q_ref, k_ref, v_ref, do_ref, mq_ref, mk_ref, lse_ref, delta_ref,
               dq_ref, dk_ref, dv_ref, kx, kt, dk, dv):
    g = pl.program_id(0)
    edges = bounds(seg, length)
    lane = lax.broadcasted_iota(jnp.int32, (1, 128), 1)
    head0 = (lane < 64)
    for i in range(npair):
        kx[i, :, :128] = k_ref[:, 128 * i:128 * i + 128]
    @pl.when(g == 0)
    def _():
        for i in range(npair):
            kx[i, :, 128:] = mk_ref[...]
    kt[...] = jnp.transpose(k_ref[...], (1, 0))
    dk[...] = jnp.zeros_like(dk)
    dv[...] = jnp.zeros_like(dv)
    def q_tile(t, _):
        row = pl.multiple_of(t * tq, tq)
        lo, hi = key_range(seg, edges, row, tq)
        rows = pl.ds(row, tq)
        mq = mq_ref[rows, :]
        qs, dom, q2, do2, lses, deltas = [], [], [], [], [], []
        for i in range(npair):
            q = q_ref[rows, 128 * i:128 * i + 128].astype(F32) * SCALE
            do = do_ref[rows, 128 * i:128 * i + 128].astype(F32)
            qm = [jnp.where(head0, q, 0.).astype(BF16), jnp.where(head0, 0., q).astype(BF16)]
            dm = [jnp.where(head0, do, 0.).astype(BF16), jnp.where(head0, 0., do).astype(BF16)]
            dom += dm
            qs += [jnp.concatenate([x, mq], 1) for x in qm]
            q2.append(jnp.concatenate(qm, 0))
            do2.append(jnp.concatenate(dm, 0))
            lses += [lse_ref[pl.ds(2 * (npair * g + i) + h, 1), rows] for h in range(2)]
            deltas += [delta_ref[pl.ds(2 * (npair * g + i) + h, 1), rows] for h in range(2)]
        def k_tile(j, dqt):
            start = pl.multiple_of(j * tk, tk)
            krow = pl.ds(start, tk)
            ps, dss, dqs = [], [], []
            for h in range(2 * npair):
                k = kx[h // 2, krow, :]
                v = v_ref[krow, 128 * (h // 2):128 * (h // 2) + 128]
                p = jnp.exp(dot_nt(k, qs[h]) - lses[h])
                dp = dot_nt(v, dom[h])
                ds = (p * (dp - deltas[h])).astype(BF16)
                ps.append(p.astype(BF16))
                dss.append(ds)
                dqs.append(dot(kt[64 * h:64 * h + 64, krow], ds))
            for i in range(npair):
                dv[i, krow, :] += dot(jnp.concatenate(ps[2 * i:2 * i + 2], 1), do2[i])
                dk[i, krow, :] += dot(jnp.concatenate(dss[2 * i:2 * i + 2], 1), q2[i])
            return dqt + jnp.concatenate(dqs, 0)
        dqt = lax.fori_loop(lo // tk, (hi + tk - 1) // tk, k_tile, jnp.zeros((128 * npair, tq), F32))
        dq_ref[rows, :] = (jnp.transpose(dqt, (1, 0)) * SCALE).astype(BF16)
        return 0
    lax.fori_loop(0, length // tq, q_tile, 0)
    for i in range(npair):
        dk_ref[:, 128 * i:128 * i + 128] = dk[i].astype(BF16)
        dv_ref[:, 128 * i:128 * i + 128] = dv[i].astype(BF16)

def attention_backward(packed, dmix, seg, mq, mk, lse, delta, tq=256, tk=256, npair=1):
    length = packed.shape[0]
    steps = 4 // npair
    w = 128 * npair
    col = lambda o: pl.BlockSpec((length, w), lambda g, s: (0, g + o * steps))
    whole = pl.BlockSpec((length, 128), lambda g, s: (0, 0))
    rowspec = pl.BlockSpec((8, length), lambda g, s: (0, 0))
    return pl.pallas_call(
        functools.partial(bwd_kernel, length, tq, tk, npair),
        grid_spec=pltpu.PrefetchScalarGridSpec(
            num_scalar_prefetch=1, grid=(steps,),
            in_specs=[col(0), col(1), col(2), col(0), whole, whole, rowspec, rowspec],
            out_specs=[col(0)] * 3,
            scratch_shapes=[pltpu.VMEM((npair, length, 256), BF16), pltpu.VMEM((w, length), BF16), pltpu.VMEM((npair, length, 128), F32), pltpu.VMEM((npair, length, 128), F32)]),
        out_shape=[jax.ShapeDtypeStruct((length, 512), BF16)] * 3,
        compiler_params=params(),
        name="attend_backward",
    )(seg, packed, packed, packed, dmix, mq, mk, lse, delta)


def position():
    dp, fs = lax.axis_index("dp"), lax.axis_index("fsdp")
    return dp // 2, dp % 2, fs // 2, fs % 2


def device(z, x, y, c):
    return (z * 2 + x, y * 2 + c)


def greet(z, x, y, c):
    barrier = pltpu.get_barrier_semaphore()
    partners = [device(lax.rem(z + k, 4), x, y, c) for k in (1, 2, 3)]
    partners += [device(z, 1 - x, y, c), device(z, x, 1 - y, c), device(z, x, y, 1 - c)]
    for partner in partners:
        pl.semaphore_signal(barrier, inc=1, device_id=partner, device_id_type=MESH)
    pl.semaphore_wait(barrier, len(partners))


def remote(src, dst, send, recv, target):
    copy = pltpu.make_async_remote_copy(
        src_ref=src, dst_ref=dst, send_sem=send, recv_sem=recv, device_id=target, device_id_type=MESH
    )
    copy.start()
    return copy


def gather_kernel(count, *refs):
    shards, wholes = refs[:count], refs[count : 2 * count]
    send, recv, local = refs[2 * count :]
    z, x, y, c = position()
    greet(z, x, y, c)
    to_x, to_y, to_core = device(z, 1 - x, y, c), device(z, x, 1 - y, c), device(z, x, y, 1 - c)
    started = []
    near, over_x, over_y, far_a, far_b = {}, {}, {}, {}, {}
    level = lambda k: lax.rem(z - k + 4, 4)

    def go(a, slot, src, dst, target):
        copy = remote(src, dst, send.at[a, slot], recv.at[a, slot], target)
        started.append(copy)
        return copy

    own = []
    for a in range(count):
        place = wholes[a].at[z, x, y, c]
        keep = pltpu.make_async_copy(shards[a], place, local.at[a])
        keep.start()
        own.append(keep)
        for k in (1, 2, 3):
            near[a, k] = go(a, k, shards[a], place, device(lax.rem(z + k, 4), x, y, c))

    def spread(a):
        for k in range(4):
            if k:
                near[a, k].wait_recv()
                src = wholes[a].at[level(k), x, y, c]
            else:
                src = shards[a]
            dst = wholes[a].at[level(k), x, y, c]
            over_x[a, k] = go(a, 4 + k, src, dst, to_x)
            over_y[a, k] = go(a, 8 + k, src, dst, to_y)
        own[a].wait()
        block = wholes[a].at[:, x, y, c]
        near[a, 0] = go(a, 0, block, block, to_core)

    def corner(a):
        half = shards[a].shape[-1] // 2
        for k in range(4):
            over_x[a, k].wait_recv()
            block = wholes[a].at[level(k), 1 - x, y, c, :, :half]
            far_a[a, k] = go(a, 12 + k, block, block, to_y)
        block = wholes[a].at[:, 1 - x, y, c]
        over_x[a, 4] = go(a, 20, block, block, to_core)
        for k in range(4):
            over_y[a, k].wait_recv()
            block = wholes[a].at[level(k), x, 1 - y, c, :, half:]
            far_b[a, k] = go(a, 16 + k, block, block, to_x)
        block = wholes[a].at[:, x, 1 - y, c]
        over_y[a, 4] = go(a, 21, block, block, to_core)

    def finish(a):
        for k in range(4):
            far_a[a, k].wait_recv()
            far_b[a, k].wait_recv()
        block = wholes[a].at[:, 1 - x, 1 - y, c]
        far_a[a, 4] = go(a, 22, block, block, to_core)

    for a in range(count + 2):
        if a < count:
            spread(a)
        if 0 <= a - 1 < count:
            corner(a - 1)
        if 0 <= a - 2 < count:
            finish(a - 2)
    for a in range(count):
        for copy in (near[a, 0], over_x[a, 4], over_y[a, 4], far_a[a, 4]):
            copy.wait_recv()
    for copy in started:
        copy.wait_send()


def gather(shards):
    count = len(shards)
    whole = [jax.ShapeDtypeStruct((4, 2, 2, 2) + s.shape, s.dtype) for s in shards]
    anywhere = pl.BlockSpec(memory_space=pl.ANY)
    outs = pl.pallas_call(
        functools.partial(gather_kernel, count),
        in_specs=[anywhere] * count,
        out_specs=[anywhere] * count,
        out_shape=whole,
        scratch_shapes=[
            pltpu.SemaphoreType.DMA((count, 23)),
            pltpu.SemaphoreType.DMA((count, 23)),
            pltpu.SemaphoreType.DMA((count,)),
        ],
        compiler_params=params(collective_id=0, has_side_effects=True),
        name="gather_parameters",
    )(*shards)
    return [o.reshape((32,) + s.shape) for o, s in zip(outs, shards)]


def add_into(dst, a, b):
    dst[...] = (a.astype(F32) + b.astype(F32)).astype(BF16)


def scatter_kernel(count, *refs):
    grads, outs = refs[:count], refs[count : 2 * count]
    bufs = refs[2 * count : 9 * count]
    send, recv, local = refs[9 * count :]
    z, x, y, c = position()
    greet(z, x, y, c)
    to_x, to_y, to_core = device(z, 1 - x, y, c), device(z, x, 1 - y, c), device(z, x, y, 1 - c)
    started, waits = [], {}

    def go(a, slot, src, dst, target):
        copy = remote(src, dst, send.at[a, slot], recv.at[a, slot], target)
        started.append(copy)
        waits[a, slot] = copy

    def part(a):
        return [bufs[7 * a + i] for i in range(7)]

    keeps = []
    for a in range(count):
        own, got, ya, xb, xa, yb, last = part(a)
        go(a, 0, grads[a].at[:, :, :, 1 - c], got, to_core)
        keep = pltpu.make_async_copy(grads[a].at[:, :, :, c], own, local.at[a])
        keep.start()
        keeps.append(keep)

    def first(a):
        own, got, ya, xb, xa, yb, last = part(a)
        half = own.shape[-1] // 2
        keeps[a].wait()
        waits[a, 0].wait_recv()
        for i in range(4):
            own[i] = (own[i].astype(F32) + got[i].astype(F32)).astype(BF16)
        go(a, 1, own.at[:, :, 1 - y, :, :half], ya, to_y)
        go(a, 2, own.at[:, 1 - x, :, :, half:], xb, to_x)

    def second(a):
        own, got, ya, xb, xa, yb, last = part(a)
        half = own.shape[-1] // 2
        waits[a, 1].wait_recv()
        for i in range(4):
            ya[i] = (own[i, :, y, :, :half].astype(F32) + ya[i].astype(F32)).astype(BF16)
        go(a, 3, ya.at[:, 1 - x], xa, to_x)
        waits[a, 2].wait_recv()
        for i in range(4):
            xb[i] = (own[i, x, :, :, half:].astype(F32) + xb[i].astype(F32)).astype(BF16)
        go(a, 4, xb.at[:, 1 - y], yb, to_y)

    def third(a):
        own, got, ya, xb, xa, yb, last = part(a)
        half = own.shape[-1] // 2
        waits[a, 3].wait_recv()
        waits[a, 4].wait_recv()
        for i in range(4):
            xa[i] = (ya[i, x].astype(F32) + xa[i].astype(F32)).astype(BF16)
            yb[i] = (xb[i, y].astype(F32) + yb[i].astype(F32)).astype(BF16)
        for k in (1, 2, 3):
            to = lax.rem(z + k, 4)
            go(a, 4 + k, xa.at[to], last.at[k - 1, :, :half], device(to, x, y, c))
            go(a, 7 + k, yb.at[to], last.at[k - 1, :, half:], device(to, x, y, c))

    def fourth(a):
        own, got, ya, xb, xa, yb, last = part(a)
        half = own.shape[-1] // 2
        for k in (1, 2, 3):
            waits[a, 4 + k].wait_recv()
            waits[a, 7 + k].wait_recv()
        rest = last[0].astype(F32) + last[1].astype(F32) + last[2].astype(F32)
        outs[a][:, :half] = xa[z].astype(F32) + rest[:, :half]
        outs[a][:, half:] = yb[z].astype(F32) + rest[:, half:]

    for a in range(count + 3):
        for step, stage in enumerate((first, second, third, fourth)):
            if 0 <= a - step < count:
                stage(a - step)
    for copy in started:
        copy.wait_send()


def scatter_sum(grads):
    count = len(grads)
    blocks = [g.reshape((4, 2, 2, 2) + g.shape[1:]) for g in grads]
    scratch = []
    for g in grads:
        rows, width = g.shape[1:]
        half = width // 2
        scratch += [pltpu.VMEM(s, BF16) for s in (
            (4, 2, 2, rows, width), (4, 2, 2, rows, width), (4, 2, rows, half), (4, 2, rows, half),
            (4, rows, half), (4, rows, half), (3, rows, width))]
    return pl.pallas_call(
        functools.partial(scatter_kernel, count),
        in_specs=[pl.BlockSpec(memory_space=pl.ANY)] * count,
        out_specs=[pl.BlockSpec(memory_space=pltpu.VMEM)] * count,
        out_shape=[jax.ShapeDtypeStruct(g.shape[1:], F32) for g in grads],
        scratch_shapes=scratch + [
            pltpu.SemaphoreType.DMA((count, 11)),
            pltpu.SemaphoreType.DMA((count, 11)),
            pltpu.SemaphoreType.DMA((count,)),
        ],
        compiler_params=params(collective_id=1, has_side_effects=True),
        name="sum_gradients",
    )(*blocks)


def per_device(fast, tokens, mask_flags, timesteps, segment_ids, mask_embed, time_table, first_gain, first_bias,
               input_proj, output_proj, output_bias, second_gain, second_bias, hidden_weight, hidden_bias,
               down_weight, down_bias, cotangent):
    count, width = tokens.shape
    hidden = hidden_weight.shape[1]
    vectors = (mask_embed, first_gain, first_bias, output_bias, second_gain, second_bias, down_bias)
    if fast:
        pieces = jnp.concatenate(vectors + (hidden_bias,))
        pieces = jnp.pad(pieces, (0, width - pieces.shape[0]))[None]
        small = jnp.concatenate([time_table, pieces, jnp.zeros((7, width), BF16)], 0)
        small, w_in, w_out, up, down = gather([small, input_proj, output_proj, hidden_weight, down_weight])
    else:
        whole = lambda a: lax.all_gather(a, AXES, axis=0, tiled=True)
        groups = whole(time_table).reshape(-1, 8, width)
        pieces = jnp.concatenate(
            [whole(v).reshape(groups.shape[0], -1) for v in vectors + (hidden_bias,)], 1
        )
        pieces = jnp.pad(pieces, ((0, 0), (0, width - pieces.shape[1])))[:, None]
        small = jnp.concatenate([groups, pieces, jnp.zeros((groups.shape[0], 7, width), BF16)], 1)
        w_in, w_out, up, down = (whole(a) for a in (input_proj, output_proj, hidden_weight, down_weight))
    w_in, w_out, up = (a.reshape(width, -1) for a in (w_in, w_out, up))
    down = down.reshape(hidden, width)
    steps = small.shape[0] * 8
    segments = segment_ids.reshape(-1)
    ids = jnp.concatenate([timesteps[None], mask_flags[None], segments[None], jnp.zeros((5, count), jnp.int32)], 0)

    start, normt, packed, mq, mk, vec, hid = embed(tokens, ids, small, w_in, hidden)
    mixture, lse = attention_forward(packed, segments, mq, mk, FTQ, FTK, FNP)
    out, gmid, dmix, delta, gup, gdown, gout, gvec2, ghid = feed(start, mixture, cotangent, w_out, up, down, vec, hid)
    dq, dk, dv = attention_backward(packed, dmix, segments, mq, mk, lse, delta, BTQ, BTK, BNP)
    gtok, gin, gsmall, gtab, gvec1 = project_back(dq, dk, dv, normt, w_in, start, gmid, ids, vec, gvec2, ghid, steps)
    if fast:
        blocks = lambda a: a.reshape((steps // 8, -1, a.shape[-1]))
        gsmall, gin, gout, gup, gdown = scatter_sum([gsmall, blocks(gin), blocks(gout), blocks(gup), blocks(gdown)])
        gtab = gsmall[:8]
        sizes = [v.shape[0] for v in vectors] + [hidden_bias.shape[0]]
        cuts = [sum(sizes[:i]) for i in range(9)]
        gmask, gg1, gb1, gob, gg2, gb2, gdb, ghb = [gsmall[8, cuts[i] : cuts[i + 1]] for i in range(8)]
    else:
        total = lambda a: lax.psum_scatter(a.astype(F32), AXES, scatter_dimension=0, tiled=True)
        gin, gout, gup, gdown = (total(a) for a in (gin, gout, gup, gdown))
        gmask = total(gtab[steps])
        gtab = total(gtab[:steps])
        gg1, gb1, gob, gg2, gb2, gdb, ghb = (
            total(a) for a in (gvec1[0], gvec1[1], gvec2[0], gvec2[1], gvec2[2], gvec2[3], ghid[0])
        )
    return (out, gtok, gmask, gtab, gg1, gb1, gin, gout, gob, gg2, gb2, gup, ghb, gdown, gdb)


def solution(mesh):
    split = P(AXES)
    rows = P(AXES, None)
    fast = tuple(mesh.shape[a] for a in AXES) == (8, 4)
    placed = (rows, split, split, rows, split, rows, split, split, rows, rows, split, split, split, rows, split, rows,
              split, rows)
    return jax.shard_map(
        functools.partial(per_device, fast),
        mesh=mesh,
        in_specs=placed,
        out_specs=(rows, rows, split, rows, split, split, rows, rows, split, split, split, rows, split, rows, split),
        check_vma=False,
    )
```

```python
import functools

import jax
import jax.numpy as jnp
from jax import lax
from jax.experimental import pallas as pl
from jax.experimental.pallas import tpu as pltpu
from jax.sharding import PartitionSpec as P

F32, BF16 = jnp.float32, jnp.bfloat16
HD = 64
SCALE = HD ** -0.5
NEG = -1e30
EPSILON = 1e-05
AXES = ("dp", "fsdp")
MESH = pl.DeviceIdType.MESH
VMEM_BYTES = 58 << 20
TILE = 512


def dot(a, b):
    return jnp.dot(a, b, preferred_element_type=F32)


def dot_nt(a, b):
    return lax.dot_general(a, b, (((1,), (1,)), ((), ())), preferred_element_type=F32)


def dot_tn(a, b):
    return lax.dot_general(a, b, (((0,), (0,)), ((), ())), preferred_element_type=F32)


def iota(shape, dim):
    return lax.broadcasted_iota(jnp.int32, shape, dim)


def params(**more):
    return pltpu.CompilerParams(vmem_limit_bytes=VMEM_BYTES, **more)


def norm_parts(h):
    centered = h - jnp.mean(h, axis=-1, keepdims=True)
    rstd = lax.rsqrt(jnp.mean(centered * centered, axis=-1, keepdims=True) + EPSILON)
    return centered * rstd, rstd


def norm_back(n, xhat, rstd, gain):
    ng = n * gain
    first = jnp.mean(ng, axis=-1, keepdims=True)
    second = jnp.mean(ng * xhat, axis=-1, keepdims=True)
    return rstd * (ng - first - xhat * second)


def position():
    dp, fs = lax.axis_index("dp"), lax.axis_index("fsdp")
    return dp // 2, dp % 2, fs // 2, fs % 2


def device(z, x, y, c):
    return (z * 2 + x, y * 2 + c)


def peer(z, k):
    return lax.rem(z + k, 4)


def greet(z, x, y, c):
    barrier = pltpu.get_barrier_semaphore()
    partners = [device(peer(z, k), x, y, c) for k in (1, 2, 3)]
    partners += [device(z, 1 - x, y, c), device(z, x, 1 - y, c), device(z, x, y, 1 - c)]
    for partner in partners:
        pl.semaphore_signal(barrier, inc=1, device_id=partner, device_id_type=MESH)
    pl.semaphore_wait(barrier, len(partners))


def remote(src, dst, send, recv, target):
    return pltpu.make_async_remote_copy(
        src_ref=src, dst_ref=dst, send_sem=send, recv_sem=recv, device_id=target, device_id_type=MESH
    )


def gather_plan(place, shard, whole, send, recv, local):
    z, x, y, c = place
    to_x, to_y, to_core = device(z, 1 - x, y, c), device(z, x, 1 - y, c), device(z, x, y, 1 - c)
    half = shard.shape[-1] // 2
    level = lambda k: peer(z, 4 - k)

    def copy(slot):
        kind, k = divmod(slot, 4)
        if slot in (1, 2, 3):
            src, dst, to = shard, whole.at[z, x, y, c], device(peer(z, k), x, y, c)
        elif kind in (1, 2):
            dst, to = whole.at[level(k), x, y, c], (to_x, to_y)[kind - 1]
            src = dst if k else shard
        elif kind == 3:
            src = dst = whole.at[level(k), 1 - x, y, c, :, :half]
            to = to_y
        elif kind == 4:
            src = dst = whole.at[level(k), x, 1 - y, c, :, half:]
            to = to_x
        else:
            xs, ys = ((x, y), (1 - x, y), (x, 1 - y), (1 - x, 1 - y))[(0, 20, 21, 22).index(slot)]
            src = dst = whole.at[:, xs, ys, c]
            to = to_core
        return remote(src, dst, send.at[slot], recv.at[slot], to)

    keep = pltpu.make_async_copy(shard, whole.at[z, x, y, c], local)

    def begin():
        keep.start()
        for k in (1, 2, 3):
            copy(k).start()

    def spread():
        for k in range(4):
            if k:
                copy(k).wait_recv()
            copy(4 + k).start()
            copy(8 + k).start()
        keep.wait()
        copy(0).start()

    def corner():
        for k in range(4):
            copy(4 + k).wait_recv()
            copy(12 + k).start()
        copy(20).start()
        for k in range(4):
            copy(8 + k).wait_recv()
            copy(16 + k).start()
        copy(21).start()

    def finish():
        for k in range(8):
            copy(12 + k).wait_recv()
        copy(22).start()

    def ready():
        for slot in (0, 20, 21, 22):
            copy(slot).wait_recv()

    def drain():
        for slot in range(23):
            copy(slot).wait_send()

    return begin, spread, corner, finish, ready, drain


GATHER_SLOTS = 23


def scatter_plan(place, full, own, got, ya, xb, xa, yb, last, send, recv):
    z, x, y, c = place
    to_x, to_y, to_core = device(z, 1 - x, y, c), device(z, x, 1 - y, c), device(z, x, y, 1 - c)
    half = full.shape[-1] // 2

    def copy(slot):
        if slot == 0:
            src, dst, to = full.at[:, :, :, 1 - c], got, to_core
        elif slot == 1:
            src, dst, to = own.at[:, :, 1 - y, :, :half], ya, to_y
        elif slot == 2:
            src, dst, to = own.at[:, 1 - x, :, :, half:], xb, to_x
        elif slot == 3:
            src, dst, to = ya.at[:, 1 - x], xa, to_x
        elif slot == 4:
            src, dst, to = xb.at[:, 1 - y], yb, to_y
        elif slot < 8:
            k = slot - 4
            src, dst, to = xa.at[peer(z, k)], last.at[k - 1, :, :half], device(peer(z, k), x, y, c)
        else:
            k = slot - 7
            src, dst, to = yb.at[peer(z, k)], last.at[k - 1, :, half:], device(peer(z, k), x, y, c)
        return remote(src, dst, send.at[slot], recv.at[slot], to)

    def to_sibling():
        copy(0).start()

    def to_plane():
        copy(0).wait_recv()
        for i in range(4):
            own[i] = (full[i, :, :, c].astype(F32) + got[i].astype(F32)).astype(BF16)
        copy(1).start()
        copy(2).start()

    def to_corner():
        copy(1).wait_recv()
        for i in range(4):
            ya[i] = (own[i, :, y, :, :half].astype(F32) + ya[i].astype(F32)).astype(BF16)
        copy(3).start()
        copy(2).wait_recv()
        for i in range(4):
            xb[i] = (own[i, x, :, :, half:].astype(F32) + xb[i].astype(F32)).astype(BF16)
        copy(4).start()

    def to_levels():
        copy(3).wait_recv()
        copy(4).wait_recv()
        for i in range(4):
            xa[i] = (ya[i, x].astype(F32) + xa[i].astype(F32)).astype(BF16)
            yb[i] = (xb[i, y].astype(F32) + yb[i].astype(F32)).astype(BF16)
        for k in (1, 2, 3):
            copy(4 + k).start()
            copy(7 + k).start()

    def total(out):
        for slot in range(5, 11):
            copy(slot).wait_recv()
        rest = last[0].astype(F32) + last[1].astype(F32) + last[2].astype(F32)
        out[:, :half] = xa[z].astype(F32) + rest[:, :half]
        out[:, half:] = yb[z].astype(F32) + rest[:, half:]

    def drain():
        for slot in range(11):
            copy(slot).wait_send()

    return to_sibling, to_plane, to_corner, to_levels, total, drain


SCATTER_SLOTS = 11


def scatter_buffers(rows, width):
    half = width // 2
    return [pltpu.VMEM(s, BF16) for s in (
        (4, 2, 2, 2, rows, width), (4, 2, 2, rows, width), (4, 2, 2, rows, width), (4, 2, rows, half),
        (4, 2, rows, half), (4, rows, half), (4, rows, half), (3, rows, width))]


def enter_kernel(tok, ids, s_small, s_in, s_out, s_up, s_down,
                 start_o, normt_o, packed_o, mq_o, mk_o, vec_o, hid_o, win_o, wout_o, feed_o,
                 small, w_in, tokv, startv, normv, normtv, packv, mqv, mkv, table,
                 send, recv, local, fsend, frecv, flocal, moved):
    place = position()
    z, x, y, c = place
    count, width = tok.shape
    rows = min(TILE, count)
    tiles = count // rows
    fetch = pltpu.make_async_copy(tok, tokv, moved.at[0])
    fetch.start()
    greet(*place)
    plans = [
        gather_plan(place, s, w, send.at[a], recv.at[a], local.at[a])
        for a, (s, w) in enumerate(((s_small, small), (s_in, w_in), (s_out, wout_o)))
    ]
    parts = [(s_down, 0, 64)] + [(s_up.at[:, width * j : width * j + width], 64 + 16 * j, 16) for j in range(4)]

    def feed_copy(j, k):
        src, at, size = parts[j]
        dst = feed_o.at[z, at : at + size, :]
        if k == 0:
            return pltpu.make_async_copy(src, dst, flocal.at[j])
        return remote(src, dst, fsend.at[j, k - 1], frecv.at[j, k - 1], device(peer(z, k), x, y, c))

    for plan in plans:
        plan[0]()
    feeds = [feed_copy(j, k) for j in range(5) for k in range(4)]
    for copy in feeds:
        copy.start()
    plans[0][1]()
    plans[1][1]()
    plans[0][2]()
    plans[0][3]()
    plans[1][2]()
    plans[2][1]()
    plans[0][4]()
    small_flat = small[...].reshape((32,) + small.shape[4:])
    unpack_small(small_flat, vec_o, hid_o, table)
    fetch.wait()
    moves = []

    def move(src, dst):
        copy = pltpu.make_async_copy(src, dst, moved.at[len(moves) + 1])
        copy.start()
        moves.append(copy)

    for t in range(tiles):
        at = slice(rows * t, rows * t + rows)
        start_tile(tokv[at, :], ids[:, at], table, vec_o, startv, normv, normtv, mqv, mkv, at)
        move(startv.at[at, :], start_o.at[at, :])
        if t == 0:
            plans[1][3]()
        if t == 1:
            plans[2][2]()
        if t == 2:
            plans[2][3]()
    move(normtv, normt_o)
    move(mqv, mq_o)
    move(mkv, mk_o)
    plans[1][4]()
    move(w_in, win_o)
    weights = w_in[...].reshape(width, w_in.shape[-1])
    for t in range(tiles):
        at = slice(rows * t, rows * t + rows)
        packv[at, :] = dot(normv[at, :], weights).astype(BF16)
        move(packv.at[at, :], packed_o.at[at, :])
    for copy in moves:
        copy.wait()
    plans[2][4]()
    for plan in plans:
        plan[5]()
    for i, copy in enumerate(feeds):
        copy.wait()


def unpack_small(flat16, vec_o, hid_o, table):
    devices, _, width = flat16.shape
    steps = devices * 8
    flat = flat16.astype(F32)
    row = flat[:, 8, :].astype(BF16)
    per = width // devices
    lane = iota((devices, width), 1)
    spread = jnp.concatenate([jnp.where(lane // per == i, row, jnp.zeros_like(row)) for i in range(7)], 0)
    same = (iota((width, width), 0) % per == iota((width, width), 1) % per).astype(BF16)
    wide = dot(spread, same).reshape(7, devices, width)
    mine = (lane // per == iota((devices, width), 0))[None]
    vecs = jnp.sum(jnp.where(mine, wide, 0.0), axis=1)
    vec_o[...] = jnp.concatenate([vecs, jnp.zeros((1, width), F32)], 0)
    hidden = hid_o.shape[1]
    part = hidden // devices
    at = iota((width, hidden), 0) - 7 * per
    pick = (at == iota((width, hidden), 1) % part).astype(BF16)
    own = iota((devices, hidden), 1) // part == iota((devices, hidden), 0)
    hid_o[...] = jnp.sum(jnp.where(own, dot(row, pick), 0.0), axis=0, keepdims=True)
    table[:steps, :] = flat[:, :8, :].reshape(steps, width).astype(BF16)
    table[steps:, :] = jnp.where(iota((16, width), 0) == 0, vecs[0:1], 0.0).astype(BF16)


def start_tile(tok, ids, table, vec, startv, normv, normtv, mqv, mkv, at):
    rows = tok.shape[0]
    steps = table.shape[0] - 16
    start = tok.astype(F32) + dot_tn(token_selector(ids, steps, rows), table[...])
    startv[at, :] = start
    xhat, _ = norm_parts(start)
    normed = (xhat * vec[1:2, :] + vec[2:3, :]).astype(BF16)
    normv[at, :] = normed
    normtv[:, at] = jnp.transpose(normed, (1, 0))
    member = jnp.transpose((ids[2:3, :] == iota((128, rows), 0)).astype(F32), (1, 0))
    mqv[at, :] = member.astype(BF16)
    mkv[at, :] = jnp.where(iota((rows, 128), 1) < 4, (1.0 - member) * NEG, 0.0).astype(BF16)


def token_selector(ids, steps, rows):
    stamps = (ids[0:1, :] == iota((steps, rows), 0)).astype(F32)
    flags = jnp.where(iota((16, rows), 0) == 0, ids[1:2, :].astype(F32), 0.0)
    return jnp.concatenate([stamps, flags], 0).astype(BF16)


def enter_shapes(count, width, hidden):
    return [
        jax.ShapeDtypeStruct((count, width), F32),
        jax.ShapeDtypeStruct((width, count), BF16),
        jax.ShapeDtypeStruct((count, 3 * width), BF16),
        jax.ShapeDtypeStruct((count, 128), BF16),
        jax.ShapeDtypeStruct((count, 128), BF16),
        jax.ShapeDtypeStruct((8, width), F32),
        jax.ShapeDtypeStruct((1, hidden), F32),
    ]


def enter(tokens, ids, shards):
    count, width = tokens.shape
    small, w_in, w_out, up, down = shards
    hidden = up.shape[1]
    anywhere = pl.BlockSpec(memory_space=pl.ANY)
    inside = pl.BlockSpec(memory_space=pltpu.VMEM)
    full = lambda a: (4, 2, 2, 2) + a.shape
    lot = lambda *s: pltpu.SemaphoreType.DMA(s)
    big = lambda w, d: pltpu.VMEM((count, w), d)
    outs = pl.pallas_call(
        enter_kernel,
        in_specs=[anywhere, inside] + [anywhere] * 5,
        out_specs=[anywhere] * 5 + [inside] * 2 + [anywhere] * 3,
        out_shape=enter_shapes(count, width, hidden) + [
            jax.ShapeDtypeStruct(full(w_in), BF16),
            jax.ShapeDtypeStruct(full(w_out), BF16),
            jax.ShapeDtypeStruct((4, down.shape[0] + 64, width), BF16),
        ],
        scratch_shapes=[
            pltpu.VMEM(full(small), BF16), pltpu.VMEM(full(w_in), BF16), big(width, BF16), big(width, F32),
            big(width, BF16), pltpu.VMEM((width, count), BF16), big(3 * width, BF16), big(128, BF16), big(128, BF16),
            pltpu.VMEM((32 * 8 + 16, width), BF16),
            lot(3, GATHER_SLOTS), lot(3, GATHER_SLOTS), lot(3), lot(5, 3), lot(5, 3), lot(5), lot(16),
        ],
        compiler_params=params(collective_id=0, has_side_effects=True),
        name="enter",
    )(tokens, ids, *shards)
    return list(outs[:7]) + [outs[7].reshape(width, -1), outs[8].reshape(width, -1), outs[9]]


def embed_kernel(tok, ids, small, w_in, start_o, normt_o, packed_o, mq_o, mk_o, vec_o, hid_o, table, normv):
    @pl.when(pl.program_id(0) == 0)
    def _():
        unpack_small(small[...], vec_o, hid_o, table)

    start_tile(tok[...], ids[...], table, vec_o, start_o, normv, normt_o, mq_o, mk_o, slice(None))
    packed_o[...] = dot(normv[...], w_in[...]).astype(BF16)


def embed(tokens, ids, small, w_in, hidden):
    count, width = tokens.shape
    rows = min(TILE, count)
    tile = lambda w: pl.BlockSpec((rows, w), lambda i: (i, 0))
    whole = lambda a: pl.BlockSpec(a, lambda i: (0,) * len(a))
    return pl.pallas_call(
        embed_kernel,
        grid=(count // rows,),
        in_specs=[tile(width), pl.BlockSpec((8, rows), lambda i: (0, i)), whole(small.shape), whole(w_in.shape)],
        out_specs=[tile(width), pl.BlockSpec((width, rows), lambda i: (0, i)), tile(3 * width), tile(128), tile(128),
                   whole((8, width)), whole((1, hidden))],
        out_shape=enter_shapes(count, width, hidden),
        scratch_shapes=[pltpu.VMEM((small.shape[0] * 8 + 16, width), BF16), pltpu.VMEM((rows, width), BF16)],
        compiler_params=params(),
        name="embed_project",
    )(tokens, ids, small, w_in)


def bounds(seg, length):
    def first_at_least(s):
        def step(_, lh):
            lo, hi = lh
            mid = (lo + hi) // 2
            below = seg[jnp.minimum(mid, length - 1)] < s
            live = lo < hi
            return (jnp.where(live & below, mid + 1, lo), jnp.where(live & ~below, mid, hi))
        lo, _ = lax.fori_loop(0, length.bit_length(), step, (jnp.int32(0), jnp.int32(length)))
        return lo
    return [jnp.int32(0)] + [first_at_least(s) for s in (1, 2, 3)] + [jnp.int32(length)]

def pick(vals, i):
    out = vals[0]
    for j in range(1, len(vals)):
        out = jnp.where(i == j, vals[j], out)
    return out

def key_range(seg, edges, row, rows):
    first, last = seg[row], seg[row + rows - 1]
    return pick(edges[:-1], first), pick(edges[1:], last)


def list_tiles(seg, length, tile, qi, ki):
    edges = bounds(seg, length)
    blank = length // tile
    qi[0], ki[0] = jnp.int32(blank), jnp.int32(blank)

    def one(t, n):
        lo, hi = key_range(seg, edges, t * tile, tile)

        def put(j, n):
            qi[n], ki[n] = t, j
            return n + 1

        return lax.fori_loop(lo // tile, (hi + tile - 1) // tile, put, n)

    n = lax.fori_loop(0, blank, one, jnp.int32(1))
    for i in range(2):
        qi[n + i], ki[n + i] = jnp.int32(blank), jnp.int32(blank)
    return (n - 1) // 2 + 1


def spots(qi, ki, i, tile, length):
    q, k = pl.multiple_of(qi[i] * tile, tile), pl.multiple_of(ki[i] * tile, tile)
    q_in, k_in = (pl.multiple_of(jnp.where(v >= length, 0, v), tile) for v in (q, k))
    return pl.ds(q_in, tile), pl.ds(k_in, tile), pl.ds(q, tile), pl.ds(k, tile)


def fwd_kernel(length, tile, npair, seg, q_ref, k_ref, v_ref, mq_ref, mk_ref, o_ref, lse_ref,
               qx, kx, vt, acc, top, alpha, ps, qi, ki):
    g = pl.program_id(0)
    heads = 2 * npair
    head0 = iota((1, 128), 1) < HD
    count = list_tiles(seg, length, tile, qi, ki)
    for i in range(npair):
        cols = slice(128 * i, 128 * i + 128)
        kx[i, :, :128] = k_ref[:, cols]
        kx[i, :, 128:] = mk_ref[...]
        q = q_ref[:, cols].astype(F32) * SCALE
        vi = jnp.transpose(v_ref[:, cols], (1, 0))
        for h in range(2):
            qx[2 * i + h, :, :128] = jnp.where(head0 == (h == 0), q, 0.0).astype(BF16)
            qx[2 * i + h, :, 128:] = mq_ref[...]
            vt[2 * i + h, :HD] = vi[HD * h : HD * h + HD]
            vt[2 * i + h, HD:] = jnp.ones((16, length), BF16)
    acc[...] = jnp.zeros_like(acc)
    top[...] = jnp.full_like(top, -3e38)

    def scan(i, slot, hs):
        q_in, k_in, q, _ = spots(qi, ki, i, tile, length)
        for h in hs:
            s = dot_nt(kx[h // 2, k_in, :], qx[h, q_in, :])
            old = top[h : h + 1, q]
            new = jnp.maximum(old, jnp.max(s, axis=0, keepdims=True))
            top[h : h + 1, q] = new
            alpha[slot, h : h + 1] = jnp.exp(old - new)
            ps[slot, h] = jnp.exp(s - new).astype(BF16)

    def mix(i, slot, hs):
        _, k_in, q, _ = spots(qi, ki, i, tile, length)
        for h in hs:
            acc[h, :, q] = acc[h, :, q] * alpha[slot, h : h + 1] + dot(vt[h, :, k_in], ps[slot, h])

    def step(m, _):
        def both(a, sa, b, sb):
            for h in range(heads):
                mix(a, sa, [h])
                scan(b, sb, [h])

        both(2 * m, 1, 2 * m + 1, 0)
        both(2 * m + 1, 0, 2 * m + 2, 1)
        return 0

    lax.fori_loop(0, count, step, 0)
    for i in range(npair):
        both = []
        for h in (2 * i, 2 * i + 1):
            total = acc[h, HD : HD + 1, :length]
            both.append(acc[h, :HD, :length] / total)
            lse_ref[pl.ds(heads * g + h, 1), :] = top[h : h + 1, :length] + jnp.log(total)
        o_ref[:, 128 * i : 128 * i + 128] = jnp.transpose(jnp.concatenate(both, 0), (1, 0)).astype(BF16)


def attention_forward(packed, seg, mq, mk, tile, npair):
    length = packed.shape[0]
    steps = 4 // npair
    w, heads = 128 * npair, 2 * npair
    most = (length // tile) ** 2 + 8
    col = lambda o: pl.BlockSpec((length, w), lambda g, s: (0, g + o * steps))
    whole = pl.BlockSpec((length, 128), lambda g, s: (0, 0))
    return pl.pallas_call(
        functools.partial(fwd_kernel, length, tile, npair),
        grid_spec=pltpu.PrefetchScalarGridSpec(
            num_scalar_prefetch=1, grid=(steps,),
            in_specs=[col(0), col(1), col(2), whole, whole],
            out_specs=[col(0), pl.BlockSpec((8, length), lambda g, s: (0, 0))],
            scratch_shapes=[
                pltpu.VMEM((heads, length, 256), BF16),
                pltpu.VMEM((npair, length, 256), BF16),
                pltpu.VMEM((heads, HD + 16, length), BF16),
                pltpu.VMEM((heads, HD + 16, length + tile), F32),
                pltpu.VMEM((8, length + tile), F32),
                pltpu.VMEM((2, 8, tile), F32),
                pltpu.VMEM((2, heads, tile, tile), BF16),
                pltpu.SMEM((most,), jnp.int32),
                pltpu.SMEM((most,), jnp.int32),
            ]),
        out_shape=[jax.ShapeDtypeStruct((length, 512), BF16), jax.ShapeDtypeStruct((8, length), F32)],
        compiler_params=params(),
        name="attend_forward",
    )(seg, packed, packed, packed, mq, mk)


def bwd_kernel(length, tile, npair, seg, q_ref, k_ref, v_ref, do_ref, mq_ref, mk_ref, lse_ref, delta_ref,
               dq_ref, dk_ref, dv_ref, qx, kx, kt, dox, dk, dv, dqt, ps, dss, qi, ki):
    g = pl.program_id(0)
    heads = 2 * npair
    head0 = iota((1, 128), 1) < HD
    count = list_tiles(seg, length, tile, qi, ki)
    for i in range(npair):
        cols = slice(128 * i, 128 * i + 128)
        kx[i, :, :128] = k_ref[:, cols]
        kx[i, :, 128:] = mk_ref[...]
        kt[cols, :] = jnp.transpose(k_ref[:, cols], (1, 0))
        q = q_ref[:, cols].astype(F32) * SCALE
        do = do_ref[:, cols].astype(F32)
        for h in range(2):
            qx[2 * i + h, :, :128] = jnp.where(head0 == (h == 0), q, 0.0).astype(BF16)
            qx[2 * i + h, :, 128:] = mq_ref[...]
            dox[2 * i + h] = jnp.where(head0 == (h == 0), do, 0.0).astype(BF16)
    for ref in (dk, dv, dqt):
        ref[...] = jnp.zeros_like(ref)

    def scan(i, slot, hs):
        q_in, k_in, _, _ = spots(qi, ki, i, tile, length)
        for h in hs:
            lse = lse_ref[pl.ds(heads * g + h, 1), q_in]
            delta = delta_ref[pl.ds(heads * g + h, 1), q_in]
            p = jnp.exp(dot_nt(kx[h // 2, k_in, :], qx[h, q_in, :]) - lse)
            dp = dot_nt(v_ref[k_in, 128 * (h // 2) : 128 * (h // 2) + 128], dox[h, q_in, :])
            cols = slice(tile * (h % 2), tile * (h % 2) + tile)
            ps[slot, h // 2, :, cols] = p.astype(BF16)
            dss[slot, h // 2, :, cols] = (p * (dp - delta)).astype(BF16)

    def mixp(i, slot, p, kinds):
        q_in, k_in, q, k = spots(qi, ki, i, tile, length)
        for kind in kinds:
            if kind == 0:
                both = jnp.concatenate([dox[2 * p, q_in, :], dox[2 * p + 1, q_in, :]], 0)
                dv[p, k, :] += dot(ps[slot, p], both)
            elif kind == 1:
                both = jnp.concatenate([qx[2 * p, q_in, :128], qx[2 * p + 1, q_in, :128]], 0)
                dk[p, k, :] += dot(dss[slot, p], both)
            else:
                h = 2 * p + kind - 2
                rows = slice(HD * h, HD * h + HD)
                cols = slice(tile * (h % 2), tile * (h % 2) + tile)
                dqt[rows, q] += dot(kt[rows, k_in], dss[slot, p, :, cols])

    def mix(i, slot, hs):
        for p in sorted({h // 2 for h in hs}):
            mixp(i, slot, p, (0, 1, 2, 3))

    def step(m, _):
        def both(a, sa, b, sb):
            scan(b, sb, range(heads))
            mix(a, sa, range(heads))

        both(2 * m, 1, 2 * m + 1, 0)
        both(2 * m + 1, 0, 2 * m + 2, 1)
        return 0

    lax.fori_loop(0, count, step, 0)
    for i in range(npair):
        cols = slice(128 * i, 128 * i + 128)
        dk_ref[:, cols] = dk[i, :length].astype(BF16)
        dv_ref[:, cols] = dv[i, :length].astype(BF16)
        dq_ref[:, cols] = jnp.transpose(dqt[cols, :length] * SCALE, (1, 0)).astype(BF16)


def attention_backward(packed, dmix, seg, mq, mk, lse, delta, tile, npair):
    length = packed.shape[0]
    steps = 4 // npair
    w, heads = 128 * npair, 2 * npair
    most = (length // tile) ** 2 + 8
    col = lambda o: pl.BlockSpec((length, w), lambda g, s: (0, g + o * steps))
    whole = pl.BlockSpec((length, 128), lambda g, s: (0, 0))
    rowspec = pl.BlockSpec((8, length), lambda g, s: (0, 0))
    return pl.pallas_call(
        functools.partial(bwd_kernel, length, tile, npair),
        grid_spec=pltpu.PrefetchScalarGridSpec(
            num_scalar_prefetch=1, grid=(steps,),
            in_specs=[col(0), col(1), col(2), col(0), whole, whole, rowspec, rowspec],
            out_specs=[col(0)] * 3,
            scratch_shapes=[
                pltpu.VMEM((heads, length, 256), BF16),
                pltpu.VMEM((npair, length, 256), BF16),
                pltpu.VMEM((w, length), BF16),
                pltpu.VMEM((heads, length, 128), BF16),
                pltpu.VMEM((npair, length + tile, 128), F32),
                pltpu.VMEM((npair, length + tile, 128), F32),
                pltpu.VMEM((w, length + tile), F32),
                pltpu.VMEM((2, npair, tile, 2 * tile), BF16),
                pltpu.VMEM((2, npair, tile, 2 * tile), BF16),
                pltpu.SMEM((most,), jnp.int32),
                pltpu.SMEM((most,), jnp.int32),
            ]),
        out_shape=[jax.ShapeDtypeStruct((length, 512), BF16)] * 3,
        compiler_params=params(),
        name="attend_backward",
    )(seg, packed, packed, packed, dmix, mq, mk, lse, delta)


def gelu_parts(v):
    phi = 0.5 * lax.erf(v * 0.7071067811865476) + 0.5
    return v * phi, phi + v * (jnp.exp(v * v * -0.5) * 0.3989422804014327)


def feed_kernel(linked, tiles, chunks, start, mix, cot, w_out, vec, hid, *refs):
    if linked:
        lands = refs[:4]
        out_o, gmid_o, dmix_o, delta_o, gvec_o, ghid_o = refs[4:10]
        leaves = refs[10:14]
        refs = refs[14:]
    else:
        up_all, down_all = refs[:2]
        out_o, gmid_o, dmix_o, delta_o, gvec_o, ghid_o, gup_o, gdown_o, gout_o = refs[2:11]
        refs = refs[11:]
    mid, res, gn2, n2, n2t, br, brt, act0, act1, gpre0, gpre1, gup, gdt, gout = refs[:14]
    s = pl.program_id(0)
    t_rows, width = start.shape
    f = act0.shape[1]
    half = tiles // 2
    middle_steps = chunks * half
    if linked:
        up, down, sent, kept, got, lsem, lsend, lrecv, esend, erecv, eout = refs[14:]
        place = position()
        z, x, y, c = place
        sibling = device(z, x, y, 1 - c)
        spots = ((x, y), (1 - x, y), (x, 1 - y), (1 - x, 1 - y))

        def arrive(i, j, kind):
            xs, ys = spots[i]
            if j == 0:
                src, dst = lands[i].at[:, :64, :], down.at[:, xs, ys, c]
            else:
                src = lands[i].at[:, 48 + 16 * j : 64 + 16 * j, :]
                dst = up.at[:, xs, ys, c, :, width * (j - 1) : width * j]
            if kind == 0:
                return pltpu.make_async_copy(src, dst, lsem.at[i, j])
            return remote(src, dst, lsend.at[i, j], lrecv.at[i, j], sibling)

        arrivals = [(i, j) for i in range(4) for j in range(5)]

        def exchange(j):
            at = slice(0, 128) if j == 0 else slice(128, 144)
            return remote(sent.at[:, :, :, at, :], got.at[:, :, :, at, :], esend.at[j], erecv.at[j], sibling)

        def leave(i):
            xs, ys = spots[i]
            return pltpu.make_async_copy(got.at[:, xs, ys], leaves[i], eout.at[i])


    def rows_at(t):
        return pl.ds(pl.multiple_of(t * t_rows, t_rows), t_rows)

    def cols_at(c):
        return pl.ds(pl.multiple_of(c * f, f), f)

    def up_chunk(ch):
        if linked:
            return up[:, :, :, :, :, cols_at(ch)].reshape(width, f)
        return up_all[:, cols_at(ch)]

    def down_chunk(ch):
        if linked:
            return down[ch].reshape(f, width)
        return down_all[cols_at(ch), :]

    @pl.when(s == 0)
    def _():
        if linked:
            barrier = pltpu.get_barrier_semaphore()
            pl.semaphore_signal(barrier, inc=1, device_id=sibling, device_id_type=MESH)
            pl.semaphore_wait(barrier, 1)
            for i, j in arrivals:
                arrive(i, j, 0).start()
                arrive(i, j, 1).start()
        for ref in (act1, gpre1, gup, gdt, gn2, gout, gvec_o, ghid_o):
            ref[...] = jnp.zeros_like(ref)

    @pl.when(s < tiles)
    def _():
        rows = rows_at(s)
        middle = start[...] + dot(mix[...], w_out[...]) + vec[3:4, :]
        mid[rows, :] = middle
        res[rows, :] = middle + vec[6:7, :]
        xhat, _ = norm_parts(middle)
        normed = (xhat * vec[4:5, :] + vec[5:6, :]).astype(BF16)
        n2[rows, :] = normed
        n2t[:, rows] = jnp.transpose(normed, (1, 0))
        branch = cot[...].astype(BF16)
        br[rows, :] = branch
        brt[:, rows] = jnp.transpose(branch, (1, 0))
        gvec_o[3:4, :] += jnp.sum(branch.astype(F32), axis=0, keepdims=True)

    if linked:
        @pl.when(s == tiles)
        def _():
            for i, j in arrivals:
                arrive(i, j, 0).wait()
                arrive(i, j, 1).wait()

    def inner(ch, t, act, gpre):
        cols, rows = cols_at(ch), rows_at(t)
        pre = dot(n2[rows, :], up_chunk(ch)) + hid[:, cols]
        grad = dot_nt(br[rows, :], down_chunk(ch))
        value, slope = gelu_parts(pre)
        act[...] = value.astype(BF16)
        low = (grad * slope).astype(BF16)
        gpre[...] = low
        ghid_o[:, cols] += jnp.sum(low.astype(F32), axis=0, keepdims=True)

    def outer(ch, t, act, gpre):
        cols, rows = cols_at(ch), rows_at(t)
        a, g = act[...], gpre[...]
        res[rows, :] += dot(a, down_chunk(ch))
        gn2[rows, :] += dot_nt(g, up_chunk(ch))
        gup[:, cols] += dot(n2t[:, rows], g)
        gdt[:, cols] += dot(brt[:, rows], a)

    @pl.when((s >= tiles) & (s < tiles + middle_steps))
    def _():
        b = s - tiles
        before = jnp.maximum(b - 1, 0)
        ch, t = b // half, 2 * (b % half)
        outer(before // half, 2 * (before % half) + 1, act1, gpre1)
        inner(ch, t, act0, gpre0)
        outer(ch, t, act0, gpre0)
        inner(ch, t + 1, act1, gpre1)

    @pl.when(s == tiles + middle_steps)
    def _():
        outer(chunks - 1, tiles - 1, act1, gpre1)
        if linked:
            for i in range(4):
                block = jnp.transpose(gdt[:, 512 * i : 512 * i + 512], (1, 0)).reshape(2, 2, 2, 64, width)
                first, second = block[:, :, 0], block[:, :, 1]
                kept[i, :, :, :64, :] = jnp.where(c == 0, first, second).astype(BF16)
                sent[i, :, :, :64, :] = jnp.where(c == 0, second, first).astype(BF16)
                cols = slice(width * i, width * i + width)
                block = gup[:, cols].reshape(4, 2, 2, 2, 16, width)
                first, second = block[:, :, :, 0], block[:, :, :, 1]
                at = slice(64 + 16 * i, 80 + 16 * i)
                kept[:, :, :, at, :] = jnp.where(c == 0, first, second).astype(BF16)
                sent[:, :, :, at, :] = jnp.where(c == 0, second, first).astype(BF16)
            exchange(0).start()
        else:
            for i in range(chunks):
                gup_o[:, i * f : (i + 1) * f] = gup[:, i * f : (i + 1) * f].astype(BF16)
                gdown_o[i * f : (i + 1) * f, :] = jnp.transpose(gdt[:, i * f : (i + 1) * f], (1, 0)).astype(BF16)

    @pl.when(s >= tiles + middle_steps)
    def _():
        rows = rows_at(s - tiles - middle_steps)
        out_o[...] = res[rows, :].astype(BF16)
        xhat, rstd = norm_parts(mid[rows, :])
        n = gn2[rows, :]
        grad = cot[...] + norm_back(n, xhat, rstd, vec[4:5, :])
        gmid_o[...] = grad
        low = grad.astype(BF16)
        gvec_o[0:1, :] += jnp.sum(low.astype(F32), axis=0, keepdims=True)
        gvec_o[1:2, :] += jnp.sum(n * xhat, axis=0, keepdims=True)
        gvec_o[2:3, :] += jnp.sum(n, axis=0, keepdims=True)
        mixed = mix[...]
        gout[...] += dot_tn(mixed, low)
        dmix = dot_nt(low, w_out[...]).astype(BF16)
        dmix_o[...] = dmix
        prod = dmix.astype(F32) * mixed.astype(F32)
        high = prod.astype(BF16)
        rest = (prod - high.astype(F32)).astype(BF16)
        heads = (iota((16, prod.shape[1]), 1) // HD == iota((16, prod.shape[1]), 0)).astype(BF16)
        delta_o[...] = (dot_nt(heads, high) + dot_nt(heads, rest))[:8]

    @pl.when(s == 2 * tiles + middle_steps - 1)
    def _():
        if linked:
            block = gout[...].reshape(4, 2, 2, 2, 16, width)
            first, second = block[:, :, :, 0], block[:, :, :, 1]
            kept[:, :, :, 128:, :] = jnp.where(c == 0, first, second).astype(BF16)
            sent[:, :, :, 128:, :] = jnp.where(c == 0, second, first).astype(BF16)
            exchange(1).start()
            exchange(0).wait()
            exchange(1).wait()
            for i in range(4):
                got[i] = (got[i].astype(F32) + kept[i].astype(F32)).astype(BF16)
            for i in range(4):
                leave(i).start()
            for i in range(4):
                leave(i).wait()
        else:
            gout_o[...] = gout[...].astype(BF16)


def feed(start, mixture, cotangent, w_out, vec, hid, weights, linked):
    count, width = start.shape
    hidden = hid.shape[1]
    rows = min(TILE, count)
    f = min(512, hidden)
    tiles, chunks = count // rows, hidden // f
    middle = chunks * (tiles // 2)
    first = lambda s: jnp.minimum(s, tiles - 1)
    last = lambda s: jnp.maximum(s - tiles - middle, 0)
    both = lambda s: jnp.where(s < tiles + middle, first(s), last(s))
    tile = lambda at: pl.BlockSpec((rows, width), lambda s: (at(s), 0))
    whole = lambda *a: pl.BlockSpec(a, lambda s: (0,) * len(a))
    anywhere = pl.BlockSpec(memory_space=pl.ANY)
    big = lambda d: pltpu.VMEM((count, width), d)
    lot = lambda *s: pltpu.SemaphoreType.DMA(s)
    scratch = (
        [big(F32), big(F32), big(F32), big(BF16), pltpu.VMEM((width, count), BF16), big(BF16),
         pltpu.VMEM((width, count), BF16)]
        + [pltpu.VMEM((rows, f), BF16)] * 4
        + [pltpu.VMEM((width, hidden), F32)] * 2
        + [pltpu.VMEM((width, width), F32)]
    )
    common = [
        jax.ShapeDtypeStruct((count, width), BF16),
        jax.ShapeDtypeStruct((count, width), F32),
        jax.ShapeDtypeStruct((count, width), BF16),
        jax.ShapeDtypeStruct((8, count), F32),
        jax.ShapeDtypeStruct((8, width), F32),
        jax.ShapeDtypeStruct((1, hidden), F32),
    ]
    if linked:
        weight_specs = [anywhere] * 4
        more = [jax.ShapeDtypeStruct((4, 144, width), BF16)] * 4
        more_specs = [anywhere] * 4
        scratch += [
            pltpu.VMEM((4, 2, 2, 2, 16, hidden), BF16), pltpu.VMEM((4, 2, 2, 2, 64, width), BF16),
        ] + [pltpu.VMEM((4, 2, 2, 144, width), BF16)] * 3 + [lot(4, 5), lot(4, 5), lot(4, 5), lot(2), lot(2), lot(4)]
        compiler = params(collective_id=1, has_side_effects=True)
    else:
        weight_specs = [whole(width, hidden), whole(hidden, width)]
        more = [jax.ShapeDtypeStruct(s, BF16) for s in ((width, hidden), (hidden, width), (width, width))]
        more_specs = [whole(width, hidden), whole(hidden, width), whole(width, width)]
        compiler = params()
    return pl.pallas_call(
        functools.partial(feed_kernel, linked, tiles, chunks),
        grid=(tiles + middle + tiles,),
        in_specs=[tile(first), tile(both), tile(both), whole(width, width), whole(8, width), whole(1, hidden)] + weight_specs,
        out_specs=[tile(last), tile(last), tile(last), pl.BlockSpec((8, rows), lambda s: (0, last(s))),
                   whole(8, width), whole(1, hidden)] + more_specs,
        out_shape=common + more,
        scratch_shapes=scratch,
        compiler_params=compiler,
        name="feed_forward",
    )(start, mixture, cotangent, w_out, vec, hid, *weights)


def leave_kernel(linked, tiles, dq, dk, dv, normt, w_in, start, gmid, ids, vec, gvec2, ghid, *refs):
    if linked:
        pieces = refs[:4]
        gtok_o, gin_o, gsmall_o, gfeed_o, gtab, gvec, gin, packs, esum, egot, esend, erecv = refs[4:16]
        places = [refs[16 + 10 * i : 26 + 10 * i] for i in range(2)]
    else:
        gtok_o, gin_o, gtab, gvec, gin, packs = refs
    s = pl.program_id(0)
    rows, width = start.shape
    steps = gtab.shape[0] - 16
    if linked:
        place = position()
        z, x, y, c = place
        plans = [scatter_plan(place, *p) for p in places]

        def level(k):
            return remote(esum.at[peer(z, k)], egot.at[k - 1], esend.at[k - 1], erecv.at[k - 1],
                          device(peer(z, k), x, y, c))

    @pl.when(s == 0)
    def _():
        if linked:
            greet(*place)
            for i in range(4):
                parts = [p[i].astype(F32) for p in pieces]
                esum[i] = (parts[0] + parts[1] + parts[2] + parts[3]).astype(BF16)
            for k in (1, 2, 3):
                level(k).start()
        for ref in (gin, gtab, gvec):
            ref[...] = jnp.zeros_like(ref)

    def rows_at(t):
        return pl.ds(pl.multiple_of(t * rows, rows), rows)

    @pl.when(s < tiles)
    def _():
        at = rows_at(s)
        for i, d in enumerate((dq, dk, dv)):
            cols = slice(width * i, width * (i + 1))
            low = d[...]
            packs[at, cols] = low
            gin[:, cols] += dot(normt[...], low)

    @pl.when(s == tiles - 1)
    def _():
        if linked:
            places[0][0][...] = gin[...].astype(BF16).reshape(places[0][0].shape)
            plans[0][0]()
        else:
            gin_o[...] = gin[...].astype(BF16)

    @pl.when(s >= tiles)
    def _():
        at = rows_at(s - tiles)
        n = dot_nt(packs[at, :], w_in[...])
        xhat, rstd = norm_parts(start[...])
        grad = gmid[...] + norm_back(n, xhat, rstd, vec[1:2, :])
        gtok_o[...] = grad
        gvec[0:1, :] += jnp.sum(n * xhat, axis=0, keepdims=True)
        gvec[1:2, :] += jnp.sum(n, axis=0, keepdims=True)
        gtab[...] += dot(token_selector(ids, steps, rows), grad.astype(BF16))

    if linked:
        for i in range(3):
            @pl.when(s == tiles + i)
            def _():
                plans[0][1 + i]()

        @pl.when(s == 2 * tiles - 1)
        def _():
            pack_small(places[1][0], steps, gtab, gvec, gvec2, ghid)
            plans[1][0]()
            plans[1][1]()
            for k in (1, 2, 3):
                level(k).wait_recv()
            gfeed_o[...] = (esum[z].astype(F32) + egot[0].astype(F32)) + (egot[1].astype(F32) + egot[2].astype(F32))
            plans[1][2]()
            plans[0][4](gin_o)
            plans[1][3]()
            plans[1][4](gsmall_o)
            plans[0][5]()
            plans[1][5]()
            for k in (1, 2, 3):
                level(k).wait_send()


def pack_small(full, steps, gtab, gvec, gvec2, ghid):
    width = gtab.shape[1]
    groups = steps // 8
    per = width // groups
    sums = [gtab[steps : steps + 1, :], gvec[0:1, :], gvec[1:2, :]]
    sums += [gvec2[i : i + 1, :] for i in range(4)]
    mine = iota((groups, width), 1) // per == iota((groups, width), 0)
    spread = jnp.concatenate([jnp.where(mine, v, 0.0) for v in sums], 0).astype(BF16)
    same = (iota((width, width), 0) % per == iota((width, width), 1) % per).astype(BF16)
    wide = dot(spread, same).reshape(7, groups, width)
    lane = iota((1, width), 1)
    row = jnp.zeros((groups, width), F32)
    for i in range(7):
        row = jnp.where(lane // per == i, wide[i], row)
    hidden = ghid.shape[1]
    part = hidden // groups
    own = iota((groups, hidden), 1) // part == iota((groups, hidden), 0)
    pick = (iota((hidden, width), 0) % part == iota((hidden, width), 1) - 7 * per).astype(BF16)
    row = row + dot(jnp.where(own, ghid[...], 0.0).astype(BF16), pick)
    table = gtab[:steps, :].reshape(groups, 8, width)
    below = jnp.where(iota((groups, 8, width), 1) == 0, row[:, None, :], 0.0)
    full[...] = jnp.concatenate([table, below], 1).astype(BF16).reshape(full.shape)


def leave(dq, dk, dv, normt, w_in, start, gmid, ids, vec, gvec2, ghid, steps, pieces, linked):
    count, width = start.shape
    rows = min(TILE, count)
    tiles = count // rows
    first = lambda s: jnp.minimum(s, tiles - 1)
    last = lambda s: jnp.maximum(s - tiles, 0)
    tile = lambda at: pl.BlockSpec((rows, width), lambda s: (at(s), 0))
    whole = lambda *a: pl.BlockSpec(a, lambda s: (0,) * len(a))
    lot = lambda *s: pltpu.SemaphoreType.DMA(s)
    scratch = [pltpu.VMEM((width, 3 * width), F32), pltpu.VMEM((count, 3 * width), BF16)]
    sums = [jax.ShapeDtypeStruct((steps + 16, width), F32), jax.ShapeDtypeStruct((8, width), F32)]
    held = [pltpu.VMEM(a.shape, F32) for a in sums]
    if linked:
        more = [jax.ShapeDtypeStruct(s, F32) for s in ((16, 3 * width), (16, width), (144, width))]
        scratch = held + scratch + [pltpu.VMEM((4, 144, width), BF16), pltpu.VMEM((3, 144, width), BF16), lot(3), lot(3)]
        for w in (3 * width, width):
            scratch += scatter_buffers(16, w) + [lot(SCATTER_SLOTS), lot(SCATTER_SLOTS)]
        compiler = params(collective_id=2, has_side_effects=True)
    else:
        more = [jax.ShapeDtypeStruct((width, 3 * width), BF16)] + sums
        compiler = params()
    return pl.pallas_call(
        functools.partial(leave_kernel, linked, tiles),
        grid=(2 * tiles,),
        in_specs=[tile(first)] * 3 + [pl.BlockSpec((width, rows), lambda s: (0, first(s))), whole(*w_in.shape), tile(last),
                  tile(last), pl.BlockSpec((8, rows), lambda s: (0, last(s))), whole(8, width), whole(8, width),
                  whole(*ghid.shape)] + [whole(*p.shape) for p in pieces],
        out_specs=[tile(last)] + [whole(*a.shape) for a in more],
        out_shape=[jax.ShapeDtypeStruct((count, width), F32)] + more,
        scratch_shapes=scratch,
        compiler_params=compiler,
        name="leave",
    )(dq, dk, dv, normt, w_in, start, gmid, ids, vec, gvec2, ghid, *pieces)


def unpack_kernel(sizes, gsmall, gfeed, gtab_o, gout_o, gup_o, gdown_o, *vecs):
    width = gsmall.shape[1]
    gtab_o[...] = gsmall[:8, :]
    gdown_o[...] = gfeed[:64, :]
    for i in range(gup_o.shape[1] // width):
        gup_o[:, width * i : width * (i + 1)] = gfeed[64 + 16 * i : 80 + 16 * i, :]
    gout_o[...] = gfeed[128:144, :]
    at = 0
    for ref, size in zip(vecs, sizes):
        ref[...] = gsmall[8:9, at : at + size]
        at += size


def unpack(gsmall, gfeed, hidden, sizes):
    width = gsmall.shape[1]
    shapes = [(8, width), (16, width), (16, hidden), (64, width)] + [(1, n) for n in sizes]
    return pl.pallas_call(
        functools.partial(unpack_kernel, sizes),
        out_shape=[jax.ShapeDtypeStruct(s, F32) for s in shapes],
        compiler_params=params(),
        name="unpack",
    )(gsmall, gfeed)


def exchange_plane(arrays):
    out = [arrays[0]]
    for array, (dx, dy) in zip(arrays[1:], ((1, 0), (0, 1), (1, 1))):
        pairs = [(4 * dp + fs, 4 * (dp ^ dx) + (fs ^ (2 * dy))) for dp in range(8) for fs in range(4)]
        out.append(lax.ppermute(array, AXES, pairs))
    return out


def per_device(fast, tokens, mask_flags, timesteps, segment_ids, mask_embed, time_table, first_gain, first_bias,
               input_proj, output_proj, output_bias, second_gain, second_bias, hidden_weight, hidden_bias,
               down_weight, down_bias, cotangent):
    count, width = tokens.shape
    hidden = hidden_weight.shape[1]
    vectors = (mask_embed, first_gain, first_bias, output_bias, second_gain, second_bias, down_bias)
    segments = segment_ids.reshape(-1)
    ids = (jnp.pad(timesteps[None], ((0, 7), (0, 0))) + jnp.pad(mask_flags[None], ((1, 6), (0, 0)))
           + jnp.pad(segment_ids.reshape(1, -1), ((2, 5), (0, 0))))
    if fast:
        sizes = [v.shape[0] for v in vectors] + [hidden_bias.shape[0]]
        small = jnp.pad(time_table.astype(F32), ((0, 8), (0, 0)))
        at = 0
        for v, size in zip(vectors + (hidden_bias,), sizes):
            small = small + jnp.pad(v.astype(F32)[None], ((8, 7), (at, width - at - size)))
            at += size
        shards = [small.astype(BF16), input_proj, output_proj, hidden_weight, down_weight]
        start, normt, packed, mq, mk, vec, hid, w_in, w_out, own = enter(tokens, ids, shards)
        steps = time_table.shape[0] * 32
        weights = exchange_plane([own] * 4)
    else:
        whole = lambda a: lax.all_gather(a, AXES, axis=0, tiled=True)
        groups = whole(time_table).reshape(-1, 8, width)
        pieces = jnp.concatenate(
            [whole(v).reshape(groups.shape[0], -1) for v in vectors + (hidden_bias,)], 1
        )
        pieces = jnp.pad(pieces, ((0, 0), (0, width - pieces.shape[1])))[:, None]
        small = jnp.concatenate([groups, pieces, jnp.zeros((groups.shape[0], 7, width), BF16)], 1)
        w_in, w_out = whole(input_proj), whole(output_proj)
        weights = [whole(hidden_weight), whole(down_weight)]
        steps = groups.shape[0] * 8
        start, normt, packed, mq, mk, vec, hid = embed(tokens, ids, small, w_in, hidden)

    mixture, lse = attention_forward(packed, segments, mq, mk, 256, 4)
    out, gmid, dmix, delta, gvec2, ghid, *grads = feed(start, mixture, cotangent, w_out, vec, hid, weights, fast)
    pieces = exchange_plane(grads) if fast else []
    dq, dk, dv = attention_backward(packed, dmix, segments, mq, mk, lse, delta, 256, 2)
    gtok, gin, *rest = leave(dq, dk, dv, normt, w_in, start, gmid, ids, vec, gvec2, ghid, steps, pieces, fast)
    if fast:
        gtab, gout, gup, gdown, *small = unpack(rest[0], rest[1], hidden, sizes)
        gmask, gg1, gb1, gob, gg2, gb2, gdb, ghb = [v.reshape(-1) for v in small]
    else:
        total = lambda a: lax.psum_scatter(a.astype(F32), AXES, scatter_dimension=0, tiled=True)
        gtab, gvec1 = rest
        gup, gdown, gout = grads
        gin, gout, gup, gdown = (total(a) for a in (gin, gout, gup, gdown))
        gmask = total(gtab[steps])
        gtab = total(gtab[:steps])
        gg1, gb1, gob, gg2, gb2, gdb, ghb = (
            total(a) for a in (gvec1[0], gvec1[1], gvec2[0], gvec2[1], gvec2[2], gvec2[3], ghid[0])
        )
    return (out, gtok, gmask, gtab, gg1, gb1, gin, gout, gob, gg2, gb2, gup, ghb, gdown, gdb)


def solution(mesh):
    split = P(AXES)
    rows = P(AXES, None)
    fast = tuple(mesh.shape[a] for a in AXES) == (8, 4)
    placed = (rows, split, split, rows, split, rows, split, split, rows, rows, split, split, split, rows, split, rows,
              split, rows)
    return jax.shard_map(
        functools.partial(per_device, fast),
        mesh=mesh,
        in_specs=placed,
        out_specs=(rows, rows, split, rows, split, split, rows, rows, split, split, split, rows, split, rows, split),
        check_vma=False,
    )
```

```python
import functools

import jax
import jax.numpy as jnp
from jax import lax
from jax.experimental import pallas as pl
from jax.experimental.pallas import tpu as pltpu
from jax.sharding import PartitionSpec as P

F32, BF16 = jnp.float32, jnp.bfloat16
HD = 64
SEGMENTS = 4
SCALE = HD ** -0.5
NEG = -1e30
EPSILON = 1e-05
AXES = ("dp", "fsdp")
MESH = pl.DeviceIdType.MESH
VMEM_BYTES = 58 << 20
TILE = 512


def dot(a, b):
    return jnp.dot(a, b, preferred_element_type=F32)


def dot_nt(a, b):
    return lax.dot_general(a, b, (((1,), (1,)), ((), ())), preferred_element_type=F32)


def dot_tn(a, b):
    return lax.dot_general(a, b, (((0,), (0,)), ((), ())), preferred_element_type=F32)


def iota(shape, dim):
    return lax.broadcasted_iota(jnp.int32, shape, dim)


def params(**more):
    return pltpu.CompilerParams(vmem_limit_bytes=VMEM_BYTES, **more)


def norm_parts(h):
    centered = h - jnp.mean(h, axis=-1, keepdims=True)
    rstd = lax.rsqrt(jnp.mean(centered * centered, axis=-1, keepdims=True) + EPSILON)
    return centered * rstd, rstd


def norm_back(n, xhat, rstd, gain):
    ng = n * gain
    first = jnp.mean(ng, axis=-1, keepdims=True)
    second = jnp.mean(ng * xhat, axis=-1, keepdims=True)
    return rstd * (ng - first - xhat * second)


def position():
    dp, fs = lax.axis_index("dp"), lax.axis_index("fsdp")
    return dp // 2, dp % 2, fs // 2, fs % 2


def device(z, x, y, c):
    return (z * 2 + x, y * 2 + c)


def peer(z, k):
    return lax.rem(z + k, 4)


def greet(z, x, y, c):
    barrier = pltpu.get_barrier_semaphore()
    partners = [device(peer(z, k), x, y, c) for k in (1, 2, 3)]
    partners += [device(z, xs, ys, c) for xs, ys in plane(x, y)[1:]] + [device(z, x, y, 1 - c)]
    for partner in partners:
        pl.semaphore_signal(barrier, inc=1, device_id=partner, device_id_type=MESH)
    pl.semaphore_wait(barrier, len(partners))


def remote(src, dst, send, recv, target):
    return pltpu.make_async_remote_copy(
        src_ref=src, dst_ref=dst, send_sem=send, recv_sem=recv, device_id=target, device_id_type=MESH
    )


def plane(x, y):
    return ((x, y), (1 - x, y), (x, 1 - y), (1 - x, 1 - y))


def gather_plan(place, shard, whole, send, recv, local):
    z, x, y, c = place
    spots = plane(x, y)
    level = lambda k: peer(z, 4 - k)

    def copy(slot):
        if slot < 4 and slot:
            src, dst, to = shard, whole.at[z, x, y, c], device(peer(z, slot), x, y, c)
        elif 4 <= slot < 16:
            k = slot % 4
            dst, to = whole.at[level(k), x, y, c], device(z, *spots[slot // 4], c)
            src = dst if k else shard
        else:
            xs, ys = spots[max(slot - 15, 0)]
            src = dst = whole.at[:, xs, ys, c]
            to = device(z, x, y, 1 - c)
        return remote(src, dst, send.at[slot], recv.at[slot], to)

    keep = pltpu.make_async_copy(shard, whole.at[z, x, y, c], local)

    def begin():
        keep.start()
        for k in (1, 2, 3):
            copy(k).start()

    def spread():
        for k in range(4):
            if k:
                copy(k).wait_recv()
            for kind in (4, 8, 12):
                copy(kind + k).start()
        keep.wait()
        copy(0).start()

    def finish():
        for i in range(3):
            for k in range(4):
                copy(4 + 4 * i + k).wait_recv()
            copy(16 + i).start()

    def ready():
        for slot in (0, 16, 17, 18):
            copy(slot).wait_recv()

    def drain():
        for slot in range(GATHER_SLOTS):
            copy(slot).wait_send()

    return begin, spread, finish, ready, drain


GATHER_SLOTS = 19


def scatter_plan(place, full, own, got, land, last, send, recv):
    z, x, y, c = place
    spots = plane(x, y)

    def copy(slot):
        if slot == 0:
            src, dst, to = full.at[:, :, :, 1 - c], got, device(z, x, y, 1 - c)
        elif slot < 4:
            xs, ys = spots[slot]
            src, dst, to = own.at[:, xs, ys], land.at[slot - 1], device(z, xs, ys, c)
        else:
            k = slot - 3
            src, dst, to = got.at[peer(z, k), 0, 0], last.at[k - 1], device(peer(z, k), x, y, c)
        return remote(src, dst, send.at[slot], recv.at[slot], to)

    def to_sibling():
        copy(0).start()

    def to_plane():
        copy(0).wait_recv()
        for i in range(4):
            own[i] = (full[i, :, :, c].astype(F32) + got[i].astype(F32)).astype(BF16)
        for slot in (1, 2, 3):
            copy(slot).start()

    def to_levels():
        for slot in (1, 2, 3):
            copy(slot).wait_recv()
        for i in range(4):
            parts = [own[i, x, y]] + [land[j, i] for j in range(3)]
            parts = [p.astype(F32) for p in parts]
            got[i, 0, 0] = (parts[0] + parts[1] + parts[2] + parts[3]).astype(BF16)
        for slot in (4, 5, 6):
            copy(slot).start()

    def total(out):
        for slot in (4, 5, 6):
            copy(slot).wait_recv()
        rest = last[0].astype(F32) + last[1].astype(F32) + last[2].astype(F32)
        out[...] = got[z, 0, 0].astype(F32) + rest

    def drain():
        for slot in range(SCATTER_SLOTS):
            copy(slot).wait_send()

    return to_sibling, to_plane, to_levels, total, drain


SCATTER_SLOTS = 7


def scatter_buffers(rows, width):
    return [pltpu.VMEM(s, BF16) for s in (
        (4, 2, 2, 2, rows, width), (4, 2, 2, rows, width), (4, 2, 2, rows, width), (3, 4, rows, width),
        (3, rows, width))]


def find_cuts(seg, length, cuts):
    def first_at_least(s):
        def step(_, span):
            lo, hi = span
            mid = (lo + hi) // 2
            below = seg[jnp.minimum(mid, length - 1)] < s
            live = lo < hi
            return jnp.where(live & below, mid + 1, lo), jnp.where(live & jnp.logical_not(below), mid, hi)

        return lax.fori_loop(0, length.bit_length(), step, (jnp.int32(0), jnp.int32(length)))[0]

    edges = [jnp.int32(0)] + [first_at_least(s) for s in range(1, SEGMENTS)] + [jnp.int32(length)]
    sizes = [edges[i + 1] - edges[i] for i in range(SEGMENTS)]
    roll, most = edges[0], sizes[0]
    for edge, size in zip(edges[1:], sizes[1:]):
        roll = jnp.where(size > most, edge, roll)
        most = jnp.maximum(size, most)
    cuts[0] = roll
    firsts = []
    for i in range(SEGMENTS):
        at = edges[i] - roll
        firsts.append(jnp.where(at < 0, at + length, at))
        cuts[1 + i] = firsts[i]
        cuts[1 + SEGMENTS + i] = sizes[i]
    return roll, firsts, sizes


def turned(ref, first, rows):
    length = ref.shape[1] - rows
    at = jnp.where(first >= length, first - length, first)
    at = jnp.where(at < 0, at + length, at)
    return jnp.concatenate([ref[i, pl.ds(at, rows), :] for i in range(ref.shape[0])], 1)


def put_columns(ref, at, value):
    for i in range(ref.shape[0]):
        ref[i, at, :] = value[:, 128 * i : 128 * i + 128]


def wrap_columns(ref, rows):
    length = ref.shape[1] - rows
    for i in range(ref.shape[0]):
        ref[i, length:, :] = ref[i, :rows, :]


def enter_kernel(linked, seg, tok, stamps, flags, *refs):
    if linked:
        vectors, stamps_table, s_in, s_out, s_up, s_down = refs[:8], *refs[8:13]
        refs = refs[13:]
        (start_o, normt_o, packed_o, mq_o, mk_o, vec_o, hid_o, cuts, win_o, wout_o, feed_o,
         s_small, small, w_in, send, recv, local, fsend, frecv, flocal) = refs[:20]
        refs = refs[20:]
    else:
        small, w_in, start_o, normt_o, packed_o, mq_o, mk_o, vec_o, hid_o, cuts = refs[:10]
        refs = refs[10:]
    tokv, startf, startv, normv, normtv, packv, mqv, mkv, table, moved = refs
    count, width = tok.shape
    rows = min(TILE, count)
    tiles = count // rows
    fetch = pltpu.make_async_copy(tok, tokv, moved.at[0])
    fetch.start()
    if linked:
        place = position()
        z, x, y, c = place
        greet(*place)
        row = jnp.zeros((1, width), F32)
        at = 0
        for v in vectors:
            size = v.shape[1]
            row = row + dot(v[...], (iota((size, width), 1) == iota((size, width), 0) + at).astype(BF16))
            at += size
        s_small[...] = jnp.concatenate([stamps_table[...].astype(F32), row, jnp.zeros((7, width), F32)], 0).astype(BF16)
        plans = [
            gather_plan(place, s, w, send.at[a], recv.at[a], local.at[a])
            for a, (s, w) in enumerate(
                [(s_small, small)]
                + [(s_in.at[:, width * i : width * i + width], w_in.at[i]) for i in range(3)]
                + [(s_out, wout_o)]
            )
        ]
        first, *middle, final = plans
        parts = [(s_down, 0, 64)] + [(s_up.at[:, width * j : width * j + width], 64 + 16 * j, 16) for j in range(4)]

        def feed_copy(j, k):
            src, at, size = parts[j]
            dst = feed_o.at[z, at : at + size, :]
            if k == 0:
                return pltpu.make_async_copy(src, dst, flocal.at[j])
            return remote(src, dst, fsend.at[j, k - 1], frecv.at[j, k - 1], device(peer(z, k), x, y, c))

        feeds = [feed_copy(j, k) for j in range(5) for k in range(4)]
        for plan in plans[:4]:
            plan[0]()
    roll, firsts, sizes = find_cuts(seg, count, cuts)
    if linked:
        for plan in plans[:4]:
            plan[1]()
        final[0]()
        for copy in feeds:
            copy.start()
        first[2]()
        first[3]()
    unpack_small(small[...].reshape((-1,) + small.shape[-2:]), vec_o, hid_o, table)
    fetch.wait()
    moves = []

    def move(src, dst):
        copy = pltpu.make_async_copy(src, dst, moved.at[len(moves) + 1])
        copy.start()
        moves.append(copy)

    for t in range(tiles):
        at = slice(rows * t, rows * t + rows)
        select = token_selector(stamps[:, at], flags[:, at], table.shape[0] - 16)
        put_columns(startf, at, tokv[at, :].astype(F32) + dot_tn(select, table[...]))
    wrap_columns(startf, rows)
    lane = iota((1, 128), 1)
    lows, highs = jnp.zeros((1, 128), jnp.int32), jnp.zeros((1, 128), jnp.int32)
    for i in range(SEGMENTS):
        lows = jnp.where(lane == i, firsts[i], lows)
        highs = jnp.where(lane == i, firsts[i] + sizes[i], highs)
    if linked:
        final[1]()
    for t in range(tiles):
        at = slice(rows * t, rows * t + rows)
        start = turned(startf, roll + rows * t, rows)
        startv[at, :] = start
        move(startv.at[at, :], start_o.at[at, :])
        xhat, _ = norm_parts(start)
        normed = (xhat * vec_o[1:2, :] + vec_o[2:3, :]).astype(BF16)
        normv[at, :] = normed
        normtv[:, at] = jnp.transpose(normed, (1, 0))
        row = iota((rows, 128), 0) + rows * t
        member = (row >= lows) & (row < highs)
        mqv[at, :] = jnp.where(member, 1.0, 0.0).astype(BF16)
        mkv[at, :] = jnp.where(member | (lane >= SEGMENTS), 0.0, NEG).astype(BF16)
        if linked and t == 2:
            middle[0][2]()
    move(normtv, normt_o)
    move(mqv, mq_o)
    move(mkv, mk_o)
    for i in range(3):
        cols = slice(width * i, width * i + width)
        if linked:
            middle[i][3]()
            weights = w_in[i].reshape(width, width)
            if i < 2:
                middle[i + 1][2]()
            else:
                final[2]()
        else:
            weights = w_in[:, cols]
        for t in range(tiles):
            at = slice(rows * t, rows * t + rows)
            value = dot(normv[at, :], weights)
            packv[at, cols] = (value * SCALE if i == 0 else value).astype(BF16)
        move(packv.at[:, cols], packed_o.at[:, cols])
    if linked:
        move(w_in, win_o)
    for copy in moves:
        copy.wait()
    if linked:
        final[3]()
        for plan in plans:
            plan[4]()
        for copy in feeds:
            copy.wait()


def unpack_small(flat16, vec_o, hid_o, table):
    devices, _, width = flat16.shape
    steps = devices * 8
    flat = flat16.astype(F32)
    row = flat[:, 8, :].astype(BF16)
    per = width // devices
    lane = iota((devices, width), 1)
    spread = jnp.concatenate([jnp.where(lane // per == i, row, jnp.zeros_like(row)) for i in range(7)], 0)
    same = (iota((width, width), 0) % per == iota((width, width), 1) % per).astype(BF16)
    wide = dot(spread, same).reshape(7, devices, width)
    mine = (lane // per == iota((devices, width), 0))[None]
    vecs = jnp.sum(jnp.where(mine, wide, 0.0), axis=1)
    vec_o[...] = jnp.concatenate([vecs, jnp.zeros((1, width), F32)], 0)
    hidden = hid_o.shape[1]
    part = hidden // devices
    at = iota((width, hidden), 0) - 7 * per
    pick = (at == iota((width, hidden), 1) % part).astype(BF16)
    own = iota((devices, hidden), 1) // part == iota((devices, hidden), 0)
    hid_o[...] = jnp.sum(jnp.where(own, dot(row, pick), 0.0), axis=0, keepdims=True)
    table[:steps, :] = flat[:, :8, :].reshape(steps, width).astype(BF16)
    table[steps:, :] = jnp.where(iota((16, width), 0) == 0, vecs[0:1], 0.0).astype(BF16)


def token_selector(stamps, flags, steps):
    rows = stamps.shape[1]
    chosen = (stamps == iota((steps, rows), 0)).astype(F32)
    flagged = jnp.where(iota((16, rows), 0) == 0, flags.astype(F32), 0.0)
    return jnp.concatenate([chosen, flagged], 0).astype(BF16)


def enter(tokens, segments, stamps, flags, hidden, shards, small, w_in):
    count, width = tokens.shape
    linked = shards is not None
    rows = min(TILE, count)
    anywhere = pl.BlockSpec(memory_space=pl.ANY)
    inside = pl.BlockSpec(memory_space=pltpu.VMEM)
    scalars = pl.BlockSpec(memory_space=pltpu.SMEM)
    lot = lambda *s: pltpu.SemaphoreType.DMA(s)
    big = lambda w, d: pltpu.VMEM((count, w), d)
    full = lambda a: (4, 2, 2, 2) + a
    outs = [
        jax.ShapeDtypeStruct((count, width), F32),
        jax.ShapeDtypeStruct((width, count), BF16),
        jax.ShapeDtypeStruct((count, 3 * width), BF16),
        jax.ShapeDtypeStruct((count, 128), BF16),
        jax.ShapeDtypeStruct((count, 128), BF16),
        jax.ShapeDtypeStruct((8, width), F32),
        jax.ShapeDtypeStruct((1, hidden), F32),
        jax.ShapeDtypeStruct((16,), jnp.int32),
    ]
    out_specs = [anywhere] * 5 + [inside] * 2 + [scalars]
    if linked:
        *vectors, stamps_table, s_in, s_out, s_up, s_down = shards
        operands = shards
        in_specs = [inside] * 9 + [anywhere] * 4
        outs += [
            jax.ShapeDtypeStruct((3,) + full(s_out.shape), BF16),
            jax.ShapeDtypeStruct(full(s_out.shape), BF16),
            jax.ShapeDtypeStruct((4, s_down.shape[0] + 64, width), BF16),
        ]
        out_specs += [anywhere] * 3
        scratch = [
            pltpu.VMEM((16, width), BF16), pltpu.VMEM(full((16, width)), BF16),
            pltpu.VMEM((3,) + full(s_out.shape), BF16),
            lot(5, GATHER_SLOTS), lot(5, GATHER_SLOTS), lot(5), lot(5, 3), lot(5, 3), lot(5),
        ]
        steps = 256
        compiler = params(collective_id=0, has_side_effects=True)
    else:
        operands, in_specs, scratch = [small, w_in], [inside] * 2, []
        steps = small.shape[0] * 8
        compiler = params()
    outs = pl.pallas_call(
        functools.partial(enter_kernel, linked),
        in_specs=[scalars, anywhere, inside, inside] + in_specs,
        out_specs=out_specs,
        out_shape=outs,
        scratch_shapes=scratch + [
            big(width, BF16), pltpu.VMEM((width // 128, count + rows, 128), F32), big(width, F32), big(width, BF16),
            pltpu.VMEM((width, count), BF16), big(3 * width, BF16), big(128, BF16), big(128, BF16),
            pltpu.VMEM((steps + 16, width), BF16), lot(16),
        ],
        compiler_params=compiler,
        name="enter",
    )(segments, tokens, stamps, flags, *operands)
    return list(outs)


def key_range(cuts, row, rows):
    lo, hi = jnp.int32(1 << 20), jnp.int32(0)
    for i in range(SEGMENTS):
        first, size = cuts[1 + i], cuts[1 + SEGMENTS + i]
        meets = (size > 0) & (first < row + rows) & (first + size > row)
        lo = jnp.where(meets, jnp.minimum(lo, first), lo)
        hi = jnp.where(meets, jnp.maximum(hi, first + size), hi)
    return lo, hi


def list_tiles(cuts, length, tile, qi, ki):
    blank = length // tile
    qi[0], ki[0] = jnp.int32(blank), jnp.int32(blank)

    def one(t, n):
        lo, hi = key_range(cuts, t * tile, tile)

        def put(j, n):
            qi[n], ki[n] = t, j
            return n + 1

        return lax.fori_loop(lo // tile, (hi + tile - 1) // tile, put, n)

    n = lax.fori_loop(0, blank, one, jnp.int32(1))
    for i in range(2):
        qi[n + i], ki[n + i] = jnp.int32(blank), jnp.int32(blank)
    return (n - 1) // 2 + 1


def spots(qi, ki, i, tile, length):
    q, k = pl.multiple_of(qi[i] * tile, tile), pl.multiple_of(ki[i] * tile, tile)
    q_in, k_in = (pl.multiple_of(jnp.where(v >= length, 0, v), tile) for v in (q, k))
    return pl.ds(q_in, tile), pl.ds(k_in, tile), pl.ds(q, tile), pl.ds(k, tile)


def head_masks():
    first = iota((1, 128), 1) < HD
    return [jnp.where(first == (h == 0), 1.0, 0.0).astype(BF16) for h in range(2)]


def fwd_kernel(length, tile, npair, cuts, q_ref, k_ref, v_ref, mq_ref, mk_ref, o_ref, lse_ref,
               vt, acc, top, alpha, ps, qi, ki):
    g = pl.program_id(0)
    heads = 2 * npair
    only = head_masks()
    ones = jnp.ones((16, tile), BF16)
    count = list_tiles(cuts, length, tile, qi, ki)
    vt[...] = jnp.transpose(v_ref[...], (1, 0))
    acc[...] = jnp.zeros_like(acc)
    top[...] = jnp.full_like(top, -3e38)

    def scan(i, slot, hs):
        q_in, k_in, q, _ = spots(qi, ki, i, tile, length)
        for h in hs:
            cols = slice(128 * (h // 2), 128 * (h // 2) + 128)
            s = dot_nt(jnp.concatenate([k_ref[k_in, cols], mk_ref[k_in, :]], 1),
                       jnp.concatenate([q_ref[q_in, cols] * only[h % 2], mq_ref[q_in, :]], 1))
            old = top[h : h + 1, q]
            new = jnp.maximum(old, jnp.max(s, axis=0, keepdims=True))
            top[h : h + 1, q] = new
            alpha[slot, h : h + 1] = jnp.exp(old - new)
            ps[slot, h] = jnp.exp(s - new).astype(BF16)

    def mix(i, slot, hs):
        _, k_in, q, _ = spots(qi, ki, i, tile, length)
        for h in hs:
            values = jnp.concatenate([vt[HD * h : HD * h + HD, k_in], ones], 0)
            acc[h, :, q] = acc[h, :, q] * alpha[slot, h : h + 1] + dot(values, ps[slot, h])

    def step(m, _):
        def both(a, sa, b, sb):
            for h in range(heads):
                mix(a, sa, [h])
                scan(b, sb, [h])

        both(2 * m, 1, 2 * m + 1, 0)
        both(2 * m + 1, 0, 2 * m + 2, 1)
        return 0

    lax.fori_loop(0, count, step, 0)
    for i in range(npair):
        both = []
        for h in (2 * i, 2 * i + 1):
            total = acc[h, HD : HD + 1, :length]
            both.append(acc[h, :HD, :length] / total)
            lse_ref[pl.ds(heads * g + h, 1), :] = top[h : h + 1, :length] + jnp.log(total)
        o_ref[:, 128 * i : 128 * i + 128] = jnp.transpose(jnp.concatenate(both, 0), (1, 0)).astype(BF16)


def attention_forward(packed, cuts, mq, mk, tile, npair):
    length = packed.shape[0]
    steps = 4 // npair
    w, heads = 128 * npair, 2 * npair
    most = (length // tile) ** 2 + 8
    col = lambda o: pl.BlockSpec((length, w), lambda g, s: (0, g + o * steps))
    whole = pl.BlockSpec((length, 128), lambda g, s: (0, 0))
    return pl.pallas_call(
        functools.partial(fwd_kernel, length, tile, npair),
        grid_spec=pltpu.PrefetchScalarGridSpec(
            num_scalar_prefetch=1, grid=(steps,),
            in_specs=[col(0), col(1), col(2), whole, whole],
            out_specs=[col(0), pl.BlockSpec((8, length), lambda g, s: (0, 0))],
            scratch_shapes=[
                pltpu.VMEM((w, length), BF16),
                pltpu.VMEM((heads, HD + 16, length + tile), F32),
                pltpu.VMEM((8, length + tile), F32),
                pltpu.VMEM((2, 8, tile), F32),
                pltpu.VMEM((2, heads, tile, tile), BF16),
                pltpu.SMEM((most,), jnp.int32),
                pltpu.SMEM((most,), jnp.int32),
            ]),
        out_shape=[jax.ShapeDtypeStruct((length, 512), BF16), jax.ShapeDtypeStruct((8, length), F32)],
        compiler_params=params(),
        name="attend_forward",
    )(cuts, packed, packed, packed, mq, mk)


def bwd_kernel(length, tile, npair, cuts, q_ref, k_ref, v_ref, do_ref, mq_ref, mk_ref, lse_ref, delta_ref,
               dq_ref, dk_ref, dv_ref, kt, dk, dv, dqt, ps, dss, qi, ki):
    g = pl.program_id(0)
    heads = 2 * npair
    only = head_masks()
    count = list_tiles(cuts, length, tile, qi, ki)
    kt[...] = jnp.transpose(k_ref[...], (1, 0))
    for ref in (dk, dv, dqt):
        ref[...] = jnp.zeros_like(ref)

    def scan(i, slot):
        q_in, k_in, _, _ = spots(qi, ki, i, tile, length)
        for h in range(heads):
            at = slice(128 * (h // 2), 128 * (h // 2) + 128)
            lse = lse_ref[pl.ds(heads * g + h, 1), q_in]
            delta = delta_ref[pl.ds(heads * g + h, 1), q_in]
            s = dot_nt(jnp.concatenate([k_ref[k_in, at], mk_ref[k_in, :]], 1),
                       jnp.concatenate([q_ref[q_in, at] * only[h % 2], mq_ref[q_in, :]], 1))
            p = jnp.exp(s - lse)
            dp = dot_nt(v_ref[k_in, at], do_ref[q_in, at] * only[h % 2])
            cols = slice(tile * (h % 2), tile * (h % 2) + tile)
            ps[slot, h // 2, :, cols] = p.astype(BF16)
            dss[slot, h // 2, :, cols] = (p * (dp - delta)).astype(BF16)

    def mix(i, slot):
        q_in, k_in, q, k = spots(qi, ki, i, tile, length)
        for i in range(npair):
            at = slice(128 * i, 128 * i + 128)
            part = do_ref[q_in, at]
            dv[i, k, :] += dot(ps[slot, i], jnp.concatenate([part * only[0], part * only[1]], 0))
            part = q_ref[q_in, at]
            dk[i, k, :] += dot(dss[slot, i], jnp.concatenate([part * only[0], part * only[1]], 0))
            for h in (2 * i, 2 * i + 1):
                rows = slice(HD * h, HD * h + HD)
                cols = slice(tile * (h % 2), tile * (h % 2) + tile)
                dqt[rows, q] += dot(kt[rows, k_in], dss[slot, i, :, cols])

    def step(m, _):
        scan(2 * m + 1, 0)
        mix(2 * m, 1)
        scan(2 * m + 2, 1)
        mix(2 * m + 1, 0)
        return 0

    lax.fori_loop(0, count, step, 0)
    for i in range(npair):
        cols = slice(128 * i, 128 * i + 128)
        dk_ref[:, cols] = dk[i, :length].astype(BF16)
        dv_ref[:, cols] = dv[i, :length].astype(BF16)
        dq_ref[:, cols] = jnp.transpose(dqt[cols, :length] * SCALE, (1, 0)).astype(BF16)


def attention_backward(packed, dmix, cuts, mq, mk, lse, delta, tile, npair):
    length = packed.shape[0]
    steps = 4 // npair
    w, heads = 128 * npair, 2 * npair
    most = (length // tile) ** 2 + 8
    col = lambda o: pl.BlockSpec((length, w), lambda g, s: (0, g + o * steps))
    whole = pl.BlockSpec((length, 128), lambda g, s: (0, 0))
    rowspec = pl.BlockSpec((8, length), lambda g, s: (0, 0))
    return pl.pallas_call(
        functools.partial(bwd_kernel, length, tile, npair),
        grid_spec=pltpu.PrefetchScalarGridSpec(
            num_scalar_prefetch=1, grid=(steps,),
            in_specs=[col(0), col(1), col(2), col(0), whole, whole, rowspec, rowspec],
            out_specs=[col(0)] * 3,
            scratch_shapes=[
                pltpu.VMEM((w, length), BF16),
                pltpu.VMEM((npair, length + tile, 128), F32),
                pltpu.VMEM((npair, length + tile, 128), F32),
                pltpu.VMEM((w, length + tile), F32),
                pltpu.VMEM((2, npair, tile, 2 * tile), BF16),
                pltpu.VMEM((2, npair, tile, 2 * tile), BF16),
                pltpu.SMEM((most,), jnp.int32),
                pltpu.SMEM((most,), jnp.int32),
            ]),
        out_shape=[jax.ShapeDtypeStruct((length, 512), BF16)] * 3,
        compiler_params=params(),
        name="attend_backward",
    )(cuts, packed, packed, packed, dmix, mq, mk, lse, delta)


def gelu_parts(v):
    phi = 0.5 * lax.erf(v * 0.7071067811865476) + 0.5
    return v * phi, phi + v * (jnp.exp(v * v * -0.5) * 0.3989422804014327)


def feed_kernel(linked, tiles, chunks, cuts, start, mix, cot, w_out, vec, hid, *refs):
    if linked:
        lands = refs[:4]
        out_o, gmid_o, dmix_o, delta_o, gvec_o, ghid_o = refs[4:10]
        leaves = refs[10:14]
        refs = refs[14:]
    else:
        up_all, down_all = refs[:2]
        out_o, gmid_o, dmix_o, delta_o, gvec_o, ghid_o, gup_o, gdown_o, gout_o = refs[2:11]
        refs = refs[11:]
    mid, res, gn2, n2, n2t, br, brt, act0, act1, gpre0, gpre1, gup, gdt, gout, cotf, csem = refs[:16]
    s = pl.program_id(0)
    t_rows, width = start.shape
    f = act0.shape[1]
    roll = cuts[0]
    count = mid.shape[0]

    def cot_copy(i, j):
        at = pl.ds(0, count) if j == 0 else pl.ds(0, t_rows)
        to = pl.ds(0, count) if j == 0 else pl.ds(count, t_rows)
        return pltpu.make_async_copy(cot.at[at, pl.ds(128 * i, 128)], cotf.at[i, to, :], csem.at[i, j])

    cot_copies = [(i, j) for i in range(width // 128) for j in range(2)]
    half = tiles // 2
    middle_steps = chunks * half
    if linked:
        up, down, sent, kept, got, lsem, lsend, lrecv, esend, erecv, eout = refs[16:]
        place = position()
        z, x, y, c = place
        sibling = device(z, x, y, 1 - c)
        spots = ((x, y), (1 - x, y), (x, 1 - y), (1 - x, 1 - y))

        def arrive(i, j, kind):
            xs, ys = spots[i]
            if j == 0:
                src, dst = lands[i].at[:, :64, :], down.at[:, xs, ys, c]
            else:
                src = lands[i].at[:, 48 + 16 * j : 64 + 16 * j, :]
                dst = up.at[:, xs, ys, c, :, width * (j - 1) : width * j]
            if kind == 0:
                return pltpu.make_async_copy(src, dst, lsem.at[i, j])
            return remote(src, dst, lsend.at[i, j], lrecv.at[i, j], sibling)

        arrivals = [(i, j) for i in range(4) for j in range(5)]

        def exchange(j):
            at = slice(0, 128) if j == 0 else slice(128, 144)
            return remote(sent.at[:, :, :, at, :], got.at[:, :, :, at, :], esend.at[j], erecv.at[j], sibling)

        def leave(i):
            xs, ys = spots[i]
            return pltpu.make_async_copy(got.at[:, xs, ys], leaves[i], eout.at[i])


    def rows_at(t):
        return pl.ds(pl.multiple_of(t * t_rows, t_rows), t_rows)

    def cols_at(c):
        return pl.ds(pl.multiple_of(c * f, f), f)

    def up_chunk(ch):
        if linked:
            return up[:, :, :, :, :, cols_at(ch)].reshape(width, f)
        return up_all[:, cols_at(ch)]

    def down_chunk(ch):
        if linked:
            return down[ch].reshape(f, width)
        return down_all[cols_at(ch), :]

    @pl.when(s == 0)
    def _():
        if linked:
            barrier = pltpu.get_barrier_semaphore()
            pl.semaphore_signal(barrier, inc=1, device_id=sibling, device_id_type=MESH)
            pl.semaphore_wait(barrier, 1)
            for i, j in arrivals:
                arrive(i, j, 0).start()
                arrive(i, j, 1).start()
        for i, j in cot_copies:
            cot_copy(i, j).start()
        for ref in (act1, gpre1, gup, gdt, gn2, gout, gvec_o, ghid_o):
            ref[...] = jnp.zeros_like(ref)
        for i, j in cot_copies:
            cot_copy(i, j).wait()

    @pl.when(s < tiles)
    def _():
        rows = rows_at(s)
        middle = start[...] + dot(mix[...], w_out[...]) + vec[3:4, :]
        mid[rows, :] = middle
        put_columns(res, rows, middle + vec[6:7, :])
        xhat, _ = norm_parts(middle)
        normed = (xhat * vec[4:5, :] + vec[5:6, :]).astype(BF16)
        n2[rows, :] = normed
        n2t[:, rows] = jnp.transpose(normed, (1, 0))
        branch = turned(cotf, roll + s * t_rows, t_rows).astype(BF16)
        br[rows, :] = branch
        brt[:, rows] = jnp.transpose(branch, (1, 0))
        gvec_o[3:4, :] += jnp.sum(branch.astype(F32), axis=0, keepdims=True)

    if linked:
        @pl.when(s == tiles)
        def _():
            for i, j in arrivals:
                arrive(i, j, 0).wait()
                arrive(i, j, 1).wait()

    def inner(ch, t, act, gpre):
        cols, rows = cols_at(ch), rows_at(t)
        pre = dot(n2[rows, :], up_chunk(ch)) + hid[:, cols]
        grad = dot_nt(br[rows, :], down_chunk(ch))
        value, slope = gelu_parts(pre)
        act[...] = value.astype(BF16)
        low = (grad * slope).astype(BF16)
        gpre[...] = low
        ghid_o[:, cols] += jnp.sum(low.astype(F32), axis=0, keepdims=True)

    def outer(ch, t, act, gpre):
        cols, rows = cols_at(ch), rows_at(t)
        a, g = act[...], gpre[...]
        more = dot(a, down_chunk(ch))
        for i in range(width // 128):
            res[i, rows, :] += more[:, 128 * i : 128 * i + 128]
        gn2[rows, :] += dot_nt(g, up_chunk(ch))
        gup[:, cols] += dot(n2t[:, rows], g)
        gdt[:, cols] += dot(brt[:, rows], a)

    @pl.when((s >= tiles) & (s < tiles + middle_steps))
    def _():
        b = s - tiles
        before = jnp.maximum(b - 1, 0)
        ch, t = b // half, 2 * (b % half)
        outer(before // half, 2 * (before % half) + 1, act1, gpre1)
        inner(ch, t, act0, gpre0)
        outer(ch, t, act0, gpre0)
        inner(ch, t + 1, act1, gpre1)

    @pl.when(s == tiles + middle_steps)
    def _():
        outer(chunks - 1, tiles - 1, act1, gpre1)
        wrap_columns(res, t_rows)
        if linked:
            for i in range(4):
                block = jnp.transpose(gdt[:, 512 * i : 512 * i + 512], (1, 0)).reshape(2, 2, 2, 64, width)
                first, second = block[:, :, 0], block[:, :, 1]
                kept[i, :, :, :64, :] = jnp.where(c == 0, first, second).astype(BF16)
                sent[i, :, :, :64, :] = jnp.where(c == 0, second, first).astype(BF16)
                cols = slice(width * i, width * i + width)
                block = gup[:, cols].reshape(4, 2, 2, 2, 16, width)
                first, second = block[:, :, :, 0], block[:, :, :, 1]
                at = slice(64 + 16 * i, 80 + 16 * i)
                kept[:, :, :, at, :] = jnp.where(c == 0, first, second).astype(BF16)
                sent[:, :, :, at, :] = jnp.where(c == 0, second, first).astype(BF16)
            exchange(0).start()
        else:
            for i in range(chunks):
                gup_o[:, i * f : (i + 1) * f] = gup[:, i * f : (i + 1) * f].astype(BF16)
                gdown_o[i * f : (i + 1) * f, :] = jnp.transpose(gdt[:, i * f : (i + 1) * f], (1, 0)).astype(BF16)

    @pl.when(s >= tiles + middle_steps)
    def _():
        t = s - tiles - middle_steps
        rows = rows_at(t)
        out_o[...] = turned(res, t * t_rows - roll, t_rows).astype(BF16)
        xhat, rstd = norm_parts(mid[rows, :])
        n = gn2[rows, :]
        grad = turned(cotf, roll + t * t_rows, t_rows) + norm_back(n, xhat, rstd, vec[4:5, :])
        gmid_o[...] = grad
        low = grad.astype(BF16)
        gvec_o[0:1, :] += jnp.sum(low.astype(F32), axis=0, keepdims=True)
        gvec_o[1:2, :] += jnp.sum(n * xhat, axis=0, keepdims=True)
        gvec_o[2:3, :] += jnp.sum(n, axis=0, keepdims=True)
        mixed = mix[...]
        gout[...] += dot_tn(mixed, low)
        dmix = dot_nt(low, w_out[...]).astype(BF16)
        dmix_o[...] = dmix
        prod = dmix.astype(F32) * mixed.astype(F32)
        high = prod.astype(BF16)
        rest = (prod - high.astype(F32)).astype(BF16)
        heads = (iota((16, prod.shape[1]), 1) // HD == iota((16, prod.shape[1]), 0)).astype(BF16)
        delta_o[...] = (dot_nt(heads, high) + dot_nt(heads, rest))[:8]

    @pl.when(s == 2 * tiles + middle_steps - 1)
    def _():
        if linked:
            block = gout[...].reshape(4, 2, 2, 2, 16, width)
            first, second = block[:, :, :, 0], block[:, :, :, 1]
            kept[:, :, :, 128:, :] = jnp.where(c == 0, first, second).astype(BF16)
            sent[:, :, :, 128:, :] = jnp.where(c == 0, second, first).astype(BF16)
            exchange(1).start()
            exchange(0).wait()
            exchange(1).wait()
            for i in range(4):
                got[i] = (got[i].astype(F32) + kept[i].astype(F32)).astype(BF16)
            for i in range(4):
                leave(i).start()
            for i in range(4):
                leave(i).wait()
        else:
            gout_o[...] = gout[...].astype(BF16)


def feed(cuts, start, mixture, cotangent, w_out, vec, hid, weights, linked):
    count, width = start.shape
    hidden = hid.shape[1]
    rows = min(TILE, count)
    f = min(512, hidden)
    tiles, chunks = count // rows, hidden // f
    middle = chunks * (tiles // 2)
    first = lambda s: jnp.minimum(s, tiles - 1)
    last = lambda s: jnp.maximum(s - tiles - middle, 0)
    both = lambda s: jnp.where(s < tiles + middle, first(s), last(s))
    tile = lambda at: pl.BlockSpec((rows, width), lambda s: (at(s), 0))
    whole = lambda *a: pl.BlockSpec(a, lambda s: (0,) * len(a))
    anywhere = pl.BlockSpec(memory_space=pl.ANY)
    big = lambda d: pltpu.VMEM((count, width), d)
    turning = pltpu.VMEM((width // 128, count + rows, 128), F32)
    lot = lambda *s: pltpu.SemaphoreType.DMA(s)
    scratch = (
        [big(F32), turning, big(F32), big(BF16), pltpu.VMEM((width, count), BF16), big(BF16),
         pltpu.VMEM((width, count), BF16)]
        + [pltpu.VMEM((rows, f), BF16)] * 4
        + [pltpu.VMEM((width, hidden), F32)] * 2
        + [pltpu.VMEM((width, width), F32), turning, lot(width // 128, 2)]
    )
    common = [
        jax.ShapeDtypeStruct((count, width), BF16),
        jax.ShapeDtypeStruct((count, width), F32),
        jax.ShapeDtypeStruct((count, width), BF16),
        jax.ShapeDtypeStruct((8, count), F32),
        jax.ShapeDtypeStruct((8, width), F32),
        jax.ShapeDtypeStruct((1, hidden), F32),
    ]
    if linked:
        weight_specs = [anywhere] * 4
        more = [jax.ShapeDtypeStruct((4, 144, width), BF16)] * 4
        more_specs = [anywhere] * 4
        scratch += [
            pltpu.VMEM((4, 2, 2, 2, 16, hidden), BF16), pltpu.VMEM((4, 2, 2, 2, 64, width), BF16),
        ] + [pltpu.VMEM((4, 2, 2, 144, width), BF16)] * 3 + [lot(4, 5), lot(4, 5), lot(4, 5), lot(2), lot(2), lot(4)]
        compiler = params(collective_id=1, has_side_effects=True)
    else:
        weight_specs = [whole(width, hidden), whole(hidden, width)]
        more = [jax.ShapeDtypeStruct(s, BF16) for s in ((width, hidden), (hidden, width), (width, width))]
        more_specs = [whole(width, hidden), whole(hidden, width), whole(width, width)]
        compiler = params()
    return pl.pallas_call(
        functools.partial(feed_kernel, linked, tiles, chunks),
        grid=(tiles + middle + tiles,),
        in_specs=[pl.BlockSpec(memory_space=pltpu.SMEM), tile(first), tile(both), anywhere, whole(width, width), whole(8, width), whole(1, hidden)] + weight_specs,
        out_specs=[tile(last), tile(last), tile(last), pl.BlockSpec((8, rows), lambda s: (0, last(s))),
                   whole(8, width), whole(1, hidden)] + more_specs,
        out_shape=common + more,
        scratch_shapes=scratch,
        compiler_params=compiler,
        name="feed_forward",
    )(cuts, start, mixture, cotangent, w_out, vec, hid, *weights)


def leave_kernel(linked, tiles, cuts, dq, dk, dv, normt, w_in, start, gmid, stamps, flags, vec, gvec2, ghid, *refs):
    if linked:
        pieces = refs[:4]
        gtok_o, gin_o, gsmall_o, gfeed_o, gtab, gvec, gin, packs, gtokf, esum, egot, esend, erecv = refs[4:17]
        places = [refs[17 + 7 * i : 24 + 7 * i] for i in range(2)]
    else:
        gtok_o, gin_o, gtab, gvec, gin, packs, gtokf = refs
    s = pl.program_id(0)
    rows, width = start.shape
    steps = gtab.shape[0] - 16
    if linked:
        place = position()
        z, x, y, c = place
        plans = [scatter_plan(place, *p) for p in places]

        def level(k):
            return remote(esum.at[peer(z, k)], egot.at[k - 1], esend.at[k - 1], erecv.at[k - 1],
                          device(peer(z, k), x, y, c))

    @pl.when(s == 0)
    def _():
        if linked:
            greet(*place)
            for i in range(4):
                parts = [p[i].astype(F32) for p in pieces]
                esum[i] = (parts[0] + parts[1] + parts[2] + parts[3]).astype(BF16)
            for k in (1, 2, 3):
                level(k).start()
        for ref in (gin, gtab, gvec):
            ref[...] = jnp.zeros_like(ref)

    def rows_at(t):
        return pl.ds(pl.multiple_of(t * rows, rows), rows)

    @pl.when(s < tiles)
    def _():
        at = rows_at(s)
        for i, d in enumerate((dq, dk, dv)):
            cols = slice(width * i, width * (i + 1))
            low = d[...]
            packs[at, cols] = low
            gin[:, cols] += dot(normt[...], low)

    @pl.when(s == tiles - 1)
    def _():
        if linked:
            places[0][0][...] = gin[...].astype(BF16).reshape(places[0][0].shape)
            plans[0][0]()
        else:
            gin_o[...] = gin[...].astype(BF16)

    @pl.when((s >= tiles) & (s < 2 * tiles))
    def _():
        at = rows_at(s - tiles)
        n = sum(dot_nt(packs[at, width * i : width * i + width], w_in[i]) for i in range(3))
        xhat, rstd = norm_parts(start[...])
        grad = gmid[...] + norm_back(n, xhat, rstd, vec[1:2, :])
        put_columns(gtokf, at, grad)
        gvec[0:1, :] += jnp.sum(n * xhat, axis=0, keepdims=True)
        gvec[1:2, :] += jnp.sum(n, axis=0, keepdims=True)

    @pl.when(s == 2 * tiles - 1)
    def _():
        wrap_columns(gtokf, rows)

    @pl.when(s >= 2 * tiles)
    def _():
        grad = turned(gtokf, (s - 2 * tiles) * rows - cuts[0], rows)
        gtok_o[...] = grad
        gtab[...] += dot(token_selector(stamps[...], flags[...], steps), grad.astype(BF16))

    if linked:
        @pl.when(s == tiles)
        def _():
            plans[0][1]()

        @pl.when(s == 3 * tiles - 1)
        def _():
            pack_small(places[1][0], steps, gtab, gvec, gvec2, ghid)
            plans[1][0]()
            plans[0][2]()
            plans[1][1]()
            for k in (1, 2, 3):
                level(k).wait_recv()
            gfeed_o[...] = (esum[z].astype(F32) + egot[0].astype(F32)) + (egot[1].astype(F32) + egot[2].astype(F32))
            plans[1][2]()
            plans[0][3](gin_o)
            plans[1][3](gsmall_o)
            plans[0][4]()
            plans[1][4]()
            for k in (1, 2, 3):
                level(k).wait_send()


def pack_small(full, steps, gtab, gvec, gvec2, ghid):
    width = gtab.shape[1]
    groups = steps // 8
    per = width // groups
    sums = [gtab[steps : steps + 1, :], gvec[0:1, :], gvec[1:2, :]]
    sums += [gvec2[i : i + 1, :] for i in range(4)]
    mine = iota((groups, width), 1) // per == iota((groups, width), 0)
    spread = jnp.concatenate([jnp.where(mine, v, 0.0) for v in sums], 0).astype(BF16)
    same = (iota((width, width), 0) % per == iota((width, width), 1) % per).astype(BF16)
    wide = dot(spread, same).reshape(7, groups, width)
    lane = iota((1, width), 1)
    row = jnp.zeros((groups, width), F32)
    for i in range(7):
        row = jnp.where(lane // per == i, wide[i], row)
    hidden = ghid.shape[1]
    part = hidden // groups
    own = iota((groups, hidden), 1) // part == iota((groups, hidden), 0)
    pick = (iota((hidden, width), 0) % part == iota((hidden, width), 1) - 7 * per).astype(BF16)
    row = row + dot(jnp.where(own, ghid[...], 0.0).astype(BF16), pick)
    table = gtab[:steps, :].reshape(groups, 8, width)
    below = jnp.where(iota((groups, 8, width), 1) == 0, row[:, None, :], 0.0)
    full[...] = jnp.concatenate([table, below], 1).astype(BF16).reshape(full.shape)


def leave(cuts, dq, dk, dv, normt, w_in, start, gmid, stamps, flags, vec, gvec2, ghid, steps, pieces, linked):
    count, width = start.shape
    rows = min(TILE, count)
    tiles = count // rows
    first = lambda s: jnp.minimum(s, tiles - 1)
    second = lambda s: jnp.clip(s - tiles, 0, tiles - 1)
    last = lambda s: jnp.maximum(s - 2 * tiles, 0)
    line = pl.BlockSpec((1, rows), lambda s: (0, last(s)))
    tile = lambda at: pl.BlockSpec((rows, width), lambda s: (at(s), 0))
    whole = lambda *a: pl.BlockSpec(a, lambda s: (0,) * len(a))
    lot = lambda *s: pltpu.SemaphoreType.DMA(s)
    scratch = [pltpu.VMEM((width, 3 * width), F32), pltpu.VMEM((count, 3 * width), BF16),
               pltpu.VMEM((width // 128, count + rows, 128), F32)]
    sums = [jax.ShapeDtypeStruct((steps + 16, width), F32), jax.ShapeDtypeStruct((8, width), F32)]
    held = [pltpu.VMEM(a.shape, F32) for a in sums]
    if linked:
        more = [jax.ShapeDtypeStruct(s, F32) for s in ((16, 3 * width), (16, width), (144, width))]
        scratch = held + scratch + [pltpu.VMEM((4, 144, width), BF16), pltpu.VMEM((3, 144, width), BF16), lot(3), lot(3)]
        for w in (3 * width, width):
            scratch += scatter_buffers(16, w) + [lot(SCATTER_SLOTS), lot(SCATTER_SLOTS)]
        compiler = params(collective_id=2, has_side_effects=True)
    else:
        more = [jax.ShapeDtypeStruct((width, 3 * width), BF16)] + sums
        compiler = params()
    return pl.pallas_call(
        functools.partial(leave_kernel, linked, tiles),
        grid=(3 * tiles,),
        in_specs=[pl.BlockSpec(memory_space=pltpu.SMEM)] + [tile(first)] * 3 + [pl.BlockSpec((width, rows), lambda s: (0, first(s))), whole(*w_in.shape), tile(second),
                  tile(second), line, line, whole(8, width), whole(8, width),
                  whole(*ghid.shape)] + [whole(*p.shape) for p in pieces],
        out_specs=[tile(last)] + [whole(*a.shape) for a in more],
        out_shape=[jax.ShapeDtypeStruct((count, width), F32)] + more,
        scratch_shapes=scratch,
        compiler_params=compiler,
        name="leave",
    )(cuts, dq, dk, dv, normt, w_in, start, gmid, stamps, flags, vec, gvec2, ghid, *pieces)


def unpack_kernel(sizes, gsmall, gfeed, gtab_o, gout_o, gup_o, gdown_o, *vecs):
    width = gsmall.shape[1]
    gtab_o[...] = gsmall[:8, :]
    gdown_o[...] = gfeed[:64, :]
    for i in range(gup_o.shape[1] // width):
        gup_o[:, width * i : width * (i + 1)] = gfeed[64 + 16 * i : 80 + 16 * i, :]
    gout_o[...] = gfeed[128:144, :]
    at = 0
    for ref, size in zip(vecs, sizes):
        ref[...] = gsmall[8:9, at : at + size]
        at += size


def unpack(gsmall, gfeed, hidden, sizes):
    width = gsmall.shape[1]
    shapes = [(8, width), (16, width), (16, hidden), (64, width)] + [(1, n) for n in sizes]
    return pl.pallas_call(
        functools.partial(unpack_kernel, sizes),
        out_shape=[jax.ShapeDtypeStruct(s, F32) for s in shapes],
        compiler_params=params(),
        name="unpack",
    )(gsmall, gfeed)


def exchange_plane(arrays):
    out = [arrays[0]]
    for array, (dx, dy) in zip(arrays[1:], ((1, 0), (0, 1), (1, 1))):
        pairs = [(4 * dp + fs, 4 * (dp ^ dx) + (fs ^ (2 * dy))) for dp in range(8) for fs in range(4)]
        out.append(lax.ppermute(array, AXES, pairs))
    return out


def per_device(fast, tokens, mask_flags, timesteps, segment_ids, mask_embed, time_table, first_gain, first_bias,
               input_proj, output_proj, output_bias, second_gain, second_bias, hidden_weight, hidden_bias,
               down_weight, down_bias, cotangent):
    count, width = tokens.shape
    hidden = hidden_weight.shape[1]
    vectors = (mask_embed, first_gain, first_bias, output_bias, second_gain, second_bias, down_bias)
    segments = segment_ids.reshape(-1)
    stamps, flags = timesteps[None], mask_flags[None]
    if fast:
        lines = [v[None] for v in vectors + (hidden_bias,)]
        sizes = [v.shape[1] for v in lines]
        shards = lines + [time_table, input_proj, output_proj, hidden_weight, down_weight]
        *kept, w_in, w_out, own = enter(tokens, segments, stamps, flags, hidden, shards, None, None)
        w_in, w_out = w_in.reshape(3, width, width), w_out.reshape(width, width)
        steps = time_table.shape[0] * 32
        weights = exchange_plane([own] * 4)
    else:
        whole = lambda a: lax.all_gather(a, AXES, axis=0, tiled=True)
        groups = whole(time_table).reshape(-1, 8, width)
        pieces = jnp.concatenate(
            [whole(v).reshape(groups.shape[0], -1) for v in vectors + (hidden_bias,)], 1
        )
        pieces = jnp.pad(pieces, ((0, 0), (0, width - pieces.shape[1])))[:, None]
        small = jnp.concatenate([groups, pieces, jnp.zeros((groups.shape[0], 7, width), BF16)], 1)
        w_in, w_out = whole(input_proj), whole(output_proj)
        weights = [whole(hidden_weight), whole(down_weight)]
        steps = groups.shape[0] * 8
        kept = enter(tokens, segments, stamps, flags, hidden, None, small, w_in)
        w_in = w_in.reshape(width, 3, width).transpose(1, 0, 2)
    start, normt, packed, mq, mk, vec, hid, cuts = kept

    mixture, lse = attention_forward(packed, cuts, mq, mk, 256, 4)
    out, gmid, dmix, delta, gvec2, ghid, *grads = feed(cuts, start, mixture, cotangent, w_out, vec, hid, weights, fast)
    pieces = exchange_plane(grads) if fast else []
    dq, dk, dv = attention_backward(packed, dmix, cuts, mq, mk, lse, delta, 256, 2)
    gtok, gin, *rest = leave(
        cuts, dq, dk, dv, normt, w_in, start, gmid, stamps, flags, vec, gvec2, ghid, steps, pieces, fast
    )
    if fast:
        gtab, gout, gup, gdown, *small = unpack(rest[0], rest[1], hidden, sizes)
        gmask, gg1, gb1, gob, gg2, gb2, gdb, ghb = [v.reshape(-1) for v in small]
    else:
        total = lambda a: lax.psum_scatter(a.astype(F32), AXES, scatter_dimension=0, tiled=True)
        gtab, gvec1 = rest
        gup, gdown, gout = grads
        gin, gout, gup, gdown = (total(a) for a in (gin, gout, gup, gdown))
        gmask = total(gtab[steps])
        gtab = total(gtab[:steps])
        gg1, gb1, gob, gg2, gb2, gdb, ghb = (
            total(a) for a in (gvec1[0], gvec1[1], gvec2[0], gvec2[1], gvec2[2], gvec2[3], ghid[0])
        )
    return (out, gtok, gmask, gtab, gg1, gb1, gin, gout, gob, gg2, gb2, gup, ghb, gdown, gdb)


def solution(mesh):
    split = P(AXES)
    rows = P(AXES, None)
    fast = tuple(mesh.shape[a] for a in AXES) == (8, 4)
    placed = (rows, split, split, rows, split, rows, split, split, rows, rows, split, split, split, rows, split, rows,
              split, rows)
    return jax.shard_map(
        functools.partial(per_device, fast),
        mesh=mesh,
        in_specs=placed,
        out_specs=(rows, rows, split, rows, split, split, rows, rows, split, split, split, rows, split, rows, split),
        check_vma=False,
    )
```

```python
import functools

import jax
import jax.numpy as jnp
from jax import lax
from jax.experimental import pallas as pl
from jax.experimental.pallas import tpu as pltpu
from jax.sharding import PartitionSpec as P

F32, BF16 = jnp.float32, jnp.bfloat16
HD = 64
SEGMENTS = 4
SCALE = HD ** -0.5
NEG = -1e30
EPSILON = 1e-05
AXES = ("dp", "fsdp")
MESH = pl.DeviceIdType.MESH
VMEM_BYTES = 58 << 20
TILE = 512


def dot(a, b):
    return jnp.dot(a, b, preferred_element_type=F32)


def dot_nt(a, b):
    return lax.dot_general(a, b, (((1,), (1,)), ((), ())), preferred_element_type=F32)


def dot_tn(a, b):
    return lax.dot_general(a, b, (((0,), (0,)), ((), ())), preferred_element_type=F32)


def iota(shape, dim):
    return lax.broadcasted_iota(jnp.int32, shape, dim)


def params(room=VMEM_BYTES, **more):
    return pltpu.CompilerParams(vmem_limit_bytes=room, **more)


def norm_parts(h):
    centered = h - jnp.mean(h, axis=-1, keepdims=True)
    rstd = lax.rsqrt(jnp.mean(centered * centered, axis=-1, keepdims=True) + EPSILON)
    return centered * rstd, rstd


def norm_back(n, xhat, rstd, gain):
    ng = n * gain
    first = jnp.mean(ng, axis=-1, keepdims=True)
    second = jnp.mean(ng * xhat, axis=-1, keepdims=True)
    return rstd * (ng - first - xhat * second)


def position():
    dp, fs = lax.axis_index("dp"), lax.axis_index("fsdp")
    return dp // 2, dp % 2, fs // 2, fs % 2


def device(z, x, y, c):
    return (z * 2 + x, y * 2 + c)


def peer(z, k):
    return lax.rem(z + k, 4)


def greet(z, x, y, c):
    barrier = pltpu.get_barrier_semaphore()
    partners = [device(peer(z, k), x, y, c) for k in (1, 2, 3)]
    partners += [device(z, xs, ys, c) for xs, ys in plane(x, y)[1:]] + [device(z, x, y, 1 - c)]
    for partner in partners:
        pl.semaphore_signal(barrier, inc=1, device_id=partner, device_id_type=MESH)
    pl.semaphore_wait(barrier, len(partners))


def remote(src, dst, send, recv, target):
    return pltpu.make_async_remote_copy(
        src_ref=src, dst_ref=dst, send_sem=send, recv_sem=recv, device_id=target, device_id_type=MESH
    )


def plane(x, y):
    return ((x, y), (1 - x, y), (x, 1 - y), (1 - x, 1 - y))


def gather_plan(place, shard, whole, send, recv, local):
    z, x, y, c = place
    spots = plane(x, y)
    level = lambda k: peer(z, 4 - k)

    def copy(slot):
        if slot < 4 and slot:
            src, dst, to = shard, whole.at[z, x, y, c], device(peer(z, slot), x, y, c)
        elif 4 <= slot < 16:
            k = slot % 4
            dst, to = whole.at[level(k), x, y, c], device(z, *spots[slot // 4], c)
            src = dst if k else shard
        else:
            xs, ys = spots[max(slot - 15, 0)]
            src = dst = whole.at[:, xs, ys, c]
            to = device(z, x, y, 1 - c)
        return remote(src, dst, send.at[slot], recv.at[slot], to)

    keep = pltpu.make_async_copy(shard, whole.at[z, x, y, c], local)

    def begin():
        keep.start()
        for k in (1, 2, 3):
            copy(k).start()

    def spread():
        for k in range(4):
            if k:
                copy(k).wait_recv()
            for kind in (4, 8, 12):
                copy(kind + k).start()
        keep.wait()
        copy(0).start()

    def finish():
        for i in range(3):
            for k in range(4):
                copy(4 + 4 * i + k).wait_recv()
            copy(16 + i).start()

    def ready():
        for slot in (0, 16, 17, 18):
            copy(slot).wait_recv()

    def drain():
        for slot in range(GATHER_SLOTS):
            copy(slot).wait_send()

    return begin, spread, finish, ready, drain


GATHER_SLOTS = 19


def scatter_plan(place, full, own, got, land, last, send, recv):
    z, x, y, c = place
    spots = plane(x, y)

    def copy(slot):
        if slot == 0:
            src, dst, to = full.at[:, :, :, 1 - c], got, device(z, x, y, 1 - c)
        elif slot < 4:
            xs, ys = spots[slot]
            src, dst, to = own.at[:, xs, ys], land.at[slot - 1], device(z, xs, ys, c)
        else:
            k = slot - 3
            src, dst, to = got.at[peer(z, k), 0, 0], last.at[k - 1], device(peer(z, k), x, y, c)
        return remote(src, dst, send.at[slot], recv.at[slot], to)

    def to_sibling():
        copy(0).start()

    def to_plane():
        copy(0).wait_recv()
        for i in range(4):
            own[i] = (full[i, :, :, c].astype(F32) + got[i].astype(F32)).astype(BF16)
        for slot in (1, 2, 3):
            copy(slot).start()

    def to_levels():
        for slot in (1, 2, 3):
            copy(slot).wait_recv()
        for i in range(4):
            parts = [own[i, x, y]] + [land[j, i] for j in range(3)]
            parts = [p.astype(F32) for p in parts]
            got[i, 0, 0] = (parts[0] + parts[1] + parts[2] + parts[3]).astype(BF16)
        for slot in (4, 5, 6):
            copy(slot).start()

    def total(out, at):
        for slot in (4, 5, 6):
            copy(slot).wait_recv()
        rest = last[0].astype(F32) + last[1].astype(F32) + last[2].astype(F32)
        out[:, at : at + rest.shape[1]] = got[z, 0, 0].astype(F32) + rest

    def drain():
        for slot in range(SCATTER_SLOTS):
            copy(slot).wait_send()

    return to_sibling, to_plane, to_levels, total, drain


SCATTER_SLOTS = 7


def scatter_buffers(rows, width):
    return [pltpu.VMEM(s, BF16) for s in (
        (4, 2, 2, 2, rows, width), (4, 2, 2, rows, width), (4, 2, 2, rows, width), (3, 4, rows, width),
        (3, rows, width))]


def find_cuts(seg, length, cuts):
    def first_at_least(s):
        def step(_, span):
            lo, hi = span
            mid = (lo + hi) // 2
            below = seg[jnp.minimum(mid, length - 1)] < s
            live = lo < hi
            return jnp.where(live & below, mid + 1, lo), jnp.where(live & jnp.logical_not(below), mid, hi)

        return lax.fori_loop(0, length.bit_length(), step, (jnp.int32(0), jnp.int32(length)))[0]

    edges = [jnp.int32(0)] + [first_at_least(s) for s in range(1, SEGMENTS)] + [jnp.int32(length)]
    sizes = [edges[i + 1] - edges[i] for i in range(SEGMENTS)]
    roll, most = edges[0], sizes[0]
    for edge, size in zip(edges[1:], sizes[1:]):
        roll = jnp.where(size > most, edge, roll)
        most = jnp.maximum(size, most)
    cuts[0] = roll
    firsts = []
    for i in range(SEGMENTS):
        at = edges[i] - roll
        firsts.append(jnp.where(at < 0, at + length, at))
        cuts[1 + i] = firsts[i]
        cuts[1 + SEGMENTS + i] = sizes[i]
    return roll, firsts, sizes


def turned(ref, first, rows):
    length = ref.shape[1] - rows
    at = jnp.where(first >= length, first - length, first)
    at = jnp.where(at < 0, at + length, at)
    return jnp.concatenate([ref[i, pl.ds(at, rows), :] for i in range(ref.shape[0])], 1)


def put_columns(ref, at, value):
    for i in range(ref.shape[0]):
        ref[i, at, :] = value[:, 128 * i : 128 * i + 128]


def wrap_columns(ref, rows):
    length = ref.shape[1] - rows
    for i in range(ref.shape[0]):
        ref[i, length:, :] = ref[i, :rows, :]


def enter_kernel(linked, seg, tok, stamps, flags, *refs):
    if linked:
        vectors, stamps_table, s_in, s_out, s_up, s_down = refs[:8], *refs[8:13]
        refs = refs[13:]
        (start_o, normt_o, packed_o, mq_o, mk_o, vec_o, hid_o, cuts, win_o, wout_o, feed_o,
         s_small, small, w_in, send, recv, local, fsend, frecv, flocal) = refs[:20]
        refs = refs[20:]
    else:
        small, w_in, start_o, normt_o, packed_o, mq_o, mk_o, vec_o, hid_o, cuts = refs[:10]
        refs = refs[10:]
    tokv, startf, startv, normv, normtv, packv, mqv, mkv, table, moved = refs
    count, width = tok.shape
    rows = min(TILE, count)
    tiles = count // rows
    fetch = pltpu.make_async_copy(tok, tokv, moved.at[0])
    fetch.start()
    if linked:
        place = position()
        z, x, y, c = place
        greet(*place)
        row = jnp.zeros((1, width), F32)
        at = 0
        for v in vectors:
            size = v.shape[1]
            row = row + dot(v[...], (iota((size, width), 1) == iota((size, width), 0) + at).astype(BF16))
            at += size
        s_small[...] = jnp.concatenate([stamps_table[...].astype(F32), row, jnp.zeros((7, width), F32)], 0).astype(BF16)
        plans = [
            gather_plan(place, s, w, send.at[a], recv.at[a], local.at[a])
            for a, (s, w) in enumerate(
                [(s_small, small)]
                + [(s_in.at[:, width * i : width * i + width], w_in.at[i]) for i in range(3)]
                + [(s_out, wout_o)]
            )
        ]
        first, *middle, final = plans
        parts = [(s_down, 0, 64)] + [(s_up.at[:, width * j : width * j + width], 64 + 16 * j, 16) for j in range(4)]

        def feed_copy(j, k):
            src, at, size = parts[j]
            dst = feed_o.at[z, at : at + size, :]
            if k == 0:
                return pltpu.make_async_copy(src, dst, flocal.at[j])
            return remote(src, dst, fsend.at[j, k - 1], frecv.at[j, k - 1], device(peer(z, k), x, y, c))

        feeds = [feed_copy(j, k) for j in range(5) for k in range(4)]
        for plan in plans[:4]:
            plan[0]()
    roll, firsts, sizes = find_cuts(seg, count, cuts)
    if linked:
        for plan in plans[:4]:
            plan[1]()
        final[0]()
        for copy in feeds:
            copy.start()
        first[2]()
        first[3]()
    unpack_small(small[...].reshape((-1,) + small.shape[-2:]), vec_o, hid_o, table)
    fetch.wait()
    moves = []

    def move(src, dst):
        copy = pltpu.make_async_copy(src, dst, moved.at[len(moves) + 1])
        copy.start()
        moves.append(copy)

    for t in range(tiles):
        at = slice(rows * t, rows * t + rows)
        select = token_selector(stamps[:, at], flags[:, at], table.shape[0] - 16)
        put_columns(startf, at, tokv[at, :].astype(F32) + dot_tn(select, table[...]))
    wrap_columns(startf, rows)
    lane = iota((1, 128), 1)
    lows, highs = jnp.zeros((1, 128), jnp.int32), jnp.zeros((1, 128), jnp.int32)
    for i in range(SEGMENTS):
        lows = jnp.where(lane == i, firsts[i], lows)
        highs = jnp.where(lane == i, firsts[i] + sizes[i], highs)
    if linked:
        final[1]()
    for t in range(tiles):
        at = slice(rows * t, rows * t + rows)
        start = turned(startf, roll + rows * t, rows)
        startv[at, :] = start
        move(startv.at[at, :], start_o.at[at, :])
        xhat, _ = norm_parts(start)
        normed = (xhat * vec_o[1:2, :] + vec_o[2:3, :]).astype(BF16)
        normv[at, :] = normed
        normtv[:, at] = jnp.transpose(normed, (1, 0))
        row = iota((rows, 128), 0) + rows * t
        member = (row >= lows) & (row < highs)
        mqv[at, :] = jnp.where(member, 1.0, 0.0).astype(BF16)
        mkv[at, :] = jnp.where(member | (lane >= SEGMENTS), 0.0, NEG).astype(BF16)
        if linked and t == 2:
            middle[0][2]()
    move(normtv, normt_o)
    move(mqv, mq_o)
    move(mkv, mk_o)
    for i in range(3):
        cols = slice(width * i, width * i + width)
        if linked:
            middle[i][3]()
            weights = w_in[i].reshape(width, width)
            if i < 2:
                middle[i + 1][2]()
            else:
                final[2]()
        else:
            weights = w_in[:, cols]
        for t in range(tiles):
            at = slice(rows * t, rows * t + rows)
            value = dot(normv[at, :], weights)
            packv[at, cols] = (value * SCALE if i == 0 else value).astype(BF16)
        move(packv.at[:, cols], packed_o.at[:, cols])
    if linked:
        move(w_in, win_o)
    for copy in moves:
        copy.wait()
    if linked:
        final[3]()
        for plan in plans:
            plan[4]()
        for copy in feeds:
            copy.wait()


def unpack_small(flat16, vec_o, hid_o, table):
    devices, _, width = flat16.shape
    steps = devices * 8
    flat = flat16.astype(F32)
    row = flat[:, 8, :].astype(BF16)
    per = width // devices
    lane = iota((devices, width), 1)
    spread = jnp.concatenate([jnp.where(lane // per == i, row, jnp.zeros_like(row)) for i in range(7)], 0)
    same = (iota((width, width), 0) % per == iota((width, width), 1) % per).astype(BF16)
    wide = dot(spread, same).reshape(7, devices, width)
    mine = (lane // per == iota((devices, width), 0))[None]
    vecs = jnp.sum(jnp.where(mine, wide, 0.0), axis=1)
    vec_o[...] = jnp.concatenate([vecs, jnp.zeros((1, width), F32)], 0)
    hidden = hid_o.shape[1]
    part = hidden // devices
    at = iota((width, hidden), 0) - 7 * per
    pick = (at == iota((width, hidden), 1) % part).astype(BF16)
    own = iota((devices, hidden), 1) // part == iota((devices, hidden), 0)
    hid_o[...] = jnp.sum(jnp.where(own, dot(row, pick), 0.0), axis=0, keepdims=True)
    table[:steps, :] = flat[:, :8, :].reshape(steps, width).astype(BF16)
    table[steps:, :] = jnp.where(iota((16, width), 0) == 0, vecs[0:1], 0.0).astype(BF16)


def token_selector(stamps, flags, steps):
    rows = stamps.shape[1]
    chosen = (stamps == iota((steps, rows), 0)).astype(F32)
    flagged = jnp.where(iota((16, rows), 0) == 0, flags.astype(F32), 0.0)
    return jnp.concatenate([chosen, flagged], 0).astype(BF16)


def enter(tokens, segments, stamps, flags, hidden, shards, small, w_in):
    count, width = tokens.shape
    linked = shards is not None
    rows = min(TILE, count)
    anywhere = pl.BlockSpec(memory_space=pl.ANY)
    inside = pl.BlockSpec(memory_space=pltpu.VMEM)
    scalars = pl.BlockSpec(memory_space=pltpu.SMEM)
    lot = lambda *s: pltpu.SemaphoreType.DMA(s)
    big = lambda w, d: pltpu.VMEM((count, w), d)
    full = lambda a: (4, 2, 2, 2) + a
    outs = [
        jax.ShapeDtypeStruct((count, width), F32),
        jax.ShapeDtypeStruct((width, count), BF16),
        jax.ShapeDtypeStruct((count, 3 * width), BF16),
        jax.ShapeDtypeStruct((count, 128), BF16),
        jax.ShapeDtypeStruct((count, 128), BF16),
        jax.ShapeDtypeStruct((8, width), F32),
        jax.ShapeDtypeStruct((1, hidden), F32),
        jax.ShapeDtypeStruct((16,), jnp.int32),
    ]
    out_specs = [anywhere] * 5 + [inside] * 2 + [scalars]
    if linked:
        *vectors, stamps_table, s_in, s_out, s_up, s_down = shards
        operands = shards
        in_specs = [inside] * 9 + [anywhere] * 4
        outs += [
            jax.ShapeDtypeStruct((3,) + full(s_out.shape), BF16),
            jax.ShapeDtypeStruct(full(s_out.shape), BF16),
            jax.ShapeDtypeStruct((4, s_down.shape[0] + 64, width), BF16),
        ]
        out_specs += [anywhere] * 3
        scratch = [
            pltpu.VMEM((16, width), BF16), pltpu.VMEM(full((16, width)), BF16),
            pltpu.VMEM((3,) + full(s_out.shape), BF16),
            lot(5, GATHER_SLOTS), lot(5, GATHER_SLOTS), lot(5), lot(5, 3), lot(5, 3), lot(5),
        ]
        steps = 256
        compiler = params(collective_id=0, has_side_effects=True)
    else:
        operands, in_specs, scratch = [small, w_in], [inside] * 2, []
        steps = small.shape[0] * 8
        compiler = params()
    outs = pl.pallas_call(
        functools.partial(enter_kernel, linked),
        in_specs=[scalars, anywhere, inside, inside] + in_specs,
        out_specs=out_specs,
        out_shape=outs,
        scratch_shapes=scratch + [
            big(width, BF16), pltpu.VMEM((width // 128, count + rows, 128), F32), big(width, F32), big(width, BF16),
            pltpu.VMEM((width, count), BF16), big(3 * width, BF16), big(128, BF16), big(128, BF16),
            pltpu.VMEM((steps + 16, width), BF16), lot(16),
        ],
        compiler_params=compiler,
        name="enter",
    )(segments, tokens, stamps, flags, *operands)
    return list(outs)


def key_range(cuts, row, rows):
    lo, hi = jnp.int32(1 << 20), jnp.int32(0)
    for i in range(SEGMENTS):
        first, size = cuts[1 + i], cuts[1 + SEGMENTS + i]
        meets = (size > 0) & (first < row + rows) & (first + size > row)
        lo = jnp.where(meets, jnp.minimum(lo, first), lo)
        hi = jnp.where(meets, jnp.maximum(hi, first + size), hi)
    return lo, hi


def list_tiles(cuts, length, tile, qi, ki):
    blank = length // tile

    def one(t, n):
        lo, hi = key_range(cuts, t * tile, tile)

        def put(j, n):
            qi[n], ki[n] = t, j
            return n + 1

        return lax.fori_loop(lo // tile, (hi + tile - 1) // tile, put, n)

    n = lax.fori_loop(0, blank, one, jnp.int32(1))
    for i in range(2):
        qi[n + i], ki[n + i] = jnp.int32(blank), jnp.int32(blank)
    return n // 2


def spots(qi, ki, i, tile, length):
    q, k = pl.multiple_of(qi[i] * tile, tile), pl.multiple_of(ki[i] * tile, tile)
    q_in, k_in = (pl.multiple_of(jnp.where(v >= length, 0, v), tile) for v in (q, k))
    return pl.ds(q_in, tile), pl.ds(k_in, tile), pl.ds(q, tile), pl.ds(k, tile)


def head_masks():
    first = iota((1, 128), 1) < HD
    return [jnp.where(first == (h == 0), 1.0, 0.0).astype(BF16) for h in range(2)]


def fwd_kernel(length, tile, npair, cuts, q_ref, k_ref, v_ref, mq_ref, mk_ref, o_ref, lse_ref,
               vt, acc, top, alpha, ps, qi, ki):
    g = pl.program_id(0)
    heads = 2 * npair
    only = head_masks()
    ones = jnp.ones((16, tile), BF16)
    count = list_tiles(cuts, length, tile, qi, ki)
    vt[...] = jnp.transpose(v_ref[...], (1, 0))
    acc[...] = jnp.zeros_like(acc)
    top[...] = jnp.full_like(top, -3e38)

    def scan(i, slot, hs):
        q_in, k_in, q, _ = spots(qi, ki, i, tile, length)
        for h in hs:
            cols = slice(128 * (h // 2), 128 * (h // 2) + 128)
            s = dot_nt(jnp.concatenate([k_ref[k_in, cols], mk_ref[k_in, :]], 1),
                       jnp.concatenate([q_ref[q_in, cols] * only[h % 2], mq_ref[q_in, :]], 1))
            old = top[h : h + 1, q]
            new = jnp.maximum(old, jnp.max(s, axis=0, keepdims=True))
            top[h : h + 1, q] = new
            alpha[slot, h : h + 1] = jnp.exp(old - new)
            ps[slot, h] = jnp.exp(s - new).astype(BF16)

    def mix(i, slot, hs):
        _, k_in, q, _ = spots(qi, ki, i, tile, length)
        for h in hs:
            values = jnp.concatenate([vt[HD * h : HD * h + HD, k_in], ones], 0)
            acc[h, :, q] = acc[h, :, q] * alpha[slot, h : h + 1] + dot(values, ps[slot, h])

    def step(m, _):
        def both(a, sa, b, sb):
            for h in range(heads):
                mix(a, sa, [h])
                scan(b, sb, [h])

        both(2 * m + 1, 0, 2 * m + 2, 1)
        both(2 * m + 2, 1, 2 * m + 3, 0)
        return 0

    scan(1, 0, range(heads))
    lax.fori_loop(0, count, step, 0)
    for i in range(npair):
        both = []
        for h in (2 * i, 2 * i + 1):
            total = acc[h, HD : HD + 1, :length]
            both.append(acc[h, :HD, :length] / total)
            lse_ref[pl.ds(heads * g + h, 1), :] = top[h : h + 1, :length] + jnp.log(total)
        o_ref[:, 128 * i : 128 * i + 128] = jnp.transpose(jnp.concatenate(both, 0), (1, 0)).astype(BF16)


def attention_forward(packed, cuts, mq, mk, tile, npair):
    length = packed.shape[0]
    steps = 4 // npair
    w, heads = 128 * npair, 2 * npair
    most = (length // tile) ** 2 + 8
    col = lambda o: pl.BlockSpec((length, w), lambda g, s: (0, g + o * steps))
    whole = pl.BlockSpec((length, 128), lambda g, s: (0, 0))
    return pl.pallas_call(
        functools.partial(fwd_kernel, length, tile, npair),
        grid_spec=pltpu.PrefetchScalarGridSpec(
            num_scalar_prefetch=1, grid=(steps,),
            in_specs=[col(0), col(1), col(2), whole, whole],
            out_specs=[col(0), pl.BlockSpec((8, length), lambda g, s: (0, 0))],
            scratch_shapes=[
                pltpu.VMEM((w, length), BF16),
                pltpu.VMEM((heads, HD + 16, length + tile), F32),
                pltpu.VMEM((8, length + tile), F32),
                pltpu.VMEM((2, 8, tile), F32),
                pltpu.VMEM((2, heads, tile, tile), BF16),
                pltpu.SMEM((most,), jnp.int32),
                pltpu.SMEM((most,), jnp.int32),
            ]),
        out_shape=[jax.ShapeDtypeStruct((length, 512), BF16), jax.ShapeDtypeStruct((8, length), F32)],
        compiler_params=params(),
        name="attend_forward",
    )(cuts, packed, packed, packed, mq, mk)


def bwd_kernel(length, tile, npair, cuts, q_ref, k_ref, v_ref, do_ref, mq_ref, mk_ref, lse_ref, delta_ref,
               out_ref, dq_ref, dk_ref, dv_ref, out_again, kt, dk, dv, dqt, ps, dss, qi, ki):
    g = pl.program_id(0)
    heads = 2 * npair
    out_again[...] = out_ref[...]
    only = head_masks()
    count = list_tiles(cuts, length, tile, qi, ki)
    kt[...] = jnp.transpose(k_ref[...], (1, 0))
    for ref in (dk, dv, dqt):
        ref[...] = jnp.zeros_like(ref)

    def scan(i, slot):
        q_in, k_in, _, _ = spots(qi, ki, i, tile, length)
        for h in range(heads):
            at = slice(128 * (h // 2), 128 * (h // 2) + 128)
            lse = lse_ref[pl.ds(heads * g + h, 1), q_in]
            delta = delta_ref[pl.ds(heads * g + h, 1), q_in]
            s = dot_nt(jnp.concatenate([k_ref[k_in, at], mk_ref[k_in, :]], 1),
                       jnp.concatenate([q_ref[q_in, at] * only[h % 2], mq_ref[q_in, :]], 1))
            p = jnp.exp(s - lse)
            dp = dot_nt(v_ref[k_in, at], do_ref[q_in, at] * only[h % 2])
            cols = slice(tile * (h % 2), tile * (h % 2) + tile)
            ps[slot, h // 2, :, cols] = p.astype(BF16)
            dss[slot, h // 2, :, cols] = (p * (dp - delta)).astype(BF16)

    def mix(i, slot):
        q_in, k_in, q, k = spots(qi, ki, i, tile, length)
        for i in range(npair):
            at = slice(128 * i, 128 * i + 128)
            part = do_ref[q_in, at]
            dv[i, k, :] += dot(ps[slot, i], jnp.concatenate([part * only[0], part * only[1]], 0))
            part = q_ref[q_in, at]
            dk[i, k, :] += dot(dss[slot, i], jnp.concatenate([part * only[0], part * only[1]], 0))
            for h in (2 * i, 2 * i + 1):
                rows = slice(HD * h, HD * h + HD)
                cols = slice(tile * (h % 2), tile * (h % 2) + tile)
                dqt[rows, q] += dot(kt[rows, k_in], dss[slot, i, :, cols])

    def step(m, _):
        scan(2 * m + 2, 1)
        mix(2 * m + 1, 0)
        scan(2 * m + 3, 0)
        mix(2 * m + 2, 1)
        return 0

    scan(1, 0)
    lax.fori_loop(0, count, step, 0)
    for i in range(npair):
        cols = slice(128 * i, 128 * i + 128)
        dk_ref[:, cols] = dk[i, :length].astype(BF16)
        dv_ref[:, cols] = dv[i, :length].astype(BF16)
        dq_ref[:, cols] = jnp.transpose(dqt[cols, :length] * SCALE, (1, 0)).astype(BF16)


def attention_backward(packed, dmix, cuts, mq, mk, lse, delta, out, tile, npair):
    length = packed.shape[0]
    steps = 4 // npair
    w, heads = 128 * npair, 2 * npair
    most = (length // tile) ** 2 + 8
    col = lambda o: pl.BlockSpec((length, w), lambda g, s: (0, g + o * steps))
    whole = pl.BlockSpec((length, 128), lambda g, s: (0, 0))
    rowspec = pl.BlockSpec((8, length), lambda g, s: (0, 0))
    return pl.pallas_call(
        functools.partial(bwd_kernel, length, tile, npair),
        grid_spec=pltpu.PrefetchScalarGridSpec(
            num_scalar_prefetch=1, grid=(steps,),
            in_specs=[col(0), col(1), col(2), col(0), whole, whole, rowspec, rowspec, col(0)],
            out_specs=[col(0)] * 4,
            scratch_shapes=[
                pltpu.VMEM((w, length), BF16),
                pltpu.VMEM((npair, length + tile, 128), F32),
                pltpu.VMEM((npair, length + tile, 128), F32),
                pltpu.VMEM((w, length + tile), F32),
                pltpu.VMEM((2, npair, tile, 2 * tile), BF16),
                pltpu.VMEM((2, npair, tile, 2 * tile), BF16),
                pltpu.SMEM((most,), jnp.int32),
                pltpu.SMEM((most,), jnp.int32),
            ]),
        out_shape=[jax.ShapeDtypeStruct((length, 512), BF16)] * 3 + [jax.ShapeDtypeStruct(out.shape, out.dtype)],
        compiler_params=params(),
        name="attend_backward",
    )(cuts, packed, packed, packed, dmix, mq, mk, lse, delta, out)


def gelu_parts(v):
    phi = 0.5 * lax.erf(v * 0.7071067811865476) + 0.5
    return v * phi, phi + v * (jnp.exp(v * v * -0.5) * 0.3989422804014327)


def feed_kernel(linked, rows, f, cuts, start, mix, cot, w_out, vec, hid, *refs):
    if linked:
        lands = refs[:4]
        out_o, gmid_o, dmix_o, delta_o, gvec_o, ghid_o = refs[4:10]
        leaves = refs[10:14]
        refs = refs[14:]
    else:
        up_all, down_all = refs[:2]
        out_o, gmid_o, dmix_o, delta_o, gvec_o, ghid_o, gup_o, gdown_o, gout_o = refs[2:11]
        refs = refs[11:]
    (mid, res, gn2, n2, n2t, br, brt, mixv, projv, act0, act1, gpre0, gpre1, gup, gdt, gout, cotf, rsv,
     csem, tsem, osem) = refs[:21]
    count, width = mid.shape
    hidden = gup.shape[1]
    tiles, chunks = count // rows, hidden // f
    half = tiles // 2
    roll = cuts[0]
    spans = [slice(rows * t, rows * t + rows) for t in range(tiles)]
    loads = [pltpu.make_async_copy(w_out, projv, tsem.at[2 * tiles])]
    for t, at in enumerate(spans):
        pltpu.make_async_copy(mix.at[at], mixv.at[at], tsem.at[2 * t]).start()
        pltpu.make_async_copy(start.at[at], mid.at[at], tsem.at[2 * t + 1]).start()
    for i in range(width // 128):
        cols = pl.ds(128 * i, 128)
        loads.append(pltpu.make_async_copy(cot.at[:, cols], cotf.at[i, pl.ds(0, count), :], csem.at[i, 0]))
        loads.append(pltpu.make_async_copy(cot.at[pl.ds(0, rows), cols], cotf.at[i, pl.ds(count, rows), :], csem.at[i, 1]))
    for copy in loads:
        copy.start()

    def rows_at(t):
        return pl.ds(pl.multiple_of(t * rows, rows), rows)

    if linked:
        up, down, sent, kept, got, lsem, lsend, lrecv, esend, erecv, eout = refs[21:]
        place = position()
        z, x, y, c = place
        sibling = device(z, x, y, 1 - c)

        def arrive(i, j, kind):
            xs, ys = plane(x, y)[i]
            if j == 0:
                src, dst = lands[i].at[:, :64, :], down.at[:, xs, ys, c]
            else:
                src = lands[i].at[:, 48 + 16 * j : 64 + 16 * j, :]
                dst = up.at[:, xs, ys, c, :, width * (j - 1) : width * j]
            if kind == 0:
                return pltpu.make_async_copy(src, dst, lsem.at[i, j])
            return remote(src, dst, lsend.at[i, j], lrecv.at[i, j], sibling)

        arrivals = [arrive(i, j, kind) for i in range(4) for j in range(5) for kind in range(2)]

        def exchange(j):
            at = slice(0, 128) if j == 0 else slice(128, 144)
            return remote(sent.at[:, :, :, at, :], got.at[:, :, :, at, :], esend.at[j], erecv.at[j], sibling)

        def leave(i):
            xs, ys = plane(x, y)[i]
            return pltpu.make_async_copy(got.at[:, xs, ys], leaves[i], eout.at[i])

        barrier = pltpu.get_barrier_semaphore()
        pl.semaphore_signal(barrier, inc=1, device_id=sibling, device_id_type=MESH)
        pl.semaphore_wait(barrier, 1)
        for copy in arrivals:
            copy.start()

    def cols_at(ch):
        return pl.ds(pl.multiple_of(ch * f, f), f)

    def up_chunk(ch):
        if linked:
            return up[:, :, :, :, :, cols_at(ch)].reshape(width, f)
        return up_all[:, cols_at(ch)]

    def down_chunk(ch):
        if linked:
            return down[ch].reshape(f, width)
        return down_all[cols_at(ch), :]

    for ref in (act1, gpre1, gup, gdt, gn2, gout, ghid_o, gvec_o):
        ref[...] = jnp.zeros_like(ref)
    loads[0].wait()

    def load_tile(t, i):
        at = rows_at(t)
        if i == 0:
            return pltpu.make_async_copy(mix.at[at], mixv.at[at], tsem.at[2 * t])
        return pltpu.make_async_copy(start.at[at], mid.at[at], tsem.at[2 * t + 1])

    def middle_tile(t, _):
        at = rows_at(t)
        load_tile(t, 0).wait()
        load_tile(t, 1).wait()
        middle = mid[at, :] + dot(mixv[at, :], projv[...]) + vec[3:4, :]
        put_columns(res, at, middle + vec[6:7, :])
        xhat, rstd = norm_parts(middle)
        mid[at, :] = xhat
        rsv[at, :] = jnp.broadcast_to(rstd, (rows, 128))
        normed = (xhat * vec[4:5, :] + vec[5:6, :]).astype(BF16)
        n2[at, :] = normed
        n2t[:, at] = jnp.transpose(normed, (1, 0))
        return 0

    lax.fori_loop(0, tiles, middle_tile, 0)
    for copy in loads[1:]:
        copy.wait()

    def branch_tile(t, _):
        at = rows_at(t)
        branch = turned(cotf, roll + rows * t, rows).astype(BF16)
        br[at, :] = branch
        brt[:, at] = jnp.transpose(branch, (1, 0))
        gvec_o[3:4, :] += jnp.sum(branch.astype(F32), axis=0, keepdims=True)
        return 0

    lax.fori_loop(0, tiles, branch_tile, 0)
    if linked:
        for copy in arrivals:
            copy.wait()

    def inner(ch, t, act, gpre):
        cols, at = cols_at(ch), rows_at(t)
        pre = dot(n2[at, :], up_chunk(ch)) + hid[:, cols]
        grad = dot_nt(br[at, :], down_chunk(ch))
        value, slope = gelu_parts(pre)
        act[...] = value.astype(BF16)
        low = (grad * slope).astype(BF16)
        gpre[...] = low
        ghid_o[:, cols] += jnp.sum(low.astype(F32), axis=0, keepdims=True)

    def outer(ch, t, act, gpre):
        cols, at = cols_at(ch), rows_at(t)
        a, g = act[...], gpre[...]
        more = dot(a, down_chunk(ch))
        for i in range(width // 128):
            res[i, at, :] += more[:, 128 * i : 128 * i + 128]
        gn2[at, :] += dot_nt(g, up_chunk(ch))
        gup[:, cols] += dot(n2t[:, at], g)
        gdt[:, cols] += dot(brt[:, at], a)

    def step(b, _):
        before = jnp.maximum(b - 1, 0)
        ch, t = b // half, 2 * (b % half)
        outer(before // half, 2 * (before % half) + 1, act1, gpre1)
        inner(ch, t, act0, gpre0)
        outer(ch, t, act0, gpre0)
        inner(ch, t + 1, act1, gpre1)
        return 0

    lax.fori_loop(0, chunks * half, step, 0)
    outer(chunks - 1, tiles - 1, act1, gpre1)
    wrap_columns(res, rows)
    if linked:
        for i in range(4):
            block = jnp.transpose(gdt[:, 512 * i : 512 * i + 512], (1, 0)).reshape(2, 2, 2, 64, width)
            first, second = block[:, :, 0], block[:, :, 1]
            kept[i, :, :, :64, :] = jnp.where(c == 0, first, second).astype(BF16)
            sent[i, :, :, :64, :] = jnp.where(c == 0, second, first).astype(BF16)
            cols = slice(width * i, width * i + width)
            block = gup[:, cols].reshape(4, 2, 2, 2, 16, width)
            first, second = block[:, :, :, 0], block[:, :, :, 1]
            at = slice(64 + 16 * i, 80 + 16 * i)
            kept[:, :, :, at, :] = jnp.where(c == 0, first, second).astype(BF16)
            sent[:, :, :, at, :] = jnp.where(c == 0, second, first).astype(BF16)
        exchange(0).start()
    else:
        for i in range(chunks):
            gup_o[:, i * f : (i + 1) * f] = gup[:, i * f : (i + 1) * f].astype(BF16)
            gdown_o[i * f : (i + 1) * f, :] = jnp.transpose(gdt[:, i * f : (i + 1) * f], (1, 0)).astype(BF16)
    heads = (iota((16, width), 1) // HD == iota((16, width), 0)).astype(BF16)

    def move(t, i):
        at = rows_at(t)
        src, dst = ((n2, out_o), (gn2, gmid_o), (br, dmix_o))[i]
        return pltpu.make_async_copy(src.at[at], dst.at[at], osem.at[3 * t + i])

    def last_tile(t, _):
        at = rows_at(t)
        n2[at, :] = turned(res, rows * t - roll, rows).astype(BF16)
        move(t, 0).start()
        xhat, rstd = mid[at, :], jnp.concatenate([rsv[at, :]] * (width // 128), 1)
        n = gn2[at, :]
        grad = turned(cotf, roll + rows * t, rows) + norm_back(n, xhat, rstd, vec[4:5, :])
        gn2[at, :] = grad
        move(t, 1).start()
        low = grad.astype(BF16)
        for i, term in enumerate((low.astype(F32), n * xhat, n)):
            gvec_o[i : i + 1, :] += jnp.sum(term, axis=0, keepdims=True)
        mixed = mixv[at, :]
        gout[...] += dot_tn(mixed, low)
        dmix = dot_nt(low, projv[...]).astype(BF16)
        br[at, :] = dmix
        move(t, 2).start()
        prod = dmix.astype(F32) * mixed.astype(F32)
        high = prod.astype(BF16)
        rest = (prod - high.astype(F32)).astype(BF16)
        delta_o[:, at] = (dot_nt(heads, high) + dot_nt(heads, rest))[:8]
        return 0

    lax.fori_loop(0, tiles, last_tile, 0)
    if linked:
        block = gout[...].reshape(4, 2, 2, 2, 16, width)
        first, second = block[:, :, :, 0], block[:, :, :, 1]
        kept[:, :, :, 128:, :] = jnp.where(c == 0, first, second).astype(BF16)
        sent[:, :, :, 128:, :] = jnp.where(c == 0, second, first).astype(BF16)
        exchange(1).start()
        exchange(0).wait()
        exchange(1).wait()
        for i in range(4):
            got[i] = (got[i].astype(F32) + kept[i].astype(F32)).astype(BF16)
        for i in range(4):
            leave(i).start()
        for i in range(4):
            leave(i).wait()
    else:
        gout_o[...] = gout[...].astype(BF16)
    for t in range(tiles):
        for i in range(3):
            move(t, i).wait()


def feed(cuts, start, mixture, cotangent, w_out, vec, hid, weights, linked):
    count, width = start.shape
    hidden = hid.shape[1]
    rows = min(TILE, count)
    f = min(512, hidden)
    tiles = count // rows
    anywhere = pl.BlockSpec(memory_space=pl.ANY)
    inside = pl.BlockSpec(memory_space=pltpu.VMEM)
    big = lambda d: pltpu.VMEM((count, width), d)
    flat = lambda: pltpu.VMEM((width, count), BF16)
    turning = pltpu.VMEM((width // 128, count + rows, 128), F32)
    lot = lambda *s: pltpu.SemaphoreType.DMA(s)
    scratch = (
        [big(F32), turning, big(F32), big(BF16), flat(), big(BF16), flat(), big(BF16), pltpu.VMEM((width, width), BF16)]
        + [pltpu.VMEM((rows, f), BF16)] * 4
        + [pltpu.VMEM((width, hidden), F32)] * 2
        + [pltpu.VMEM((width, width), F32), turning, pltpu.VMEM((count, 128), F32)]
        + [lot(width // 128, 2), lot(2 * tiles + 1), lot(3 * tiles)]
    )
    common = [
        jax.ShapeDtypeStruct((count, width), BF16),
        jax.ShapeDtypeStruct((count, width), F32),
        jax.ShapeDtypeStruct((count, width), BF16),
        jax.ShapeDtypeStruct((8, count), F32),
        jax.ShapeDtypeStruct((8, width), F32),
        jax.ShapeDtypeStruct((1, hidden), F32),
    ]
    if linked:
        weight_specs = [anywhere] * 4
        more = [jax.ShapeDtypeStruct((4, 144, width), BF16)] * 4
        more_specs = [anywhere] * 4
        scratch += [
            pltpu.VMEM((4, 2, 2, 2, 16, hidden), BF16), pltpu.VMEM((4, 2, 2, 2, 64, width), BF16),
        ] + [pltpu.VMEM((4, 2, 2, 144, width), BF16)] * 3 + [lot(4, 5), lot(4, 5), lot(4, 5), lot(2), lot(2), lot(4)]
        compiler = params(60 << 20, collective_id=1, has_side_effects=True)
    else:
        weight_specs = [inside] * 2
        more = [jax.ShapeDtypeStruct(s, BF16) for s in ((width, hidden), (hidden, width), (width, width))]
        more_specs = [inside] * 3
        compiler = params()
    return pl.pallas_call(
        functools.partial(feed_kernel, linked, rows, f),
        in_specs=[pl.BlockSpec(memory_space=pltpu.SMEM)] + [anywhere] * 4 + [inside] * 2 + weight_specs,
        out_specs=[anywhere] * 3 + [inside] * 3 + more_specs,
        out_shape=common + more,
        scratch_shapes=scratch,
        compiler_params=compiler,
        name="feed_forward",
    )(cuts, start, mixture, cotangent, w_out, vec, hid, *weights)


def leave_kernel(linked, cuts, dq, dk, dv, normt, w_in, start, gmid, stamps, flags, vec, gvec2, ghid, *refs):
    if linked:
        pieces = refs[:4]
        gtok_o, gin_o, gsmall_o, gfeed_o, gtab, gvec, land, esum, egot, esend, erecv, lsem = refs[4:16]
        places = [refs[16 + 7 * i : 23 + 7 * i] for i in range(4)]
        refs = refs[44:]
    else:
        gtok_o, gin_o, gtab, gvec = refs[:4]
        refs = refs[4:]
    grads, normv, startv, gmidv, weights, gtokf, gtokv, sem = refs
    count, width = start.shape
    rows = min(TILE, count)
    tiles = count // rows
    steps = gtab.shape[0] - 16
    spans = [slice(rows * t, rows * t + rows) for t in range(tiles)]
    fetches = {}

    def fetch(name, src, dst):
        fetches[name] = pltpu.make_async_copy(src, dst, sem.at[len(fetches)])
        fetches[name].start()

    fetch("normed", normt, normv)
    fetch(0, dq, grads.at[0])
    fetch(1, dk, grads.at[1])
    gtab[...] = jnp.zeros_like(gtab)
    if linked:
        place = position()
        z, x, y, c = place
        plans = [scatter_plan(place, *p) for p in places]

        def level(k):
            return remote(esum.at[peer(z, k)], egot.at[k - 1], esend.at[k - 1], erecv.at[k - 1],
                          device(peer(z, k), x, y, c))

        greet(*place)
        lands = [pltpu.make_async_copy(p, land.at[i], lsem.at[i]) for i, p in enumerate(pieces)]
    fetches["normed"].wait()
    for i in range(3):
        fetches[i].wait()
        total = dot(normv[...], grads[i]).astype(BF16)
        if linked:
            full = places[i][0]
            full[...] = total.reshape(full.shape)
            plans[i][0]()
            if i:
                plans[i - 1][1]()
        else:
            gin_o[:, width * i : width * i + width] = total
        if i == 0:
            fetch(2, dv, grads.at[2])
            if linked:
                for copy in lands:
                    copy.start()
            fetch("weights", w_in, weights)
        elif i == 1:
            for t, at in enumerate(spans):
                fetch(("start", t), start.at[at], startv.at[at])
                fetch(("gmid", t), gmid.at[at], gmidv.at[at])
    if linked:
        for copy in lands:
            copy.wait()
        for i in range(4):
            parts = [land[j, i].astype(F32) for j in range(4)]
            esum[i] = (parts[0] + parts[1] + parts[2] + parts[3]).astype(BF16)
        for k in (1, 2, 3):
            level(k).start()
    fetches["weights"].wait()
    gains, biases = jnp.zeros((1, width), F32), jnp.zeros((1, width), F32)
    for t, at in enumerate(spans):
        n = sum(dot_nt(grads[i, at, :], weights[i]) for i in range(3))
        fetches["start", t].wait()
        fetches["gmid", t].wait()
        xhat, rstd = norm_parts(startv[at, :])
        put_columns(gtokf, at, gmidv[at, :] + norm_back(n, xhat, rstd, vec[1:2, :]))
        gains = gains + jnp.sum(n * xhat, axis=0, keepdims=True)
        biases = biases + jnp.sum(n, axis=0, keepdims=True)
        if linked and t == 0:
            plans[2][1]()
    gvec[...] = jnp.concatenate([gains, biases, jnp.zeros((6, width), F32)], 0)
    wrap_columns(gtokf, rows)
    moves = []
    for t, at in enumerate(spans):
        grad = turned(gtokf, rows * t - cuts[0], rows)
        gtokv[at, :] = grad
        moves.append(pltpu.make_async_copy(gtokv.at[at], gtok_o.at[at], sem.at[len(fetches) + t]))
        moves[t].start()
        gtab[...] += dot(token_selector(stamps[:, at], flags[:, at], steps), grad.astype(BF16))
    if linked:
        pack_small(places[3][0], steps, gtab, gvec, gvec2, ghid)
        plans[3][0]()
        plans[0][2]()
        plans[3][1]()
        plans[1][2]()
        plans[2][2]()
        for k in (1, 2, 3):
            level(k).wait_recv()
        gfeed_o[...] = (esum[z].astype(F32) + egot[0].astype(F32)) + (egot[1].astype(F32) + egot[2].astype(F32))
        plans[3][2]()
        for i in range(3):
            plans[i][3](gin_o, width * i)
        plans[3][3](gsmall_o, 0)
        for plan in plans:
            plan[4]()
        for k in (1, 2, 3):
            level(k).wait_send()
    for move in moves:
        move.wait()


def pack_small(full, steps, gtab, gvec, gvec2, ghid):
    width = gtab.shape[1]
    groups = steps // 8
    per = width // groups
    sums = [gtab[steps : steps + 1, :], gvec[0:1, :], gvec[1:2, :]]
    sums += [gvec2[i : i + 1, :] for i in range(4)]
    mine = iota((groups, width), 1) // per == iota((groups, width), 0)
    spread = jnp.concatenate([jnp.where(mine, v, 0.0) for v in sums], 0).astype(BF16)
    same = (iota((width, width), 0) % per == iota((width, width), 1) % per).astype(BF16)
    wide = dot(spread, same).reshape(7, groups, width)
    lane = iota((1, width), 1)
    row = jnp.zeros((groups, width), F32)
    for i in range(7):
        row = jnp.where(lane // per == i, wide[i], row)
    hidden = ghid.shape[1]
    part = hidden // groups
    own = iota((groups, hidden), 1) // part == iota((groups, hidden), 0)
    pick = (iota((hidden, width), 0) % part == iota((hidden, width), 1) - 7 * per).astype(BF16)
    row = row + dot(jnp.where(own, ghid[...], 0.0).astype(BF16), pick)
    table = gtab[:steps, :].reshape(groups, 8, width)
    below = jnp.where(iota((groups, 8, width), 1) == 0, row[:, None, :], 0.0)
    full[...] = jnp.concatenate([table, below], 1).astype(BF16).reshape(full.shape)


def leave(cuts, dq, dk, dv, normt, w_in, start, gmid, stamps, flags, vec, gvec2, ghid, steps, pieces, linked):
    count, width = start.shape
    rows = min(TILE, count)
    tiles = count // rows
    lot = lambda *s: pltpu.SemaphoreType.DMA(s)
    anywhere = pl.BlockSpec(memory_space=pl.ANY)
    inside = pl.BlockSpec(memory_space=pltpu.VMEM)
    sums = [jax.ShapeDtypeStruct((steps + 16, width), F32), jax.ShapeDtypeStruct((8, width), F32)]
    if linked:
        more = [jax.ShapeDtypeStruct(s, F32) for s in ((16, 3 * width), (16, width), (144, width))]
        scratch = [pltpu.VMEM(a.shape, F32) for a in sums]
        scratch += [pltpu.VMEM(n + (144, width), BF16) for n in ((4, 4), (4,), (3,))] + [lot(3), lot(3), lot(4)]
        for _ in range(4):
            scratch += scatter_buffers(16, width) + [lot(SCATTER_SLOTS), lot(SCATTER_SLOTS)]
        compiler = params(collective_id=2, has_side_effects=True)
    else:
        more = [jax.ShapeDtypeStruct((width, 3 * width), BF16)] + sums
        scratch = []
        compiler = params()
    big = lambda d: pltpu.VMEM((count, width), d)
    return pl.pallas_call(
        functools.partial(leave_kernel, linked),
        in_specs=[pl.BlockSpec(memory_space=pltpu.SMEM)] + [anywhere] * 7 + [inside] * 5 + [anywhere] * len(pieces),
        out_specs=[anywhere] + [inside] * len(more),
        out_shape=[jax.ShapeDtypeStruct((count, width), F32)] + more,
        scratch_shapes=scratch + [
            pltpu.VMEM((3, count, width), BF16), pltpu.VMEM((width, count), BF16), big(F32), big(F32),
            pltpu.VMEM((3, width, width), BF16), pltpu.VMEM((width // 128, count + rows, 128), F32), big(F32),
            lot(5 + 3 * tiles),
        ],
        compiler_params=compiler,
        name="leave",
    )(cuts, dq, dk, dv, normt, w_in, start, gmid, stamps, flags, vec, gvec2, ghid, *pieces)


def unpack_kernel(sizes, gtok, gin, gsmall, gfeed, gtok_o, gin_o, gtab_o, gout_o, gup_o, gdown_o, *vecs):
    gtok_o[...] = gtok[...]
    pl.when(pl.program_id(0) == 0)(
        functools.partial(unpack_rest, sizes, gin, gsmall, gfeed, gin_o, gtab_o, gout_o, gup_o, gdown_o, *vecs)
    )


def unpack_rest(sizes, gin, gsmall, gfeed, gin_o, gtab_o, gout_o, gup_o, gdown_o, *vecs):
    width = gsmall.shape[1]
    gin_o[...] = gin[...]
    gtab_o[...] = gsmall[:8, :]
    gdown_o[...] = gfeed[:64, :]
    for i in range(gup_o.shape[1] // width):
        gup_o[:, width * i : width * (i + 1)] = gfeed[64 + 16 * i : 80 + 16 * i, :]
    gout_o[...] = gfeed[128:144, :]
    at = 0
    for ref, size in zip(vecs, sizes):
        ref[...] = gsmall[8:9, at : at + size]
        at += size


def unpack(gtok, gin, gsmall, gfeed, hidden, sizes):
    width = gsmall.shape[1]
    shapes = [gtok.shape, gin.shape, (8, width), (16, width), (16, hidden), (64, width)] + [(1, n) for n in sizes]
    whole = lambda s: pl.BlockSpec(tuple(s), lambda i: (0,) * len(s))
    rows = min(TILE, gtok.shape[0])
    tile = pl.BlockSpec((rows, width), lambda i: (i, 0))
    return pl.pallas_call(
        functools.partial(unpack_kernel, sizes),
        grid=(gtok.shape[0] // rows,),
        in_specs=[tile] + [whole(a.shape) for a in (gin, gsmall, gfeed)],
        out_specs=[tile] + [whole(s) for s in shapes[1:]],
        out_shape=[jax.ShapeDtypeStruct(s, F32) for s in shapes],
        compiler_params=params(),
        name="unpack",
    )(gtok, gin, gsmall, gfeed)


def exchange_plane(arrays):
    out = [arrays[0]]
    for array, (dx, dy) in zip(arrays[1:], ((1, 0), (0, 1), (1, 1))):
        pairs = [(4 * dp + fs, 4 * (dp ^ dx) + (fs ^ (2 * dy))) for dp in range(8) for fs in range(4)]
        out.append(lax.ppermute(array, AXES, pairs))
    return out


def per_device(fast, tokens, mask_flags, timesteps, segment_ids, mask_embed, time_table, first_gain, first_bias,
               input_proj, output_proj, output_bias, second_gain, second_bias, hidden_weight, hidden_bias,
               down_weight, down_bias, cotangent):
    count, width = tokens.shape
    hidden = hidden_weight.shape[1]
    vectors = (mask_embed, first_gain, first_bias, output_bias, second_gain, second_bias, down_bias)
    segments = segment_ids.reshape(-1)
    stamps, flags = timesteps[None], mask_flags[None]
    if fast:
        lines = [v[None] for v in vectors + (hidden_bias,)]
        sizes = [v.shape[1] for v in lines]
        shards = lines + [time_table, input_proj, output_proj, hidden_weight, down_weight]
        *kept, w_in, w_out, own = enter(tokens, segments, stamps, flags, hidden, shards, None, None)
        w_in, w_out = w_in.reshape(3, width, width), w_out.reshape(width, width)
        steps = time_table.shape[0] * 32
        weights = exchange_plane([own] * 4)
    else:
        whole = lambda a: lax.all_gather(a, AXES, axis=0, tiled=True)
        groups = whole(time_table).reshape(-1, 8, width)
        pieces = jnp.concatenate(
            [whole(v).reshape(groups.shape[0], -1) for v in vectors + (hidden_bias,)], 1
        )
        pieces = jnp.pad(pieces, ((0, 0), (0, width - pieces.shape[1])))[:, None]
        small = jnp.concatenate([groups, pieces, jnp.zeros((groups.shape[0], 7, width), BF16)], 1)
        w_in, w_out = whole(input_proj), whole(output_proj)
        weights = [whole(hidden_weight), whole(down_weight)]
        steps = groups.shape[0] * 8
        kept = enter(tokens, segments, stamps, flags, hidden, None, small, w_in)
        w_in = w_in.reshape(width, 3, width).transpose(1, 0, 2)
    start, normt, packed, mq, mk, vec, hid, cuts = kept

    mixture, lse = attention_forward(packed, cuts, mq, mk, 256, 4)
    out, gmid, dmix, delta, gvec2, ghid, *grads = feed(cuts, start, mixture, cotangent, w_out, vec, hid, weights, fast)
    pieces = exchange_plane(grads) if fast else []
    dq, dk, dv, out = attention_backward(packed, dmix, cuts, mq, mk, lse, delta, out, 256, 2)
    gtok, gin, *rest = leave(
        cuts, dq, dk, dv, normt, w_in, start, gmid, stamps, flags, vec, gvec2, ghid, steps, pieces, fast
    )
    if fast:
        gtok, gin, gtab, gout, gup, gdown, *small = unpack(gtok, gin, rest[0], rest[1], hidden, sizes)
        gmask, gg1, gb1, gob, gg2, gb2, gdb, ghb = [v.reshape(-1) for v in small]
    else:
        total = lambda a: lax.psum_scatter(a.astype(F32), AXES, scatter_dimension=0, tiled=True)
        gtab, gvec1 = rest
        gup, gdown, gout = grads
        gin, gout, gup, gdown = (total(a) for a in (gin, gout, gup, gdown))
        gmask = total(gtab[steps])
        gtab = total(gtab[:steps])
        gg1, gb1, gob, gg2, gb2, gdb, ghb = (
            total(a) for a in (gvec1[0], gvec1[1], gvec2[0], gvec2[1], gvec2[2], gvec2[3], ghid[0])
        )
    return (out, gtok, gmask, gtab, gg1, gb1, gin, gout, gob, gg2, gb2, gup, ghb, gdown, gdb)


def solution(mesh):
    split = P(AXES)
    rows = P(AXES, None)
    fast = tuple(mesh.shape[a] for a in AXES) == (8, 4)
    placed = (rows, split, split, rows, split, rows, split, split, rows, rows, split, split, split, rows, split, rows,
              split, rows)
    return jax.shard_map(
        functools.partial(per_device, fast),
        mesh=mesh,
        in_specs=placed,
        out_specs=(rows, rows, split, rows, split, split, rows, rows, split, split, split, rows, split, rows, split),
        check_vma=False,
    )
```

```python
import functools

import jax
import jax.numpy as jnp
from jax import lax
from jax.experimental import pallas as pl
from jax.experimental.pallas import tpu as pltpu
from jax.sharding import PartitionSpec as P

F32, BF16 = jnp.float32, jnp.bfloat16
HD = 64
SEGMENTS = 4
SCALE = HD ** -0.5
NEG = -1e30
EPSILON = 1e-05
AXES = ("dp", "fsdp")
MESH = pl.DeviceIdType.MESH
VMEM_BYTES = 58 << 20
TILE = 512


def dot(a, b):
    return jnp.dot(a, b, preferred_element_type=F32)


def dot_nt(a, b):
    return lax.dot_general(a, b, (((1,), (1,)), ((), ())), preferred_element_type=F32)


def dot_tn(a, b):
    return lax.dot_general(a, b, (((0,), (0,)), ((), ())), preferred_element_type=F32)


def iota(shape, dim):
    return lax.broadcasted_iota(jnp.int32, shape, dim)


def params(room=VMEM_BYTES, **more):
    return pltpu.CompilerParams(vmem_limit_bytes=room, **more)


def norm_parts(h):
    centered = h - jnp.mean(h, axis=-1, keepdims=True)
    rstd = lax.rsqrt(jnp.mean(centered * centered, axis=-1, keepdims=True) + EPSILON)
    return centered * rstd, rstd


def norm_back(n, xhat, rstd, gain):
    ng = n * gain
    first = jnp.mean(ng, axis=-1, keepdims=True)
    second = jnp.mean(ng * xhat, axis=-1, keepdims=True)
    return rstd * (ng - first - xhat * second)


def position():
    dp, fs = lax.axis_index("dp"), lax.axis_index("fsdp")
    return dp // 2, dp % 2, fs // 2, fs % 2


def device(z, x, y, c):
    return (z * 2 + x, y * 2 + c)


def peer(z, k):
    return lax.rem(z + k, 4)


def greet(z, x, y, c):
    barrier = pltpu.get_barrier_semaphore()
    partners = [device(peer(z, k), x, y, c) for k in (1, 2, 3)]
    partners += [device(z, xs, ys, c) for xs, ys in plane(x, y)[1:]] + [device(z, x, y, 1 - c)]
    for partner in partners:
        pl.semaphore_signal(barrier, inc=1, device_id=partner, device_id_type=MESH)
    pl.semaphore_wait(barrier, len(partners))


def remote(src, dst, send, recv, target):
    return pltpu.make_async_remote_copy(
        src_ref=src, dst_ref=dst, send_sem=send, recv_sem=recv, device_id=target, device_id_type=MESH
    )


def plane(x, y):
    return ((x, y), (1 - x, y), (x, 1 - y), (1 - x, 1 - y))


def gather_plan(place, shard, whole, send, recv, local):
    z, x, y, c = place
    spots = plane(x, y)
    level = lambda k: peer(z, 4 - k)

    def copy(slot):
        if slot < 4 and slot:
            src, dst, to = shard, whole.at[z, x, y, c], device(peer(z, slot), x, y, c)
        elif 4 <= slot < 16:
            k = slot % 4
            dst, to = whole.at[level(k), x, y, c], device(z, *spots[slot // 4], c)
            src = dst if k else shard
        else:
            xs, ys = spots[max(slot - 15, 0)]
            src = dst = whole.at[:, xs, ys, c]
            to = device(z, x, y, 1 - c)
        return remote(src, dst, send.at[slot], recv.at[slot], to)

    keep = pltpu.make_async_copy(shard, whole.at[z, x, y, c], local)

    def begin():
        keep.start()
        for k in (1, 2, 3):
            copy(k).start()

    def spread():
        for k in range(4):
            if k:
                copy(k).wait_recv()
            for kind in (4, 8, 12):
                copy(kind + k).start()
        keep.wait()
        copy(0).start()

    def finish():
        for i in range(3):
            for k in range(4):
                copy(4 + 4 * i + k).wait_recv()
            copy(16 + i).start()

    def ready():
        for slot in (0, 16, 17, 18):
            copy(slot).wait_recv()

    def drain():
        for slot in range(GATHER_SLOTS):
            copy(slot).wait_send()

    return begin, spread, finish, ready, drain


GATHER_SLOTS = 19


def scatter_plan(place, full, own, got, land, last, send, recv):
    z, x, y, c = place
    spots = plane(x, y)

    def copy(slot):
        if slot == 0:
            src, dst, to = full.at[:, :, :, 1 - c], got, device(z, x, y, 1 - c)
        elif slot < 4:
            xs, ys = spots[slot]
            src, dst, to = own.at[:, xs, ys], land.at[slot - 1], device(z, xs, ys, c)
        else:
            k = slot - 3
            src, dst, to = got.at[peer(z, k), 0, 0], last.at[k - 1], device(peer(z, k), x, y, c)
        return remote(src, dst, send.at[slot], recv.at[slot], to)

    def to_sibling():
        copy(0).start()

    def to_plane():
        copy(0).wait_recv()
        for i in range(4):
            own[i] = (full[i, :, :, c].astype(F32) + got[i].astype(F32)).astype(BF16)
        for slot in (1, 2, 3):
            copy(slot).start()

    def to_levels():
        for slot in (1, 2, 3):
            copy(slot).wait_recv()
        for i in range(4):
            parts = [own[i, x, y]] + [land[j, i] for j in range(3)]
            parts = [p.astype(F32) for p in parts]
            got[i, 0, 0] = (parts[0] + parts[1] + parts[2] + parts[3]).astype(BF16)
        for slot in (4, 5, 6):
            copy(slot).start()

    def total(out, at):
        for slot in (4, 5, 6):
            copy(slot).wait_recv()
        rest = last[0].astype(F32) + last[1].astype(F32) + last[2].astype(F32)
        out[:, at : at + rest.shape[1]] = got[z, 0, 0].astype(F32) + rest

    def drain():
        for slot in range(SCATTER_SLOTS):
            copy(slot).wait_send()

    return to_sibling, to_plane, to_levels, total, drain


SCATTER_SLOTS = 7


def scatter_buffers(rows, width):
    return [pltpu.VMEM(s, BF16) for s in (
        (4, 2, 2, 2, rows, width), (4, 2, 2, rows, width), (4, 2, 2, rows, width), (3, 4, rows, width),
        (3, rows, width))]


def find_cuts(seg, length, cuts):
    def first_at_least(s):
        def step(_, span):
            lo, hi = span
            mid = (lo + hi) // 2
            below = seg[jnp.minimum(mid, length - 1)] < s
            live = lo < hi
            return jnp.where(live & below, mid + 1, lo), jnp.where(live & jnp.logical_not(below), mid, hi)

        return lax.fori_loop(0, length.bit_length(), step, (jnp.int32(0), jnp.int32(length)))[0]

    edges = [jnp.int32(0)] + [first_at_least(s) for s in range(1, SEGMENTS)] + [jnp.int32(length)]
    sizes = [edges[i + 1] - edges[i] for i in range(SEGMENTS)]
    roll, most = edges[0], sizes[0]
    for edge, size in zip(edges[1:], sizes[1:]):
        roll = jnp.where(size > most, edge, roll)
        most = jnp.maximum(size, most)
    cuts[0] = roll
    firsts = []
    for i in range(SEGMENTS):
        at = edges[i] - roll
        firsts.append(jnp.where(at < 0, at + length, at))
        cuts[1 + i] = firsts[i]
        cuts[1 + SEGMENTS + i] = sizes[i]
    return roll, firsts, sizes


def turned(ref, first, rows):
    length = ref.shape[1] - rows
    at = jnp.where(first >= length, first - length, first)
    at = jnp.where(at < 0, at + length, at)
    return jnp.concatenate([ref[i, pl.ds(at, rows), :] for i in range(ref.shape[0])], 1)


def put_columns(ref, at, value):
    for i in range(ref.shape[0]):
        ref[i, at, :] = value[:, 128 * i : 128 * i + 128]


def wrap_columns(ref, rows):
    length = ref.shape[1] - rows
    for i in range(ref.shape[0]):
        ref[i, length:, :] = ref[i, :rows, :]


def enter_kernel(linked, seg, tok, stamps, flags, *refs):
    if linked:
        vectors, stamps_table, s_in, s_out, s_up, s_down = refs[:8], *refs[8:13]
        refs = refs[13:]
        (start_o, normt_o, packed_o, mq_o, mk_o, vec_o, hid_o, cuts, win_o, wout_o, feed_o,
         s_small, small, w_in, send, recv, local, fsend, frecv, flocal) = refs[:20]
        refs = refs[20:]
    else:
        small, w_in, start_o, normt_o, packed_o, mq_o, mk_o, vec_o, hid_o, cuts = refs[:10]
        refs = refs[10:]
    tokv, startf, startv, normv, normtv, packv, mqv, mkv, table, moved, tsem = refs
    count, width = tok.shape
    rows = min(TILE, count)
    tiles = count // rows
    fetch = pltpu.make_async_copy(tok, tokv, moved.at[0])
    fetch.start()
    if linked:
        place = position()
        z, x, y, c = place
        greet(*place)
        row = jnp.zeros((1, width), F32)
        at = 0
        for v in vectors:
            size = v.shape[1]
            row = row + dot(v[...], (iota((size, width), 1) == iota((size, width), 0) + at).astype(BF16))
            at += size
        s_small[...] = pack_block(stamps_table[...].astype(F32), row[:, : 2 * SIDE]).astype(BF16)
        plans = [
            gather_plan(place, s, w, send.at[a], recv.at[a], local.at[a])
            for a, (s, w) in enumerate(
                [(s_small, small)]
                + [(s_in.at[:, width * i : width * i + width], w_in.at[i]) for i in range(3)]
                + [(s_out, wout_o)]
            )
        ]
        first, *middle, final = plans
        parts = [(s_down, 0, 64)] + [(s_up.at[:, width * j : width * j + width], 64 + 16 * j, 16) for j in range(4)]

        def feed_copy(j, k):
            src, at, size = parts[j]
            dst = feed_o.at[z, at : at + size, :]
            if k == 0:
                return pltpu.make_async_copy(src, dst, flocal.at[j])
            return remote(src, dst, fsend.at[j, k - 1], frecv.at[j, k - 1], device(peer(z, k), x, y, c))

        feeds = [feed_copy(j, k) for j in range(5) for k in range(4)]
        for plan in plans[:4]:
            plan[0]()
    roll, firsts, sizes = find_cuts(seg, count, cuts)
    if linked:
        for plan in plans[:4]:
            plan[1]()
        final[0]()
        for copy in feeds:
            copy.start()
        first[2]()
        first[3]()
    unpack_small(small[...].reshape((-1,) + small.shape[-2:]), vec_o, hid_o, table)
    fetch.wait()
    moves = []

    def move(src, dst):
        copy = pltpu.make_async_copy(src, dst, moved.at[len(moves) + 1])
        copy.start()
        moves.append(copy)

    def rows_at(t):
        return pl.ds(t * rows if isinstance(t, int) else pl.multiple_of(t * rows, rows), rows)

    def start_tile(t, _):
        at = rows_at(t)
        select = token_selector(stamps[:, at], flags[:, at], table.shape[0] - 16)
        put_columns(startf, at, tokv[at, :].astype(F32) + dot_tn(select, table[...]))
        return 0

    lax.fori_loop(0, tiles, start_tile, 0)
    wrap_columns(startf, rows)
    lane = iota((1, 128), 1)
    lows, highs = jnp.zeros((1, 128), jnp.int32), jnp.zeros((1, 128), jnp.int32)
    for i in range(SEGMENTS):
        lows = jnp.where(lane == i, firsts[i], lows)
        highs = jnp.where(lane == i, firsts[i] + sizes[i], highs)
    if linked:
        final[1]()
    def save(t):
        return pltpu.make_async_copy(startv.at[rows_at(t)], start_o.at[rows_at(t)], tsem.at[t])

    def norm_tile(t, _):
        at = rows_at(t)
        start = turned(startf, roll + rows * t, rows)
        startv[at, :] = start
        save(t).start()
        xhat, _ = norm_parts(start)
        normed = (xhat * vec_o[1:2, :] + vec_o[2:3, :]).astype(BF16)
        normv[at, :] = normed
        normtv[:, at] = jnp.transpose(normed, (1, 0))
        row = iota((rows, 128), 0) + rows * t
        member = (row >= lows) & (row < highs)
        mqv[at, :] = jnp.where(member, 1.0, 0.0).astype(BF16)
        mkv[at, :] = jnp.where(member | (lane >= SEGMENTS), 0.0, NEG).astype(BF16)
        return 0

    lax.fori_loop(0, tiles, norm_tile, 0)
    if linked:
        middle[0][2]()
    move(normtv, normt_o)
    move(mqv, mq_o)
    move(mkv, mk_o)
    for i in range(3):
        cols = slice(width * i, width * i + width)
        if linked:
            middle[i][3]()
            weights = w_in[i].reshape(width, width)
            if i < 2:
                middle[i + 1][2]()
            else:
                final[2]()
        else:
            weights = w_in[:, cols]
        scale = SCALE if i == 0 else 1.0

        def project(t, _):
            at = rows_at(t)
            packv[at, cols] = (dot(normv[at, :], weights) * scale).astype(BF16)
            return 0

        for t in range(tiles):
            project(t, 0)
        move(packv.at[:, cols], packed_o.at[:, cols])
    if linked:
        move(w_in, win_o)
    for copy in moves:
        copy.wait()
    for t in range(tiles):
        save(t).wait()
    if linked:
        final[3]()
        for plan in plans:
            plan[4]()
        for copy in feeds:
            copy.wait()


SIDE = 128


def pack_block(table, row):
    half = table.shape[-1] // 2
    left = jnp.concatenate([table[..., :half], table[..., half:]], -2)
    lines = jnp.concatenate([row[..., :SIDE], row[..., SIDE:]], -2)
    empty = jnp.zeros(left.shape[:-2] + (left.shape[-2] - 2, SIDE), F32)
    return jnp.concatenate([left, jnp.concatenate([lines, empty], -2)], -1)


def unpack_small(flat16, vec_o, hid_o, table):
    devices = flat16.shape[0]
    width = vec_o.shape[1]
    steps = devices * 8
    flat = flat16.astype(F32)
    half = width // 2
    row = jnp.concatenate([flat[:, 0, half:], flat[:, 1, half:]], 1).astype(BF16)
    per = width // devices
    lane = iota(row.shape, 1)
    spread = jnp.concatenate([jnp.where(lane // per == i, row, jnp.zeros_like(row)) for i in range(7)], 0)
    same = (iota((2 * SIDE, width), 0) % per == iota((2 * SIDE, width), 1) % per).astype(BF16)
    wide = dot(spread, same).reshape(7, devices, width)
    mine = (iota((devices, width), 1) // per == iota((devices, width), 0))[None]
    vecs = jnp.sum(jnp.where(mine, wide, 0.0), axis=1)
    vec_o[...] = jnp.concatenate([vecs, jnp.zeros((1, width), F32)], 0)
    hidden = hid_o.shape[1]
    part = hidden // devices
    at = iota((2 * SIDE, hidden), 0) - 7 * per
    pick = (at == iota((2 * SIDE, hidden), 1) % part).astype(BF16)
    own = iota((devices, hidden), 1) // part == iota((devices, hidden), 0)
    hid_o[...] = jnp.sum(jnp.where(own, dot(row, pick), 0.0), axis=0, keepdims=True)
    entries = jnp.concatenate([flat[:, :8, :half], flat[:, 8:, :half]], 2)
    table[:steps, :] = entries.reshape(steps, width).astype(BF16)
    table[steps:, :] = jnp.where(iota((16, width), 0) == 0, vecs[0:1], 0.0).astype(BF16)


def token_selector(stamps, flags, steps):
    rows = stamps.shape[1]
    chosen = (stamps == iota((steps, rows), 0)).astype(F32)
    flagged = jnp.where(iota((16, rows), 0) == 0, flags.astype(F32), 0.0)
    return jnp.concatenate([chosen, flagged], 0).astype(BF16)


def enter(tokens, segments, stamps, flags, hidden, shards, small, w_in):
    count, width = tokens.shape
    linked = shards is not None
    rows = min(TILE, count)
    tiles = count // rows
    anywhere = pl.BlockSpec(memory_space=pl.ANY)
    inside = pl.BlockSpec(memory_space=pltpu.VMEM)
    scalars = pl.BlockSpec(memory_space=pltpu.SMEM)
    lot = lambda *s: pltpu.SemaphoreType.DMA(s)
    big = lambda w, d: pltpu.VMEM((count, w), d)
    full = lambda a: (4, 2, 2, 2) + a
    outs = [
        jax.ShapeDtypeStruct((count, width), F32),
        jax.ShapeDtypeStruct((width, count), BF16),
        jax.ShapeDtypeStruct((count, 3 * width), BF16),
        jax.ShapeDtypeStruct((count, 128), BF16),
        jax.ShapeDtypeStruct((count, 128), BF16),
        jax.ShapeDtypeStruct((8, width), F32),
        jax.ShapeDtypeStruct((1, hidden), F32),
        jax.ShapeDtypeStruct((16,), jnp.int32),
    ]
    out_specs = [anywhere] * 5 + [inside] * 2 + [scalars]
    if linked:
        *vectors, stamps_table, s_in, s_out, s_up, s_down = shards
        operands = shards
        in_specs = [inside] * 9 + [anywhere] * 4
        outs += [
            jax.ShapeDtypeStruct((3,) + full(s_out.shape), BF16),
            jax.ShapeDtypeStruct(full(s_out.shape), BF16),
            jax.ShapeDtypeStruct((4, s_down.shape[0] + 64, width), BF16),
        ]
        out_specs += [anywhere] * 3
        scratch = [
            pltpu.VMEM((16, width // 2 + SIDE), BF16), pltpu.VMEM(full((16, width // 2 + SIDE)), BF16),
            pltpu.VMEM((3,) + full(s_out.shape), BF16),
            lot(5, GATHER_SLOTS), lot(5, GATHER_SLOTS), lot(5), lot(5, 3), lot(5, 3), lot(5),
        ]
        steps = 256
        compiler = params(collective_id=0, has_side_effects=True)
    else:
        operands, in_specs, scratch = [small, w_in], [inside] * 2, []
        steps = small.shape[0] * 8
        compiler = params()
    outs = pl.pallas_call(
        functools.partial(enter_kernel, linked),
        in_specs=[scalars, anywhere, inside, inside] + in_specs,
        out_specs=out_specs,
        out_shape=outs,
        scratch_shapes=scratch + [
            big(width, BF16), pltpu.VMEM((width // 128, count + rows, 128), F32), big(width, F32), big(width, BF16),
            pltpu.VMEM((width, count), BF16), big(3 * width, BF16), big(128, BF16), big(128, BF16),
            pltpu.VMEM((steps + 16, width), BF16), lot(16), lot(tiles),
        ],
        compiler_params=compiler,
        name="enter",
    )(segments, tokens, stamps, flags, *operands)
    return list(outs)


def key_range(cuts, row, rows):
    lo, hi = jnp.int32(1 << 20), jnp.int32(0)
    for i in range(SEGMENTS):
        first, size = cuts[1 + i], cuts[1 + SEGMENTS + i]
        meets = (size > 0) & (first < row + rows) & (first + size > row)
        lo = jnp.where(meets, jnp.minimum(lo, first), lo)
        hi = jnp.where(meets, jnp.maximum(hi, first + size), hi)
    return lo, hi


def list_tiles(cuts, length, tile, qi, ki):
    blank = length // tile

    def one(t, n):
        lo, hi = key_range(cuts, t * tile, tile)

        def put(j, n):
            qi[n], ki[n] = t, j
            return n + 1

        return lax.fori_loop(lo // tile, (hi + tile - 1) // tile, put, n)

    n = lax.fori_loop(0, blank, one, jnp.int32(1))
    for i in range(2):
        qi[n + i], ki[n + i] = jnp.int32(blank), jnp.int32(blank)
    return n // 2


def spots(qi, ki, i, tile, length):
    q, k = pl.multiple_of(qi[i] * tile, tile), pl.multiple_of(ki[i] * tile, tile)
    q_in, k_in = (pl.multiple_of(jnp.where(v >= length, 0, v), tile) for v in (q, k))
    return pl.ds(q_in, tile), pl.ds(k_in, tile), pl.ds(q, tile), pl.ds(k, tile)


def head_masks():
    first = iota((1, 128), 1) < HD
    return [jnp.where(first == (h == 0), 1.0, 0.0).astype(BF16) for h in range(2)]


def fwd_kernel(length, tile, npair, cuts, q_ref, k_ref, v_ref, mq_ref, mk_ref, o_ref, lse_ref,
               vt, acc, top, alpha, ps, qi, ki):
    g = pl.program_id(0)
    heads = 2 * npair
    only = head_masks()
    ones = jnp.ones((16, tile), BF16)
    count = list_tiles(cuts, length, tile, qi, ki)
    vt[...] = jnp.transpose(v_ref[...], (1, 0))
    acc[...] = jnp.zeros_like(acc)
    top[...] = jnp.full_like(top, -3e38)

    def scan(i, slot, hs):
        q_in, k_in, q, _ = spots(qi, ki, i, tile, length)
        for h in hs:
            cols = slice(128 * (h // 2), 128 * (h // 2) + 128)
            s = dot_nt(jnp.concatenate([k_ref[k_in, cols], mk_ref[k_in, :]], 1),
                       jnp.concatenate([q_ref[q_in, cols] * only[h % 2], mq_ref[q_in, :]], 1))
            old = top[h : h + 1, q]
            new = jnp.maximum(old, jnp.max(s, axis=0, keepdims=True))
            top[h : h + 1, q] = new
            alpha[slot, h : h + 1] = jnp.exp(old - new)
            ps[slot, h] = jnp.exp(s - new).astype(BF16)

    def mix(i, slot, hs):
        _, k_in, q, _ = spots(qi, ki, i, tile, length)
        for h in hs:
            values = jnp.concatenate([vt[HD * h : HD * h + HD, k_in], ones], 0)
            acc[h, :, q] = acc[h, :, q] * alpha[slot, h : h + 1] + dot(values, ps[slot, h])

    def step(m, _):
        def both(a, sa, b, sb):
            for h in range(heads):
                mix(a, sa, [h])
                scan(b, sb, [h])

        both(2 * m + 1, 0, 2 * m + 2, 1)
        both(2 * m + 2, 1, 2 * m + 3, 0)
        return 0

    scan(1, 0, range(heads))
    lax.fori_loop(0, count, step, 0)
    for i in range(npair):
        both = []
        for h in (2 * i, 2 * i + 1):
            total = acc[h, HD : HD + 1, :length]
            both.append(acc[h, :HD, :length] / total)
            lse_ref[pl.ds(heads * g + h, 1), :] = top[h : h + 1, :length] + jnp.log(total)
        o_ref[:, 128 * i : 128 * i + 128] = jnp.transpose(jnp.concatenate(both, 0), (1, 0)).astype(BF16)


def attention_forward(packed, cuts, mq, mk, tile, npair):
    length = packed.shape[0]
    steps = 4 // npair
    w, heads = 128 * npair, 2 * npair
    most = (length // tile) ** 2 + 8
    col = lambda o: pl.BlockSpec((length, w), lambda g, s: (0, g + o * steps))
    whole = pl.BlockSpec((length, 128), lambda g, s: (0, 0))
    return pl.pallas_call(
        functools.partial(fwd_kernel, length, tile, npair),
        grid_spec=pltpu.PrefetchScalarGridSpec(
            num_scalar_prefetch=1, grid=(steps,),
            in_specs=[col(0), col(1), col(2), whole, whole],
            out_specs=[col(0), pl.BlockSpec((8, length), lambda g, s: (0, 0))],
            scratch_shapes=[
                pltpu.VMEM((w, length), BF16),
                pltpu.VMEM((heads, HD + 16, length + tile), F32),
                pltpu.VMEM((8, length + tile), F32),
                pltpu.VMEM((2, 8, tile), F32),
                pltpu.VMEM((2, heads, tile, tile), BF16),
                pltpu.SMEM((most,), jnp.int32),
                pltpu.SMEM((most,), jnp.int32),
            ]),
        out_shape=[jax.ShapeDtypeStruct((length, 512), BF16), jax.ShapeDtypeStruct((8, length), F32)],
        compiler_params=params(63 << 20),
        name="attend_forward",
    )(cuts, packed, packed, packed, mq, mk)


def bwd_kernel(length, tile, npair, cuts, q_ref, k_ref, v_ref, do_ref, mq_ref, mk_ref, lse_ref, delta_ref,
               out_ref, dq_ref, dk_ref, dv_ref, out_again, kt, dk, dv, dqt, ps, dss, qi, ki):
    g = pl.program_id(0)
    heads = 2 * npair
    out_again[...] = out_ref[...]
    only = head_masks()
    count = list_tiles(cuts, length, tile, qi, ki)
    kt[...] = jnp.transpose(k_ref[...], (1, 0))
    for ref in (dk, dv, dqt):
        ref[...] = jnp.zeros_like(ref)

    def scan(i, slot):
        q_in, k_in, _, _ = spots(qi, ki, i, tile, length)
        for h in range(heads):
            at = slice(128 * (h // 2), 128 * (h // 2) + 128)
            lse = lse_ref[pl.ds(heads * g + h, 1), q_in]
            delta = delta_ref[pl.ds(heads * g + h, 1), q_in]
            s = dot_nt(jnp.concatenate([k_ref[k_in, at], mk_ref[k_in, :]], 1),
                       jnp.concatenate([q_ref[q_in, at] * only[h % 2], mq_ref[q_in, :]], 1))
            p = jnp.exp(s - lse)
            dp = dot_nt(v_ref[k_in, at], do_ref[q_in, at] * only[h % 2])
            cols = slice(tile * (h % 2), tile * (h % 2) + tile)
            ps[slot, h // 2, :, cols] = p.astype(BF16)
            dss[slot, h // 2, :, cols] = (p * (dp - delta)).astype(BF16)

    def mix(i, slot):
        q_in, k_in, q, k = spots(qi, ki, i, tile, length)
        for i in range(npair):
            at = slice(128 * i, 128 * i + 128)
            part = do_ref[q_in, at]
            dv[i, k, :] += dot(ps[slot, i], jnp.concatenate([part * only[0], part * only[1]], 0))
            part = q_ref[q_in, at]
            dk[i, k, :] += dot(dss[slot, i], jnp.concatenate([part * only[0], part * only[1]], 0))
            for h in (2 * i, 2 * i + 1):
                rows = slice(HD * h, HD * h + HD)
                cols = slice(tile * (h % 2), tile * (h % 2) + tile)
                dqt[rows, q] += dot(kt[rows, k_in], dss[slot, i, :, cols])

    def step(m, _):
        scan(2 * m + 2, 1)
        mix(2 * m + 1, 0)
        scan(2 * m + 3, 0)
        mix(2 * m + 2, 1)
        return 0

    scan(1, 0)
    lax.fori_loop(0, count, step, 0)
    for i in range(npair):
        cols = slice(128 * i, 128 * i + 128)
        dk_ref[:, cols] = dk[i, :length].astype(BF16)
        dv_ref[:, cols] = dv[i, :length].astype(BF16)
        dq_ref[:, cols] = jnp.transpose(dqt[cols, :length] * SCALE, (1, 0)).astype(BF16)


def attention_backward(packed, dmix, cuts, mq, mk, lse, delta, out, tile, npair):
    length = packed.shape[0]
    steps = 4 // npair
    w, heads = 128 * npair, 2 * npair
    most = (length // tile) ** 2 + 8
    col = lambda o: pl.BlockSpec((length, w), lambda g, s: (0, g + o * steps))
    whole = pl.BlockSpec((length, 128), lambda g, s: (0, 0))
    rowspec = pl.BlockSpec((8, length), lambda g, s: (0, 0))
    return pl.pallas_call(
        functools.partial(bwd_kernel, length, tile, npair),
        grid_spec=pltpu.PrefetchScalarGridSpec(
            num_scalar_prefetch=1, grid=(steps,),
            in_specs=[col(0), col(1), col(2), col(0), whole, whole, rowspec, rowspec, col(0)],
            out_specs=[col(0)] * 4,
            scratch_shapes=[
                pltpu.VMEM((w, length), BF16),
                pltpu.VMEM((npair, length + tile, 128), F32),
                pltpu.VMEM((npair, length + tile, 128), F32),
                pltpu.VMEM((w, length + tile), F32),
                pltpu.VMEM((2, npair, tile, 2 * tile), BF16),
                pltpu.VMEM((2, npair, tile, 2 * tile), BF16),
                pltpu.SMEM((most,), jnp.int32),
                pltpu.SMEM((most,), jnp.int32),
            ]),
        out_shape=[jax.ShapeDtypeStruct((length, 512), BF16)] * 3 + [jax.ShapeDtypeStruct(out.shape, out.dtype)],
        compiler_params=params(63 << 20),
        name="attend_backward",
    )(cuts, packed, packed, packed, dmix, mq, mk, lse, delta, out)


def gelu_parts(v):
    phi = 0.5 * lax.erf(v * 0.7071067811865476) + 0.5
    return v * phi, phi + v * jnp.exp2(v * v * -0.7213475204444817 - 1.3257480647361593)


def feed_kernel(linked, rows, f, cuts, start, mix, cot, w_out, vec, hid, *refs):
    if linked:
        lands = refs[:4]
        out_o, gmid_o, dmix_o, delta_o, gvec_o, ghid_o = refs[4:10]
        leaves = refs[10:14]
        refs = refs[14:]
    else:
        up_all, down_all = refs[:2]
        out_o, gmid_o, dmix_o, delta_o, gvec_o, ghid_o, gup_o, gdown_o, gout_o = refs[2:11]
        refs = refs[11:]
    (mid, res, gn2, n2, n2t, br, brt, mixv, projv, act0, act1, gpre0, gpre1, gup, gdt, gout, cotf, rsv,
     csem, tsem, osem) = refs[:21]
    count, width = mid.shape
    hidden = gup.shape[1]
    tiles, chunks = count // rows, hidden // f
    half = tiles // 2
    roll = cuts[0]
    spans = [slice(rows * t, rows * t + rows) for t in range(tiles)]
    loads = [pltpu.make_async_copy(w_out, projv, tsem.at[2 * tiles])]
    for t, at in enumerate(spans):
        pltpu.make_async_copy(mix.at[at], mixv.at[at], tsem.at[2 * t]).start()
        pltpu.make_async_copy(start.at[at], mid.at[at], tsem.at[2 * t + 1]).start()
    for i in range(width // 128):
        cols = pl.ds(128 * i, 128)
        loads.append(pltpu.make_async_copy(cot.at[:, cols], cotf.at[i, pl.ds(0, count), :], csem.at[i, 0]))
        loads.append(pltpu.make_async_copy(cot.at[pl.ds(0, rows), cols], cotf.at[i, pl.ds(count, rows), :], csem.at[i, 1]))
    for copy in loads:
        copy.start()

    def rows_at(t):
        return pl.ds(t * rows if isinstance(t, int) else pl.multiple_of(t * rows, rows), rows)

    if linked:
        up, down, sent, kept, got, lsem, lsend, lrecv, esend, erecv, eout = refs[21:]
        place = position()
        z, x, y, c = place
        sibling = device(z, x, y, 1 - c)

        def arrive(i, j, kind):
            xs, ys = plane(x, y)[i]
            if j == 0:
                src, dst = lands[i].at[:, :64, :], down.at[:, xs, ys, c]
            else:
                src = lands[i].at[:, 48 + 16 * j : 64 + 16 * j, :]
                dst = up.at[:, xs, ys, c, :, width * (j - 1) : width * j]
            if kind == 0:
                return pltpu.make_async_copy(src, dst, lsem.at[i, j])
            return remote(src, dst, lsend.at[i, j], lrecv.at[i, j], sibling)

        arrivals = [arrive(i, j, kind) for i in range(4) for j in range(5) for kind in range(2)]

        def exchange(j):
            at = slice(0, 128) if j == 0 else slice(128, 144)
            return remote(sent.at[:, :, :, at, :], got.at[:, :, :, at, :], esend.at[j], erecv.at[j], sibling)

        def leave(i):
            xs, ys = plane(x, y)[i]
            return pltpu.make_async_copy(got.at[:, xs, ys], leaves[i], eout.at[i])

        barrier = pltpu.get_barrier_semaphore()
        pl.semaphore_signal(barrier, inc=1, device_id=sibling, device_id_type=MESH)
        pl.semaphore_wait(barrier, 1)
        for copy in arrivals:
            copy.start()

    def cols_at(ch):
        return pl.ds(pl.multiple_of(ch * f, f), f)

    def up_chunk(ch):
        if linked:
            return up[:, :, :, :, :, cols_at(ch)].reshape(width, f)
        return up_all[:, cols_at(ch)]

    def down_chunk(ch):
        if linked:
            return down[ch].reshape(f, width)
        return down_all[cols_at(ch), :]

    for ref in (act1, gpre1, gup, gdt, gn2, gout, ghid_o, gvec_o):
        ref[...] = jnp.zeros_like(ref)
    loads[0].wait()

    def load_tile(t, i):
        at = rows_at(t)
        if i == 0:
            return pltpu.make_async_copy(mix.at[at], mixv.at[at], tsem.at[2 * t])
        return pltpu.make_async_copy(start.at[at], mid.at[at], tsem.at[2 * t + 1])

    def middle_tile(t, _):
        at = rows_at(t)
        load_tile(t, 0).wait()
        load_tile(t, 1).wait()
        middle = mid[at, :] + dot(mixv[at, :], projv[...]) + vec[3:4, :]
        put_columns(res, at, middle + vec[6:7, :])
        xhat, rstd = norm_parts(middle)
        mid[at, :] = xhat
        rsv[at, :] = jnp.broadcast_to(rstd, (rows, 128))
        normed = (xhat * vec[4:5, :] + vec[5:6, :]).astype(BF16)
        n2[at, :] = normed
        n2t[:, at] = jnp.transpose(normed, (1, 0))
        return 0

    lax.fori_loop(0, tiles, middle_tile, 0)
    for copy in loads[1:]:
        copy.wait()

    def branch_tile(t, _):
        at = rows_at(t)
        branch = turned(cotf, roll + rows * t, rows).astype(BF16)
        br[at, :] = branch
        brt[:, at] = jnp.transpose(branch, (1, 0))
        gvec_o[3:4, :] += jnp.sum(branch.astype(F32), axis=0, keepdims=True)
        return 0

    lax.fori_loop(0, tiles, branch_tile, 0)
    if linked:
        for copy in arrivals:
            copy.wait()

    def inner(ch, t, act, gpre):
        cols, at = cols_at(ch), rows_at(t)
        pre = dot(n2[at, :], up_chunk(ch)) + hid[:, cols]
        grad = dot_nt(br[at, :], down_chunk(ch))
        value, slope = gelu_parts(pre)
        act[...] = value.astype(BF16)
        low = (grad * slope).astype(BF16)
        gpre[...] = low
        ghid_o[:, cols] += jnp.sum(low.astype(F32), axis=0, keepdims=True)

    def outer(ch, t, act, gpre):
        cols, at = cols_at(ch), rows_at(t)
        a, g = act[...], gpre[...]
        more = dot(a, down_chunk(ch))
        for i in range(width // 128):
            res[i, at, :] += more[:, 128 * i : 128 * i + 128]
        gn2[at, :] += dot_nt(g, up_chunk(ch))
        gup[:, cols] += dot(n2t[:, at], g)
        gdt[:, cols] += dot(brt[:, at], a)

    def step(b, _):
        before = jnp.maximum(b - 1, 0)
        ch, t = b // half, 2 * (b % half)
        outer(before // half, 2 * (before % half) + 1, act1, gpre1)
        inner(ch, t, act0, gpre0)
        outer(ch, t, act0, gpre0)
        inner(ch, t + 1, act1, gpre1)
        return 0

    lax.fori_loop(0, chunks * half, step, 0)
    outer(chunks - 1, tiles - 1, act1, gpre1)
    wrap_columns(res, rows)
    if linked:
        for i in range(4):
            block = jnp.transpose(gdt[:, 512 * i : 512 * i + 512], (1, 0)).reshape(2, 2, 2, 64, width)
            first, second = block[:, :, 0], block[:, :, 1]
            kept[i, :, :, :64, :] = jnp.where(c == 0, first, second).astype(BF16)
            sent[i, :, :, :64, :] = jnp.where(c == 0, second, first).astype(BF16)
            cols = slice(width * i, width * i + width)
            block = gup[:, cols].reshape(4, 2, 2, 2, 16, width)
            first, second = block[:, :, :, 0], block[:, :, :, 1]
            at = slice(64 + 16 * i, 80 + 16 * i)
            kept[:, :, :, at, :] = jnp.where(c == 0, first, second).astype(BF16)
            sent[:, :, :, at, :] = jnp.where(c == 0, second, first).astype(BF16)
        exchange(0).start()
    else:
        for i in range(chunks):
            gup_o[:, i * f : (i + 1) * f] = gup[:, i * f : (i + 1) * f].astype(BF16)
            gdown_o[i * f : (i + 1) * f, :] = jnp.transpose(gdt[:, i * f : (i + 1) * f], (1, 0)).astype(BF16)
    heads = (iota((16, width), 1) // HD == iota((16, width), 0)).astype(BF16)

    def move(t, i):
        at = rows_at(t)
        src, dst = ((n2, out_o), (gn2, gmid_o), (br, dmix_o))[i]
        return pltpu.make_async_copy(src.at[at], dst.at[at], osem.at[3 * t + i])

    def last_tile(t, _):
        at = rows_at(t)
        n2[at, :] = turned(res, rows * t - roll, rows).astype(BF16)
        move(t, 0).start()
        xhat, rstd = mid[at, :], jnp.concatenate([rsv[at, :]] * (width // 128), 1)
        n = gn2[at, :]
        grad = turned(cotf, roll + rows * t, rows) + norm_back(n, xhat, rstd, vec[4:5, :])
        gn2[at, :] = grad
        move(t, 1).start()
        low = grad.astype(BF16)
        for i, term in enumerate((low.astype(F32), n * xhat, n)):
            gvec_o[i : i + 1, :] += jnp.sum(term, axis=0, keepdims=True)
        mixed = mixv[at, :]
        gout[...] += dot_tn(mixed, low)
        dmix = dot_nt(low, projv[...]).astype(BF16)
        br[at, :] = dmix
        move(t, 2).start()
        prod = dmix.astype(F32) * mixed.astype(F32)
        high = prod.astype(BF16)
        rest = (prod - high.astype(F32)).astype(BF16)
        delta_o[:, at] = (dot_nt(heads, high) + dot_nt(heads, rest))[:8]
        return 0

    for t in range(tiles):
        last_tile(t, 0)
    if linked:
        block = gout[...].reshape(4, 2, 2, 2, 16, width)
        first, second = block[:, :, :, 0], block[:, :, :, 1]
        kept[:, :, :, 128:, :] = jnp.where(c == 0, first, second).astype(BF16)
        sent[:, :, :, 128:, :] = jnp.where(c == 0, second, first).astype(BF16)
        exchange(1).start()
        exchange(0).wait()
        exchange(1).wait()
        for i in range(4):
            got[i] = (got[i].astype(F32) + kept[i].astype(F32)).astype(BF16)
        for i in range(4):
            leave(i).start()
        for i in range(4):
            leave(i).wait()
    else:
        gout_o[...] = gout[...].astype(BF16)
    for t in range(tiles):
        for i in range(3):
            move(t, i).wait()


def feed(cuts, start, mixture, cotangent, w_out, vec, hid, weights, linked):
    count, width = start.shape
    hidden = hid.shape[1]
    rows = min(TILE, count)
    f = min(512, hidden)
    tiles = count // rows
    anywhere = pl.BlockSpec(memory_space=pl.ANY)
    inside = pl.BlockSpec(memory_space=pltpu.VMEM)
    big = lambda d: pltpu.VMEM((count, width), d)
    flat = lambda: pltpu.VMEM((width, count), BF16)
    turning = pltpu.VMEM((width // 128, count + rows, 128), F32)
    lot = lambda *s: pltpu.SemaphoreType.DMA(s)
    scratch = (
        [big(F32), turning, big(F32), big(BF16), flat(), big(BF16), flat(), big(BF16), pltpu.VMEM((width, width), BF16)]
        + [pltpu.VMEM((rows, f), BF16)] * 4
        + [pltpu.VMEM((width, hidden), F32)] * 2
        + [pltpu.VMEM((width, width), F32), turning, pltpu.VMEM((count, 128), F32)]
        + [lot(width // 128, 2), lot(2 * tiles + 1), lot(3 * tiles)]
    )
    common = [
        jax.ShapeDtypeStruct((count, width), BF16),
        jax.ShapeDtypeStruct((count, width), F32),
        jax.ShapeDtypeStruct((count, width), BF16),
        jax.ShapeDtypeStruct((8, count), F32),
        jax.ShapeDtypeStruct((8, width), F32),
        jax.ShapeDtypeStruct((1, hidden), F32),
    ]
    if linked:
        weight_specs = [anywhere] * 4
        more = [jax.ShapeDtypeStruct((4, 144, width), BF16)] * 4
        more_specs = [anywhere] * 4
        scratch += [
            pltpu.VMEM((4, 2, 2, 2, 16, hidden), BF16), pltpu.VMEM((4, 2, 2, 2, 64, width), BF16),
        ] + [pltpu.VMEM((4, 2, 2, 144, width), BF16)] * 3 + [lot(4, 5), lot(4, 5), lot(4, 5), lot(2), lot(2), lot(4)]
        compiler = params(60 << 20, collective_id=1, has_side_effects=True)
    else:
        weight_specs = [inside] * 2
        more = [jax.ShapeDtypeStruct(s, BF16) for s in ((width, hidden), (hidden, width), (width, width))]
        more_specs = [inside] * 3
        compiler = params()
    return pl.pallas_call(
        functools.partial(feed_kernel, linked, rows, f),
        in_specs=[pl.BlockSpec(memory_space=pltpu.SMEM)] + [anywhere] * 4 + [inside] * 2 + weight_specs,
        out_specs=[anywhere] * 3 + [inside] * 3 + more_specs,
        out_shape=common + more,
        scratch_shapes=scratch,
        compiler_params=compiler,
        name="feed_forward",
    )(cuts, start, mixture, cotangent, w_out, vec, hid, *weights)


def leave_kernel(linked, cuts, dq, dk, dv, normt, w_in, start, gmid, stamps, flags, vec, gvec2, ghid, *refs):
    if linked:
        pieces = refs[:4]
        gtok_o, gin_o, gsmall_o, gfeed_o, gtab, gvec, land, esum, egot, esend, erecv, lsem = refs[4:16]
        places = [refs[16 + 7 * i : 23 + 7 * i] for i in range(4)]
        refs = refs[44:]
    else:
        gtok_o, gin_o, gtab, gvec = refs[:4]
        refs = refs[4:]
    grads, normv, startv, gmidv, weights, gtokf, gtokv, sem, tsem = refs
    count, width = start.shape
    rows = min(TILE, count)
    tiles = count // rows
    steps = gtab.shape[0] - 16
    fetches = {}

    def rows_at(t):
        return pl.ds(t * rows if isinstance(t, int) else pl.multiple_of(t * rows, rows), rows)

    def late(t, i):
        src, dst = ((start, startv), (gmid, gmidv))[i]
        return pltpu.make_async_copy(src.at[rows_at(t)], dst.at[rows_at(t)], tsem.at[2 * t + i])

    def fetch(name, src, dst):
        fetches[name] = pltpu.make_async_copy(src, dst, sem.at[len(fetches)])
        fetches[name].start()

    fetch("normed", normt, normv)
    fetch(0, dq, grads.at[0])
    fetch(1, dk, grads.at[1])
    gtab[...] = jnp.zeros_like(gtab)
    gvec[...] = jnp.zeros_like(gvec)
    if linked:
        place = position()
        z, x, y, c = place
        plans = [scatter_plan(place, *p) for p in places]

        def level(k):
            return remote(esum.at[peer(z, k)], egot.at[k - 1], esend.at[k - 1], erecv.at[k - 1],
                          device(peer(z, k), x, y, c))

        greet(*place)
        lands = [pltpu.make_async_copy(p, land.at[i], lsem.at[i]) for i, p in enumerate(pieces)]
    fetches["normed"].wait()
    for i in range(3):
        fetches[i].wait()
        total = dot(normv[...], grads[i]).astype(BF16)
        if linked:
            full = places[i][0]
            full[...] = total.reshape(full.shape)
            plans[i][0]()
            if i:
                plans[i - 1][1]()
        else:
            gin_o[:, width * i : width * i + width] = total
        if i == 0:
            fetch(2, dv, grads.at[2])
            if linked:
                for copy in lands:
                    copy.start()
            fetch("weights", w_in, weights)
        elif i == 1:
            for t in range(tiles):
                late(t, 0).start()
                late(t, 1).start()
    if linked:
        for copy in lands:
            copy.wait()
        for i in range(4):
            parts = [land[j, i].astype(F32) for j in range(4)]
            esum[i] = (parts[0] + parts[1] + parts[2] + parts[3]).astype(BF16)
        for k in (1, 2, 3):
            level(k).start()
    fetches["weights"].wait()
    if linked:
        plans[2][1]()

    def norm_tile(t, _):
        at = rows_at(t)
        n = sum(dot_nt(grads[i, at, :], weights[i]) for i in range(3))
        late(t, 0).wait()
        late(t, 1).wait()
        xhat, rstd = norm_parts(startv[at, :])
        put_columns(gtokf, at, gmidv[at, :] + norm_back(n, xhat, rstd, vec[1:2, :]))
        gvec[0:1, :] += jnp.sum(n * xhat, axis=0, keepdims=True)
        gvec[1:2, :] += jnp.sum(n, axis=0, keepdims=True)
        return 0

    lax.fori_loop(0, tiles, norm_tile, 0)
    wrap_columns(gtokf, rows)

    def move(t):
        return pltpu.make_async_copy(gtokv.at[rows_at(t)], gtok_o.at[rows_at(t)], tsem.at[2 * tiles + t])

    def back_tile(t, _):
        at = rows_at(t)
        grad = turned(gtokf, rows * t - cuts[0], rows)
        gtokv[at, :] = grad
        move(t).start()
        gtab[...] += dot(token_selector(stamps[:, at], flags[:, at], steps), grad.astype(BF16))
        return 0

    lax.fori_loop(0, tiles, back_tile, 0)
    if linked:
        pack_small(places[3][0], steps, gtab, gvec, gvec2, ghid)
        plans[3][0]()
        plans[0][2]()
        plans[3][1]()
        plans[1][2]()
        plans[2][2]()
        for k in (1, 2, 3):
            level(k).wait_recv()
        gfeed_o[...] = (esum[z].astype(F32) + egot[0].astype(F32)) + (egot[1].astype(F32) + egot[2].astype(F32))
        plans[3][2]()
        for i in range(3):
            plans[i][3](gin_o, width * i)
        plans[3][3](gsmall_o, 0)
        for plan in plans:
            plan[4]()
        for k in (1, 2, 3):
            level(k).wait_send()
    for t in range(tiles):
        move(t).wait()


def pack_small(full, steps, gtab, gvec, gvec2, ghid):
    width = gtab.shape[1]
    groups = steps // 8
    per = width // groups
    sums = [gtab[steps : steps + 1, :], gvec[0:1, :], gvec[1:2, :]]
    sums += [gvec2[i : i + 1, :] for i in range(4)]
    mine = iota((groups, width), 1) // per == iota((groups, width), 0)
    spread = jnp.concatenate([jnp.where(mine, v, 0.0) for v in sums], 0).astype(BF16)
    same = (iota((width, width), 0) % per == iota((width, width), 1) % per).astype(BF16)
    wide = dot(spread, same).reshape(7, groups, width)
    lane = iota((1, width), 1)
    row = jnp.zeros((groups, width), F32)
    for i in range(7):
        row = jnp.where(lane // per == i, wide[i], row)
    hidden = ghid.shape[1]
    part = hidden // groups
    own = iota((groups, hidden), 1) // part == iota((groups, hidden), 0)
    pick = (iota((hidden, width), 0) % part == iota((hidden, width), 1) - 7 * per).astype(BF16)
    row = row + dot(jnp.where(own, ghid[...], 0.0).astype(BF16), pick)
    table = gtab[:steps, :].reshape(groups, 8, width)
    full[...] = pack_block(table, row[:, None, : 2 * SIDE]).astype(BF16).reshape(full.shape)


def leave(cuts, dq, dk, dv, normt, w_in, start, gmid, stamps, flags, vec, gvec2, ghid, steps, pieces, linked):
    count, width = start.shape
    rows = min(TILE, count)
    tiles = count // rows
    lot = lambda *s: pltpu.SemaphoreType.DMA(s)
    anywhere = pl.BlockSpec(memory_space=pl.ANY)
    inside = pl.BlockSpec(memory_space=pltpu.VMEM)
    sums = [jax.ShapeDtypeStruct((steps + 16, width), F32), jax.ShapeDtypeStruct((8, width), F32)]
    if linked:
        more = [jax.ShapeDtypeStruct(s, F32) for s in ((16, 3 * width), (16, width // 2 + SIDE), (144, width))]
        scratch = [pltpu.VMEM(a.shape, F32) for a in sums]
        scratch += [pltpu.VMEM(n + (144, width), BF16) for n in ((4, 4), (4,), (3,))] + [lot(3), lot(3), lot(4)]
        for w in (width, width, width, width // 2 + SIDE):
            scratch += scatter_buffers(16, w) + [lot(SCATTER_SLOTS), lot(SCATTER_SLOTS)]
        compiler = params(collective_id=2, has_side_effects=True)
    else:
        more = [jax.ShapeDtypeStruct((width, 3 * width), BF16)] + sums
        scratch = []
        compiler = params()
    big = lambda d: pltpu.VMEM((count, width), d)
    return pl.pallas_call(
        functools.partial(leave_kernel, linked),
        in_specs=[pl.BlockSpec(memory_space=pltpu.SMEM)] + [anywhere] * 7 + [inside] * 5 + [anywhere] * len(pieces),
        out_specs=[anywhere] + [inside] * len(more),
        out_shape=[jax.ShapeDtypeStruct((count, width), F32)] + more,
        scratch_shapes=scratch + [
            pltpu.VMEM((3, count, width), BF16), pltpu.VMEM((width, count), BF16), big(F32), big(F32),
            pltpu.VMEM((3, width, width), BF16), pltpu.VMEM((width // 128, count + rows, 128), F32), big(F32),
            lot(5), lot(3 * tiles),
        ],
        compiler_params=compiler,
        name="leave",
    )(cuts, dq, dk, dv, normt, w_in, start, gmid, stamps, flags, vec, gvec2, ghid, *pieces)


def unpack_kernel(sizes, gtok, gin, gsmall, gfeed, gtok_o, gin_o, gtab_o, gout_o, gup_o, gdown_o, *refs):
    *vecs, held, there, back = refs
    parts = there.shape[0]
    rows = gtok.shape[0] // parts
    spans = [pl.ds(rows * i, rows) for i in range(parts)]
    reads = [pltpu.make_async_copy(gtok.at[at], held.at[at], there.at[i]) for i, at in enumerate(spans)]
    writes = [pltpu.make_async_copy(held.at[at], gtok_o.at[at], back.at[i]) for i, at in enumerate(spans)]
    for copy in reads:
        copy.start()
    for i in range(parts):
        reads[i].wait()
        writes[i].start()
        if i == 0:
            unpack_rest(sizes, gin, gsmall, gfeed, gin_o, gtab_o, gout_o, gup_o, gdown_o, *vecs)
    for copy in writes:
        copy.wait()


def unpack_rest(sizes, gin, gsmall, gfeed, gin_o, gtab_o, gout_o, gup_o, gdown_o, *vecs):
    width = gtab_o.shape[1]
    half = width // 2
    gin_o[...] = gin[...]
    gtab_o[:, :half] = gsmall[:8, :half]
    gtab_o[:, half:] = gsmall[8:, :half]
    row = jnp.concatenate([gsmall[0:1, half:], gsmall[1:2, half:]], 1)
    gdown_o[...] = gfeed[:64, :]
    for i in range(gup_o.shape[1] // width):
        gup_o[:, width * i : width * (i + 1)] = gfeed[64 + 16 * i : 80 + 16 * i, :]
    gout_o[...] = gfeed[128:144, :]
    at = 0
    for ref, size in zip(vecs, sizes):
        ref[...] = row[:, at : at + size]
        at += size


def unpack(gtok, gin, gsmall, gfeed, hidden, sizes):
    width = gfeed.shape[1]
    shapes = [gtok.shape, gin.shape, (8, width), (16, width), (16, hidden), (64, width)] + [(1, n) for n in sizes]
    anywhere = pl.BlockSpec(memory_space=pl.ANY)
    inside = pl.BlockSpec(memory_space=pltpu.VMEM)
    parts = 8
    return pl.pallas_call(
        functools.partial(unpack_kernel, sizes),
        in_specs=[anywhere] + [inside] * 3,
        out_specs=[anywhere] + [inside] * (len(shapes) - 1),
        out_shape=[jax.ShapeDtypeStruct(s, F32) for s in shapes],
        scratch_shapes=[pltpu.VMEM(gtok.shape, F32), pltpu.SemaphoreType.DMA((parts,)), pltpu.SemaphoreType.DMA((parts,))],
        compiler_params=params(),
        name="unpack",
    )(gtok, gin, gsmall, gfeed)


def exchange_plane(arrays):
    out = [arrays[0]]
    for array, (dx, dy) in zip(arrays[1:], ((1, 0), (0, 1), (1, 1))):
        pairs = [(4 * dp + fs, 4 * (dp ^ dx) + (fs ^ (2 * dy))) for dp in range(8) for fs in range(4)]
        out.append(lax.ppermute(array, AXES, pairs))
    return out


def per_device(fast, tokens, mask_flags, timesteps, segment_ids, mask_embed, time_table, first_gain, first_bias,
               input_proj, output_proj, output_bias, second_gain, second_bias, hidden_weight, hidden_bias,
               down_weight, down_bias, cotangent):
    count, width = tokens.shape
    hidden = hidden_weight.shape[1]
    vectors = (mask_embed, first_gain, first_bias, output_bias, second_gain, second_bias, down_bias)
    segments = segment_ids.reshape(-1)
    stamps, flags = timesteps[None], mask_flags[None]
    if fast:
        lines = [v[None] for v in vectors + (hidden_bias,)]
        sizes = [v.shape[1] for v in lines]
        shards = lines + [time_table, input_proj, output_proj, hidden_weight, down_weight]
        *kept, w_in, w_out, own = enter(tokens, segments, stamps, flags, hidden, shards, None, None)
        w_in, w_out = w_in.reshape(3, width, width), w_out.reshape(width, width)
        steps = time_table.shape[0] * 32
        weights = exchange_plane([own] * 4)
    else:
        whole = lambda a: lax.all_gather(a, AXES, axis=0, tiled=True)
        groups = whole(time_table).reshape(-1, 8, width)
        pieces = jnp.concatenate(
            [whole(v).reshape(groups.shape[0], -1) for v in vectors + (hidden_bias,)], 1
        )
        pieces = jnp.pad(pieces, ((0, 0), (0, 2 * SIDE - pieces.shape[1])))[:, None]
        small = pack_block(groups.astype(F32), pieces.astype(F32)).astype(BF16)
        w_in, w_out = whole(input_proj), whole(output_proj)
        weights = [whole(hidden_weight), whole(down_weight)]
        steps = groups.shape[0] * 8
        kept = enter(tokens, segments, stamps, flags, hidden, None, small, w_in)
        w_in = w_in.reshape(width, 3, width).transpose(1, 0, 2)
    start, normt, packed, mq, mk, vec, hid, cuts = kept

    mixture, lse = attention_forward(packed, cuts, mq, mk, 256, 4)
    out, gmid, dmix, delta, gvec2, ghid, *grads = feed(cuts, start, mixture, cotangent, w_out, vec, hid, weights, fast)
    pieces = exchange_plane(grads) if fast else []
    dq, dk, dv, out = attention_backward(packed, dmix, cuts, mq, mk, lse, delta, out, 256, 4)
    gtok, gin, *rest = leave(
        cuts, dq, dk, dv, normt, w_in, start, gmid, stamps, flags, vec, gvec2, ghid, steps, pieces, fast
    )
    if fast:
        gtok, gin, gtab, gout, gup, gdown, *small = unpack(gtok, gin, rest[0], rest[1], hidden, sizes)
        gmask, gg1, gb1, gob, gg2, gb2, gdb, ghb = [v.reshape(-1) for v in small]
    else:
        total = lambda a: lax.psum_scatter(a.astype(F32), AXES, scatter_dimension=0, tiled=True)
        gtab, gvec1 = rest
        gup, gdown, gout = grads
        gin, gout, gup, gdown = (total(a) for a in (gin, gout, gup, gdown))
        gmask = total(gtab[steps])
        gtab = total(gtab[:steps])
        gg1, gb1, gob, gg2, gb2, gdb, ghb = (
            total(a) for a in (gvec1[0], gvec1[1], gvec2[0], gvec2[1], gvec2[2], gvec2[3], ghid[0])
        )
    return (out, gtok, gmask, gtab, gg1, gb1, gin, gout, gob, gg2, gb2, gup, ghb, gdown, gdb)


def solution(mesh):
    split = P(AXES)
    rows = P(AXES, None)
    fast = tuple(mesh.shape[a] for a in AXES) == (8, 4)
    placed = (rows, split, split, rows, split, rows, split, split, rows, rows, split, split, split, rows, split, rows,
              split, rows)
    return jax.shard_map(
        functools.partial(per_device, fast),
        mesh=mesh,
        in_specs=placed,
        out_specs=(rows, rows, split, rows, split, split, rows, rows, split, split, split, rows, split, rows, split),
        check_vma=False,
    )
```

```python
import functools

import jax
import jax.numpy as jnp
from jax import lax
from jax.experimental import pallas as pl
from jax.experimental.pallas import tpu as pltpu
from jax.sharding import PartitionSpec as P

F32, BF16 = jnp.float32, jnp.bfloat16
HD = 64
SEGMENTS = 4
SCALE = HD ** -0.5
NEG = -1e30
EPSILON = 1e-05
AXES = ("dp", "fsdp")
MESH = pl.DeviceIdType.MESH
VMEM_BYTES = 58 << 20
TILE = 512


def dot(a, b):
    return jnp.dot(a, b, preferred_element_type=F32)


def dot_nt(a, b):
    return lax.dot_general(a, b, (((1,), (1,)), ((), ())), preferred_element_type=F32)


def dot_tn(a, b):
    return lax.dot_general(a, b, (((0,), (0,)), ((), ())), preferred_element_type=F32)


def iota(shape, dim):
    return lax.broadcasted_iota(jnp.int32, shape, dim)


def params(room=VMEM_BYTES, **more):
    return pltpu.CompilerParams(vmem_limit_bytes=room, **more)


def norm_parts(h):
    centered = h - jnp.mean(h, axis=-1, keepdims=True)
    rstd = lax.rsqrt(jnp.mean(centered * centered, axis=-1, keepdims=True) + EPSILON)
    return centered * rstd, rstd


def norm_back(n, xhat, rstd, gain):
    ng = n * gain
    first = jnp.mean(ng, axis=-1, keepdims=True)
    second = jnp.mean(ng * xhat, axis=-1, keepdims=True)
    return rstd * (ng - first - xhat * second)


def position():
    dp, fs = lax.axis_index("dp"), lax.axis_index("fsdp")
    return dp // 2, dp % 2, fs // 2, fs % 2


def device(z, x, y, c):
    return (z * 2 + x, y * 2 + c)


def peer(z, k):
    return lax.rem(z + k, 4)


def greet(z, x, y, c):
    barrier = pltpu.get_barrier_semaphore()
    partners = [device(peer(z, k), x, y, c) for k in (1, 2, 3)]
    partners += [device(z, xs, ys, c) for xs, ys in plane(x, y)[1:]] + [device(z, x, y, 1 - c)]
    for partner in partners:
        pl.semaphore_signal(barrier, inc=1, device_id=partner, device_id_type=MESH)
    pl.semaphore_wait(barrier, len(partners))


def remote(src, dst, send, recv, target):
    return pltpu.make_async_remote_copy(
        src_ref=src, dst_ref=dst, send_sem=send, recv_sem=recv, device_id=target, device_id_type=MESH
    )


def plane(x, y):
    return ((x, y), (1 - x, y), (x, 1 - y), (1 - x, 1 - y))


def gather_plan(place, shard, whole, send, recv, local):
    z, x, y, c = place
    spots = plane(x, y)
    level = lambda k: peer(z, 4 - k)

    def copy(slot):
        if slot < 4 and slot:
            src, dst, to = shard, whole.at[z, x, y, c], device(peer(z, slot), x, y, c)
        elif 4 <= slot < 16:
            k = slot % 4
            dst, to = whole.at[level(k), x, y, c], device(z, *spots[slot // 4], c)
            src = dst if k else shard
        else:
            xs, ys = spots[max(slot - 15, 0)]
            src = dst = whole.at[:, xs, ys, c]
            to = device(z, x, y, 1 - c)
        return remote(src, dst, send.at[slot], recv.at[slot], to)

    keep = pltpu.make_async_copy(shard, whole.at[z, x, y, c], local)

    def begin():
        keep.start()
        for k in (1, 2, 3):
            copy(k).start()

    def spread():
        for k in range(4):
            if k:
                copy(k).wait_recv()
            for kind in (4, 8, 12):
                copy(kind + k).start()
        keep.wait()
        copy(0).start()

    def finish():
        for i in range(3):
            for k in range(4):
                copy(4 + 4 * i + k).wait_recv()
            copy(16 + i).start()

    def ready():
        for slot in (0, 16, 17, 18):
            copy(slot).wait_recv()

    def drain():
        for slot in range(GATHER_SLOTS):
            copy(slot).wait_send()

    return begin, spread, finish, ready, drain


GATHER_SLOTS = 19


def scatter_plan(place, full, own, got, land, last, send, recv):
    z, x, y, c = place
    spots = plane(x, y)

    def copy(slot):
        if slot == 0:
            src, dst, to = full.at[:, :, :, 1 - c], got, device(z, x, y, 1 - c)
        elif slot < 4:
            xs, ys = spots[slot]
            src, dst, to = own.at[:, xs, ys], land.at[slot - 1], device(z, xs, ys, c)
        else:
            k = slot - 3
            src, dst, to = got.at[peer(z, k), 0, 0], last.at[k - 1], device(peer(z, k), x, y, c)
        return remote(src, dst, send.at[slot], recv.at[slot], to)

    def to_sibling():
        copy(0).start()

    def to_plane():
        copy(0).wait_recv()
        for i in range(4):
            own[i] = (full[i, :, :, c].astype(F32) + got[i].astype(F32)).astype(BF16)
        for slot in (1, 2, 3):
            copy(slot).start()

    def to_levels():
        for slot in (1, 2, 3):
            copy(slot).wait_recv()
        for i in range(4):
            parts = [own[i, x, y]] + [land[j, i] for j in range(3)]
            parts = [p.astype(F32) for p in parts]
            got[i, 0, 0] = (parts[0] + parts[1] + parts[2] + parts[3]).astype(BF16)
        for slot in (4, 5, 6):
            copy(slot).start()

    def total(out, at):
        for slot in (4, 5, 6):
            copy(slot).wait_recv()
        rest = last[0].astype(F32) + last[1].astype(F32) + last[2].astype(F32)
        out[:, at : at + rest.shape[1]] = got[z, 0, 0].astype(F32) + rest

    def drain():
        for slot in range(SCATTER_SLOTS):
            copy(slot).wait_send()

    return to_sibling, to_plane, to_levels, total, drain


SCATTER_SLOTS = 7


def scatter_buffers(rows, width):
    return [pltpu.VMEM(s, BF16) for s in (
        (4, 2, 2, 2, rows, width), (4, 2, 2, rows, width), (4, 2, 2, rows, width), (3, 4, rows, width),
        (3, rows, width))]


def find_cuts(seg, length, cuts):
    def first_at_least(s):
        def step(_, span):
            lo, hi = span
            mid = (lo + hi) // 2
            below = seg[jnp.minimum(mid, length - 1)] < s
            live = lo < hi
            return jnp.where(live & below, mid + 1, lo), jnp.where(live & jnp.logical_not(below), mid, hi)

        return lax.fori_loop(0, length.bit_length(), step, (jnp.int32(0), jnp.int32(length)))[0]

    edges = [jnp.int32(0)] + [first_at_least(s) for s in range(1, SEGMENTS)] + [jnp.int32(length)]
    sizes = [edges[i + 1] - edges[i] for i in range(SEGMENTS)]
    roll, most = edges[0], sizes[0]
    for edge, size in zip(edges[1:], sizes[1:]):
        roll = jnp.where(size > most, edge, roll)
        most = jnp.maximum(size, most)
    cuts[0] = roll
    firsts = []
    for i in range(SEGMENTS):
        at = edges[i] - roll
        firsts.append(jnp.where(at < 0, at + length, at))
        cuts[1 + i] = firsts[i]
        cuts[1 + SEGMENTS + i] = sizes[i]
    return roll, firsts, sizes


def turned(ref, first, rows):
    length = ref.shape[1] - rows
    at = jnp.where(first >= length, first - length, first)
    at = jnp.where(at < 0, at + length, at)
    return jnp.concatenate([ref[i, pl.ds(at, rows), :] for i in range(ref.shape[0])], 1)


def put_columns(ref, at, value):
    for i in range(ref.shape[0]):
        ref[i, at, :] = value[:, 128 * i : 128 * i + 128]


def wrap_columns(ref, rows):
    length = ref.shape[1] - rows
    for i in range(ref.shape[0]):
        ref[i, length:, :] = ref[i, :rows, :]


def enter_kernel(linked, seg, tok, stamps, flags, *refs):
    if linked:
        vectors, stamps_table, s_in, s_out, s_up, s_down = refs[:8], *refs[8:13]
        refs = refs[13:]
        (start_o, normt_o, packed_o, mq_o, mk_o, vec_o, hid_o, cuts, win_o, wout_o, feed_o,
         s_small, small, w_in, send, recv, local, fsend, frecv, flocal) = refs[:20]
        refs = refs[20:]
    else:
        small, w_in, start_o, normt_o, packed_o, mq_o, mk_o, vec_o, hid_o, cuts = refs[:10]
        refs = refs[10:]
    tokv, startf, startv, normv, normtv, packv, mqv, mkv, table, moved, tsem = refs
    count, width = tok.shape
    rows = min(TILE, count)
    tiles = count // rows
    fetch = pltpu.make_async_copy(tok, tokv, moved.at[0])
    fetch.start()
    if linked:
        place = position()
        z, x, y, c = place
        greet(*place)
        row = jnp.zeros((1, width), F32)
        at = 0
        for v in vectors:
            size = v.shape[1]
            row = row + dot(v[...], (iota((size, width), 1) == iota((size, width), 0) + at).astype(BF16))
            at += size
        s_small[...] = pack_block(stamps_table[...].astype(F32), row[:, : 2 * SIDE]).astype(BF16)
        plans = [
            gather_plan(place, s, w, send.at[a], recv.at[a], local.at[a])
            for a, (s, w) in enumerate(
                [(s_small, small)]
                + [(s_in.at[:, width * i : width * i + width], w_in.at[i]) for i in range(3)]
                + [(s_out, wout_o)]
            )
        ]
        first, *middle, final = plans
        parts = [(s_down, 0, 64)] + [(s_up.at[:, width * j : width * j + width], 64 + 16 * j, 16) for j in range(4)]

        def feed_copy(j, k):
            src, at, size = parts[j]
            dst = feed_o.at[z, at : at + size, :]
            if k == 0:
                return pltpu.make_async_copy(src, dst, flocal.at[j])
            return remote(src, dst, fsend.at[j, k - 1], frecv.at[j, k - 1], device(peer(z, k), x, y, c))

        feeds = [feed_copy(j, k) for j in range(5) for k in range(4)]
        for plan in plans[:4]:
            plan[0]()
    roll, firsts, sizes = find_cuts(seg, count, cuts)
    if linked:
        for plan in plans[:4]:
            plan[1]()
        final[0]()
        for copy in feeds:
            copy.start()
        first[2]()
        first[3]()
    unpack_small(small[...].reshape((-1,) + small.shape[-2:]), vec_o, hid_o, table)
    fetch.wait()
    moves = []

    def move(src, dst):
        copy = pltpu.make_async_copy(src, dst, moved.at[len(moves) + 1])
        copy.start()
        moves.append(copy)

    def rows_at(t):
        return pl.ds(t * rows if isinstance(t, int) else pl.multiple_of(t * rows, rows), rows)

    def start_tile(t, _):
        at = rows_at(t)
        select = token_selector(stamps[:, at], flags[:, at], table.shape[0] - 16)
        put_columns(startf, at, tokv[at, :].astype(F32) + dot_tn(select, table[...]))
        return 0

    lax.fori_loop(0, tiles, start_tile, 0)
    wrap_columns(startf, rows)
    lane = iota((1, 128), 1)
    lows, highs = jnp.zeros((1, 128), jnp.int32), jnp.zeros((1, 128), jnp.int32)
    for i in range(SEGMENTS):
        lows = jnp.where(lane == i, firsts[i], lows)
        highs = jnp.where(lane == i, firsts[i] + sizes[i], highs)
    if linked:
        final[1]()
    def save(t):
        return pltpu.make_async_copy(startv.at[rows_at(t)], start_o.at[rows_at(t)], tsem.at[t])

    def norm_tile(t, _):
        at = rows_at(t)
        start = turned(startf, roll + rows * t, rows)
        startv[at, :] = start
        save(t).start()
        xhat, _ = norm_parts(start)
        normed = (xhat * vec_o[1:2, :] + vec_o[2:3, :]).astype(BF16)
        normv[at, :] = normed
        normtv[:, at] = jnp.transpose(normed, (1, 0))
        row = iota((rows, 128), 0) + rows * t
        member = (row >= lows) & (row < highs)
        mqv[at, :] = jnp.where(member, 1.0, 0.0).astype(BF16)
        mkv[at, :] = jnp.where(member | (lane >= SEGMENTS), 0.0, NEG).astype(BF16)
        return 0

    lax.fori_loop(0, tiles, norm_tile, 0)
    if linked:
        middle[0][2]()
    move(normtv, normt_o)
    move(mqv, mq_o)
    move(mkv, mk_o)
    for i in range(3):
        cols = slice(width * i, width * i + width)
        if linked:
            middle[i][3]()
            weights = w_in[i].reshape(width, width)
            if i < 2:
                middle[i + 1][2]()
            else:
                final[2]()
        else:
            weights = w_in[:, cols]
        scale = SCALE if i == 0 else 1.0

        def project(t, _):
            at = rows_at(t)
            packv[at, cols] = (dot(normv[at, :], weights) * scale).astype(BF16)
            return 0

        for t in range(tiles):
            project(t, 0)
        move(packv.at[:, cols], packed_o.at[:, cols])
    if linked:
        move(w_in, win_o)
    for copy in moves:
        copy.wait()
    for t in range(tiles):
        save(t).wait()
    if linked:
        final[3]()
        for plan in plans:
            plan[4]()
        for copy in feeds:
            copy.wait()


SIDE = 128


def pack_block(table, row):
    half = table.shape[-1] // 2
    left = jnp.concatenate([table[..., :half], table[..., half:]], -2)
    lines = jnp.concatenate([row[..., :SIDE], row[..., SIDE:]], -2)
    empty = jnp.zeros(left.shape[:-2] + (left.shape[-2] - 2, SIDE), F32)
    return jnp.concatenate([left, jnp.concatenate([lines, empty], -2)], -1)


def unpack_small(flat16, vec_o, hid_o, table):
    devices = flat16.shape[0]
    width = vec_o.shape[1]
    steps = devices * 8
    flat = flat16.astype(F32)
    half = width // 2
    row = jnp.concatenate([flat[:, 0, half:], flat[:, 1, half:]], 1).astype(BF16)
    per = width // devices
    lane = iota(row.shape, 1)
    spread = jnp.concatenate([jnp.where(lane // per == i, row, jnp.zeros_like(row)) for i in range(7)], 0)
    same = (iota((2 * SIDE, width), 0) % per == iota((2 * SIDE, width), 1) % per).astype(BF16)
    wide = dot(spread, same).reshape(7, devices, width)
    mine = (iota((devices, width), 1) // per == iota((devices, width), 0))[None]
    vecs = jnp.sum(jnp.where(mine, wide, 0.0), axis=1)
    vec_o[...] = jnp.concatenate([vecs, jnp.zeros((1, width), F32)], 0)
    hidden = hid_o.shape[1]
    part = hidden // devices
    at = iota((2 * SIDE, hidden), 0) - 7 * per
    pick = (at == iota((2 * SIDE, hidden), 1) % part).astype(BF16)
    own = iota((devices, hidden), 1) // part == iota((devices, hidden), 0)
    hid_o[...] = jnp.sum(jnp.where(own, dot(row, pick), 0.0), axis=0, keepdims=True)
    entries = jnp.concatenate([flat[:, :8, :half], flat[:, 8:, :half]], 2)
    table[:steps, :] = entries.reshape(steps, width).astype(BF16)
    table[steps:, :] = jnp.where(iota((16, width), 0) == 0, vecs[0:1], 0.0).astype(BF16)


def token_selector(stamps, flags, steps):
    rows = stamps.shape[1]
    chosen = (stamps == iota((steps, rows), 0)).astype(F32)
    flagged = jnp.where(iota((16, rows), 0) == 0, flags.astype(F32), 0.0)
    return jnp.concatenate([chosen, flagged], 0).astype(BF16)


def enter(tokens, segments, stamps, flags, hidden, shards, small, w_in):
    count, width = tokens.shape
    linked = shards is not None
    rows = min(TILE, count)
    tiles = count // rows
    anywhere = pl.BlockSpec(memory_space=pl.ANY)
    inside = pl.BlockSpec(memory_space=pltpu.VMEM)
    scalars = pl.BlockSpec(memory_space=pltpu.SMEM)
    lot = lambda *s: pltpu.SemaphoreType.DMA(s)
    big = lambda w, d: pltpu.VMEM((count, w), d)
    full = lambda a: (4, 2, 2, 2) + a
    outs = [
        jax.ShapeDtypeStruct((count, width), F32),
        jax.ShapeDtypeStruct((width, count), BF16),
        jax.ShapeDtypeStruct((count, 3 * width), BF16),
        jax.ShapeDtypeStruct((count, 128), BF16),
        jax.ShapeDtypeStruct((count, 128), BF16),
        jax.ShapeDtypeStruct((8, width), F32),
        jax.ShapeDtypeStruct((1, hidden), F32),
        jax.ShapeDtypeStruct((16,), jnp.int32),
    ]
    out_specs = [anywhere] * 5 + [inside] * 2 + [scalars]
    if linked:
        *vectors, stamps_table, s_in, s_out, s_up, s_down = shards
        operands = shards
        in_specs = [inside] * 9 + [anywhere] * 4
        outs += [
            jax.ShapeDtypeStruct((3,) + full(s_out.shape), BF16),
            jax.ShapeDtypeStruct(full(s_out.shape), BF16),
            jax.ShapeDtypeStruct((4, s_down.shape[0] + 64, width), BF16),
        ]
        out_specs += [anywhere] * 3
        scratch = [
            pltpu.VMEM((16, width // 2 + SIDE), BF16), pltpu.VMEM(full((16, width // 2 + SIDE)), BF16),
            pltpu.VMEM((3,) + full(s_out.shape), BF16),
            lot(5, GATHER_SLOTS), lot(5, GATHER_SLOTS), lot(5), lot(5, 3), lot(5, 3), lot(5),
        ]
        steps = 256
        compiler = params(collective_id=0, has_side_effects=True)
    else:
        operands, in_specs, scratch = [small, w_in], [inside] * 2, []
        steps = small.shape[0] * 8
        compiler = params()
    outs = pl.pallas_call(
        functools.partial(enter_kernel, linked),
        in_specs=[scalars, anywhere, inside, inside] + in_specs,
        out_specs=out_specs,
        out_shape=outs,
        scratch_shapes=scratch + [
            big(width, BF16), pltpu.VMEM((width // 128, count + rows, 128), F32), big(width, F32), big(width, BF16),
            pltpu.VMEM((width, count), BF16), big(3 * width, BF16), big(128, BF16), big(128, BF16),
            pltpu.VMEM((steps + 16, width), BF16), lot(16), lot(tiles),
        ],
        compiler_params=compiler,
        name="enter",
    )(segments, tokens, stamps, flags, *operands)
    return list(outs)


def key_range(cuts, row, rows):
    lo, hi = jnp.int32(1 << 20), jnp.int32(0)
    for i in range(SEGMENTS):
        first, size = cuts[1 + i], cuts[1 + SEGMENTS + i]
        meets = (size > 0) & (first < row + rows) & (first + size > row)
        lo = jnp.where(meets, jnp.minimum(lo, first), lo)
        hi = jnp.where(meets, jnp.maximum(hi, first + size), hi)
    return lo, hi


def list_tiles(cuts, length, tile, qi, ki):
    blank = length // tile

    def one(t, n):
        lo, hi = key_range(cuts, t * tile, tile)

        def put(j, n):
            qi[n], ki[n] = t, j
            return n + 1

        return lax.fori_loop(lo // tile, (hi + tile - 1) // tile, put, n)

    n = lax.fori_loop(0, blank, one, jnp.int32(1))
    for i in range(2):
        qi[n + i], ki[n + i] = jnp.int32(blank), jnp.int32(blank)
    return n // 2


def spots(qi, ki, i, tile, length):
    q, k = pl.multiple_of(qi[i] * tile, tile), pl.multiple_of(ki[i] * tile, tile)
    q_in, k_in = (pl.multiple_of(jnp.where(v >= length, 0, v), tile) for v in (q, k))
    return pl.ds(q_in, tile), pl.ds(k_in, tile), pl.ds(q, tile), pl.ds(k, tile)


def head_masks():
    first = iota((1, 128), 1) < HD
    return [jnp.where(first == (h == 0), 1.0, 0.0).astype(BF16) for h in range(2)]


def fwd_kernel(length, tile, npair, cuts, q_ref, k_ref, v_ref, mq_ref, mk_ref, o_ref, lse_ref,
               vt, acc, top, alpha, ps, qi, ki):
    g = pl.program_id(0)
    heads = 2 * npair
    only = head_masks()
    ones = jnp.ones((16, tile), BF16)
    count = list_tiles(cuts, length, tile, qi, ki)
    vt[...] = jnp.transpose(v_ref[...], (1, 0))
    acc[...] = jnp.zeros_like(acc)
    top[...] = jnp.full_like(top, -3e38)

    def scan(i, slot, hs):
        q_in, k_in, q, _ = spots(qi, ki, i, tile, length)
        for h in hs:
            cols = slice(128 * (h // 2), 128 * (h // 2) + 128)
            s = dot_nt(jnp.concatenate([k_ref[k_in, cols], mk_ref[k_in, :]], 1),
                       jnp.concatenate([q_ref[q_in, cols] * only[h % 2], mq_ref[q_in, :]], 1))
            old = top[h : h + 1, q]
            new = jnp.maximum(old, jnp.max(s, axis=0, keepdims=True))
            top[h : h + 1, q] = new
            alpha[slot, h : h + 1] = jnp.exp(old - new)
            ps[slot, h] = jnp.exp(s - new).astype(BF16)

    def mix(i, slot, hs):
        _, k_in, q, _ = spots(qi, ki, i, tile, length)
        for h in hs:
            values = jnp.concatenate([vt[HD * h : HD * h + HD, k_in], ones], 0)
            acc[h, :, q] = acc[h, :, q] * alpha[slot, h : h + 1] + dot(values, ps[slot, h])

    def step(m, _):
        def both(a, sa, b, sb):
            for h in range(heads):
                mix(a, sa, [h])
                scan(b, sb, [h])

        both(2 * m + 1, 0, 2 * m + 2, 1)
        both(2 * m + 2, 1, 2 * m + 3, 0)
        return 0

    scan(1, 0, range(heads))
    lax.fori_loop(0, count, step, 0)
    for i in range(npair):
        both = []
        for h in (2 * i, 2 * i + 1):
            total = acc[h, HD : HD + 1, :length]
            both.append(acc[h, :HD, :length] / total)
            lse_ref[pl.ds(heads * g + h, 1), :] = top[h : h + 1, :length] + jnp.log(total)
        o_ref[:, 128 * i : 128 * i + 128] = jnp.transpose(jnp.concatenate(both, 0), (1, 0)).astype(BF16)


def attention_forward(packed, cuts, mq, mk, tile, npair):
    length = packed.shape[0]
    steps = 4 // npair
    w, heads = 128 * npair, 2 * npair
    most = (length // tile) ** 2 + 8
    col = lambda o: pl.BlockSpec((length, w), lambda g, s: (0, g + o * steps))
    whole = pl.BlockSpec((length, 128), lambda g, s: (0, 0))
    return pl.pallas_call(
        functools.partial(fwd_kernel, length, tile, npair),
        grid_spec=pltpu.PrefetchScalarGridSpec(
            num_scalar_prefetch=1, grid=(steps,),
            in_specs=[col(0), col(1), col(2), whole, whole],
            out_specs=[col(0), pl.BlockSpec((8, length), lambda g, s: (0, 0))],
            scratch_shapes=[
                pltpu.VMEM((w, length), BF16),
                pltpu.VMEM((heads, HD + 16, length + tile), F32),
                pltpu.VMEM((8, length + tile), F32),
                pltpu.VMEM((2, 8, tile), F32),
                pltpu.VMEM((2, heads, tile, tile), BF16),
                pltpu.SMEM((most,), jnp.int32),
                pltpu.SMEM((most,), jnp.int32),
            ]),
        out_shape=[jax.ShapeDtypeStruct((length, 512), BF16), jax.ShapeDtypeStruct((8, length), F32)],
        compiler_params=params(63 << 20),
        name="attend_forward",
    )(cuts, packed, packed, packed, mq, mk)


def bwd_kernel(length, tile, npair, cuts, q_ref, k_ref, v_ref, do_ref, mq_ref, mk_ref, lse_ref, delta_ref,
               out_ref, dq_ref, dk_ref, dv_ref, out_again, kt, dk, dv, dqt, ps, dss, qi, ki):
    g = pl.program_id(0)
    heads = 2 * npair
    out_again[...] = out_ref[...]
    only = head_masks()
    count = list_tiles(cuts, length, tile, qi, ki)
    kt[...] = jnp.transpose(k_ref[...], (1, 0))
    for ref in (dk, dv, dqt):
        ref[...] = jnp.zeros_like(ref)

    def scan(i, slot):
        q_in, k_in, _, _ = spots(qi, ki, i, tile, length)
        for h in range(heads):
            at = slice(128 * (h // 2), 128 * (h // 2) + 128)
            lse = lse_ref[pl.ds(heads * g + h, 1), q_in]
            delta = delta_ref[pl.ds(heads * g + h, 1), q_in]
            s = dot_nt(jnp.concatenate([k_ref[k_in, at], mk_ref[k_in, :]], 1),
                       jnp.concatenate([q_ref[q_in, at] * only[h % 2], mq_ref[q_in, :]], 1))
            p = jnp.exp(s - lse)
            dp = dot_nt(v_ref[k_in, at], do_ref[q_in, at] * only[h % 2])
            cols = slice(tile * (h % 2), tile * (h % 2) + tile)
            ps[slot, h // 2, :, cols] = p.astype(BF16)
            dss[slot, h // 2, :, cols] = (p * (dp - delta)).astype(BF16)

    def mix(i, slot):
        q_in, k_in, q, k = spots(qi, ki, i, tile, length)
        for i in range(npair):
            at = slice(128 * i, 128 * i + 128)
            part = do_ref[q_in, at]
            dv[i, k, :] += dot(ps[slot, i], jnp.concatenate([part * only[0], part * only[1]], 0))
            part = q_ref[q_in, at]
            dk[i, k, :] += dot(dss[slot, i], jnp.concatenate([part * only[0], part * only[1]], 0))
            for h in (2 * i, 2 * i + 1):
                rows = slice(HD * h, HD * h + HD)
                cols = slice(tile * (h % 2), tile * (h % 2) + tile)
                dqt[rows, q] += dot(kt[rows, k_in], dss[slot, i, :, cols])

    def step(m, _):
        scan(2 * m + 2, 1)
        mix(2 * m + 1, 0)
        scan(2 * m + 3, 0)
        mix(2 * m + 2, 1)
        return 0

    scan(1, 0)
    lax.fori_loop(0, count, step, 0)
    for i in range(npair):
        cols = slice(128 * i, 128 * i + 128)
        dk_ref[:, cols] = dk[i, :length].astype(BF16)
        dv_ref[:, cols] = dv[i, :length].astype(BF16)
        dq_ref[:, cols] = jnp.transpose(dqt[cols, :length] * SCALE, (1, 0)).astype(BF16)


def attention_backward(packed, dmix, cuts, mq, mk, lse, delta, out, tile, npair):
    length = packed.shape[0]
    steps = 4 // npair
    w, heads = 128 * npair, 2 * npair
    most = (length // tile) ** 2 + 8
    col = lambda o: pl.BlockSpec((length, w), lambda g, s: (0, g + o * steps))
    whole = pl.BlockSpec((length, 128), lambda g, s: (0, 0))
    rowspec = pl.BlockSpec((8, length), lambda g, s: (0, 0))
    return pl.pallas_call(
        functools.partial(bwd_kernel, length, tile, npair),
        grid_spec=pltpu.PrefetchScalarGridSpec(
            num_scalar_prefetch=1, grid=(steps,),
            in_specs=[col(0), col(1), col(2), col(0), whole, whole, rowspec, rowspec, col(0)],
            out_specs=[col(0)] * 4,
            scratch_shapes=[
                pltpu.VMEM((w, length), BF16),
                pltpu.VMEM((npair, length + tile, 128), F32),
                pltpu.VMEM((npair, length + tile, 128), F32),
                pltpu.VMEM((w, length + tile), F32),
                pltpu.VMEM((2, npair, tile, 2 * tile), BF16),
                pltpu.VMEM((2, npair, tile, 2 * tile), BF16),
                pltpu.SMEM((most,), jnp.int32),
                pltpu.SMEM((most,), jnp.int32),
            ]),
        out_shape=[jax.ShapeDtypeStruct((length, 512), BF16)] * 3 + [jax.ShapeDtypeStruct(out.shape, out.dtype)],
        compiler_params=params(63 << 20),
        name="attend_backward",
    )(cuts, packed, packed, packed, dmix, mq, mk, lse, delta, out)


def gelu_parts(v):
    phi = 0.5 * lax.erf(v * 0.7071067811865476) + 0.5
    return v * phi, phi + v * jnp.exp2(v * v * -0.7213475204444817 - 1.3257480647361593)


def feed_kernel(linked, rows, f, cuts, start, mix, cot, w_out, vec, hid, *refs):
    if linked:
        lands = refs[:4]
        out_o, gmid_o, dmix_o, delta_o, gvec_o, ghid_o = refs[4:10]
        leaves = refs[10:14]
        refs = refs[14:]
    else:
        up_all, down_all = refs[:2]
        out_o, gmid_o, dmix_o, delta_o, gvec_o, ghid_o, gup_o, gdown_o, gout_o = refs[2:11]
        refs = refs[11:]
    (mid, res, gn2, n2, n2t, br, brt, mixv, projv, act0, act1, gpre0, gpre1, gup, gdt, gout, cotf, rsv,
     csem, tsem, osem) = refs[:21]
    count, width = mid.shape
    hidden = gup.shape[1]
    tiles, chunks = count // rows, hidden // f
    half = tiles // 2
    roll = cuts[0]
    spans = [slice(rows * t, rows * t + rows) for t in range(tiles)]
    loads = [pltpu.make_async_copy(w_out, projv, tsem.at[2 * tiles])]
    for t, at in enumerate(spans):
        pltpu.make_async_copy(mix.at[at], mixv.at[at], tsem.at[2 * t]).start()
        pltpu.make_async_copy(start.at[at], mid.at[at], tsem.at[2 * t + 1]).start()
    for i in range(width // 128):
        cols = pl.ds(128 * i, 128)
        loads.append(pltpu.make_async_copy(cot.at[:, cols], cotf.at[i, pl.ds(0, count), :], csem.at[i, 0]))
        loads.append(pltpu.make_async_copy(cot.at[pl.ds(0, rows), cols], cotf.at[i, pl.ds(count, rows), :], csem.at[i, 1]))
    for copy in loads:
        copy.start()

    def rows_at(t):
        return pl.ds(t * rows if isinstance(t, int) else pl.multiple_of(t * rows, rows), rows)

    if linked:
        up, down, sent, kept, got, lsem, lsend, lrecv, esend, erecv, eout = refs[21:]
        place = position()
        z, x, y, c = place
        sibling = device(z, x, y, 1 - c)

        def arrive(i, j, kind):
            xs, ys = plane(x, y)[i]
            if j == 0:
                src, dst = lands[i].at[:, :64, :], down.at[:, xs, ys, c]
            else:
                src = lands[i].at[:, 48 + 16 * j : 64 + 16 * j, :]
                dst = up.at[:, xs, ys, c, :, width * (j - 1) : width * j]
            if kind == 0:
                return pltpu.make_async_copy(src, dst, lsem.at[i, j])
            return remote(src, dst, lsend.at[i, j], lrecv.at[i, j], sibling)

        arrivals = [arrive(i, j, kind) for i in range(4) for j in range(5) for kind in range(2)]

        def exchange(j):
            at = slice(0, 128) if j == 0 else slice(128, 144)
            return remote(sent.at[:, :, :, at, :], got.at[:, :, :, at, :], esend.at[j], erecv.at[j], sibling)

        def leave(i):
            xs, ys = plane(x, y)[i]
            return pltpu.make_async_copy(got.at[:, xs, ys], leaves[i], eout.at[i])

        barrier = pltpu.get_barrier_semaphore()
        pl.semaphore_signal(barrier, inc=1, device_id=sibling, device_id_type=MESH)
        pl.semaphore_wait(barrier, 1)
        for copy in arrivals:
            copy.start()

    def cols_at(ch):
        return pl.ds(pl.multiple_of(ch * f, f), f)

    def up_chunk(ch):
        if linked:
            return up[:, :, :, :, :, cols_at(ch)].reshape(width, f)
        return up_all[:, cols_at(ch)]

    def down_chunk(ch):
        if linked:
            return down[ch].reshape(f, width)
        return down_all[cols_at(ch), :]

    for ref in (act1, gpre1, gup, gdt, gn2, gout, gvec_o):
        ref[...] = jnp.zeros_like(ref)
    loads[0].wait()

    def load_tile(t, i):
        at = rows_at(t)
        if i == 0:
            return pltpu.make_async_copy(mix.at[at], mixv.at[at], tsem.at[2 * t])
        return pltpu.make_async_copy(start.at[at], mid.at[at], tsem.at[2 * t + 1])

    def middle_tile(t, _):
        at = rows_at(t)
        load_tile(t, 0).wait()
        load_tile(t, 1).wait()
        middle = mid[at, :] + dot(mixv[at, :], projv[...]) + vec[3:4, :]
        put_columns(res, at, middle + vec[6:7, :])
        xhat, rstd = norm_parts(middle)
        mid[at, :] = xhat
        rsv[at, :] = jnp.broadcast_to(rstd, (rows, 128))
        normed = (xhat * vec[4:5, :] + vec[5:6, :]).astype(BF16)
        n2[at, :] = normed
        n2t[:width, at] = jnp.transpose(normed, (1, 0))
        n2t[width:, at] = jnp.ones((16, rows), BF16)
        return 0

    lax.fori_loop(0, tiles, middle_tile, 0)
    for copy in loads[1:]:
        copy.wait()

    def branch_tile(t, _):
        at = rows_at(t)
        branch = turned(cotf, roll + rows * t, rows).astype(BF16)
        br[at, :] = branch
        brt[:, at] = jnp.transpose(branch, (1, 0))
        gvec_o[3:4, :] += jnp.sum(branch.astype(F32), axis=0, keepdims=True)
        return 0

    lax.fori_loop(0, tiles, branch_tile, 0)
    if linked:
        for copy in arrivals:
            copy.wait()

    def inner(ch, t, act, gpre):
        cols, at = cols_at(ch), rows_at(t)
        pre = dot(n2[at, :], up_chunk(ch)) + hid[:, cols]
        grad = dot_nt(br[at, :], down_chunk(ch))
        value, slope = gelu_parts(pre)
        act[...] = value.astype(BF16)
        low = (grad * slope).astype(BF16)
        gpre[...] = low

    def outer(ch, t, act, gpre):
        cols, at = cols_at(ch), rows_at(t)
        a, g = act[...], gpre[...]
        more = dot(a, down_chunk(ch))
        for i in range(width // 128):
            res[i, at, :] += more[:, 128 * i : 128 * i + 128]
        gn2[at, :] += dot_nt(g, up_chunk(ch))
        gup[:, cols] += dot(n2t[:, at], g)
        gdt[:, cols] += dot(brt[:, at], a)

    def step(b, _):
        before = jnp.maximum(b - 1, 0)
        ch, t = b // half, 2 * (b % half)
        outer(before // half, 2 * (before % half) + 1, act1, gpre1)
        inner(ch, t, act0, gpre0)
        outer(ch, t, act0, gpre0)
        inner(ch, t + 1, act1, gpre1)
        return 0

    lax.fori_loop(0, chunks * half, step, 0)
    outer(chunks - 1, tiles - 1, act1, gpre1)
    wrap_columns(res, rows)
    ghid_o[...] = gup[width : width + 1, :]
    if linked:
        for i in range(4):
            block = jnp.transpose(gdt[:, 512 * i : 512 * i + 512], (1, 0)).reshape(2, 2, 2, 64, width)
            first, second = block[:, :, 0], block[:, :, 1]
            kept[i, :, :, :64, :] = jnp.where(c == 0, first, second).astype(BF16)
            sent[i, :, :, :64, :] = jnp.where(c == 0, second, first).astype(BF16)
            cols = slice(width * i, width * i + width)
            block = gup[:width, cols].reshape(4, 2, 2, 2, 16, width)
            first, second = block[:, :, :, 0], block[:, :, :, 1]
            at = slice(64 + 16 * i, 80 + 16 * i)
            kept[:, :, :, at, :] = jnp.where(c == 0, first, second).astype(BF16)
            sent[:, :, :, at, :] = jnp.where(c == 0, second, first).astype(BF16)
        exchange(0).start()
    else:
        for i in range(chunks):
            gup_o[:, i * f : (i + 1) * f] = gup[:width, i * f : (i + 1) * f].astype(BF16)
            gdown_o[i * f : (i + 1) * f, :] = jnp.transpose(gdt[:, i * f : (i + 1) * f], (1, 0)).astype(BF16)
    heads = (iota((16, width), 1) // HD == iota((16, width), 0)).astype(BF16)

    def move(t, i):
        at = rows_at(t)
        src, dst = ((n2, out_o), (gn2, gmid_o), (br, dmix_o))[i]
        return pltpu.make_async_copy(src.at[at], dst.at[at], osem.at[3 * t + i])

    def last_tile(t, _):
        at = rows_at(t)
        n2[at, :] = turned(res, rows * t - roll, rows).astype(BF16)
        move(t, 0).start()
        xhat, rstd = mid[at, :], jnp.concatenate([rsv[at, :]] * (width // 128), 1)
        n = gn2[at, :]
        grad = turned(cotf, roll + rows * t, rows) + norm_back(n, xhat, rstd, vec[4:5, :])
        gn2[at, :] = grad
        move(t, 1).start()
        low = grad.astype(BF16)
        for i, term in enumerate((low.astype(F32), n * xhat, n)):
            gvec_o[i : i + 1, :] += jnp.sum(term, axis=0, keepdims=True)
        mixed = mixv[at, :]
        gout[...] += dot_tn(mixed, low)
        dmix = dot_nt(low, projv[...]).astype(BF16)
        br[at, :] = dmix
        move(t, 2).start()
        prod = dmix.astype(F32) * mixed.astype(F32)
        high = prod.astype(BF16)
        rest = (prod - high.astype(F32)).astype(BF16)
        delta_o[:, at] = (dot_nt(heads, high) + dot_nt(heads, rest))[:8]
        return 0

    for t in range(tiles):
        last_tile(t, 0)
    if linked:
        block = gout[...].reshape(4, 2, 2, 2, 16, width)
        first, second = block[:, :, :, 0], block[:, :, :, 1]
        kept[:, :, :, 128:, :] = jnp.where(c == 0, first, second).astype(BF16)
        sent[:, :, :, 128:, :] = jnp.where(c == 0, second, first).astype(BF16)
        exchange(1).start()
        exchange(0).wait()
        exchange(1).wait()
        for i in range(4):
            got[i] = (got[i].astype(F32) + kept[i].astype(F32)).astype(BF16)
        for i in range(4):
            leave(i).start()
        for i in range(4):
            leave(i).wait()
    else:
        gout_o[...] = gout[...].astype(BF16)
    for t in range(tiles):
        for i in range(3):
            move(t, i).wait()


def feed(cuts, start, mixture, cotangent, w_out, vec, hid, weights, linked):
    count, width = start.shape
    hidden = hid.shape[1]
    rows = min(TILE, count)
    f = min(512, hidden)
    tiles = count // rows
    anywhere = pl.BlockSpec(memory_space=pl.ANY)
    inside = pl.BlockSpec(memory_space=pltpu.VMEM)
    big = lambda d: pltpu.VMEM((count, width), d)
    flat = lambda more=0: pltpu.VMEM((width + more, count), BF16)
    turning = pltpu.VMEM((width // 128, count + rows, 128), F32)
    lot = lambda *s: pltpu.SemaphoreType.DMA(s)
    scratch = (
        [big(F32), turning, big(F32), big(BF16), flat(16), big(BF16), flat(), big(BF16), pltpu.VMEM((width, width), BF16)]
        + [pltpu.VMEM((rows, f), BF16)] * 4
        + [pltpu.VMEM((width + 16, hidden), F32), pltpu.VMEM((width, hidden), F32)]
        + [pltpu.VMEM((width, width), F32), turning, pltpu.VMEM((count, 128), F32)]
        + [lot(width // 128, 2), lot(2 * tiles + 1), lot(3 * tiles)]
    )
    common = [
        jax.ShapeDtypeStruct((count, width), BF16),
        jax.ShapeDtypeStruct((count, width), F32),
        jax.ShapeDtypeStruct((count, width), BF16),
        jax.ShapeDtypeStruct((8, count), F32),
        jax.ShapeDtypeStruct((8, width), F32),
        jax.ShapeDtypeStruct((1, hidden), F32),
    ]
    if linked:
        weight_specs = [anywhere] * 4
        more = [jax.ShapeDtypeStruct((4, 144, width), BF16)] * 4
        more_specs = [anywhere] * 4
        scratch += [
            pltpu.VMEM((4, 2, 2, 2, 16, hidden), BF16), pltpu.VMEM((4, 2, 2, 2, 64, width), BF16),
        ] + [pltpu.VMEM((4, 2, 2, 144, width), BF16)] * 3 + [lot(4, 5), lot(4, 5), lot(4, 5), lot(2), lot(2), lot(4)]
        compiler = params(60 << 20, collective_id=1, has_side_effects=True)
    else:
        weight_specs = [inside] * 2
        more = [jax.ShapeDtypeStruct(s, BF16) for s in ((width, hidden), (hidden, width), (width, width))]
        more_specs = [inside] * 3
        compiler = params()
    return pl.pallas_call(
        functools.partial(feed_kernel, linked, rows, f),
        in_specs=[pl.BlockSpec(memory_space=pltpu.SMEM)] + [anywhere] * 4 + [inside] * 2 + weight_specs,
        out_specs=[anywhere] * 3 + [inside] * 3 + more_specs,
        out_shape=common + more,
        scratch_shapes=scratch,
        compiler_params=compiler,
        name="feed_forward",
    )(cuts, start, mixture, cotangent, w_out, vec, hid, *weights)


def leave_kernel(linked, cuts, dq, dk, dv, normt, w_in, start, gmid, stamps, flags, vec, gvec2, ghid, *refs):
    if linked:
        pieces = refs[:4]
        gtok_o, gin_o, gsmall_o, gfeed_o, gtab, gvec, land, esum, egot, esend, erecv, lsem = refs[4:16]
        places = [refs[16 + 7 * i : 23 + 7 * i] for i in range(4)]
        refs = refs[44:]
    else:
        gtok_o, gin_o, gtab, gvec = refs[:4]
        refs = refs[4:]
    grads, normv, startv, gmidv, weights, gtokf, gtokv, sem, tsem = refs
    count, width = start.shape
    rows = min(TILE, count)
    tiles = count // rows
    steps = gtab.shape[0] - 16
    fetches = {}

    def rows_at(t):
        return pl.ds(t * rows if isinstance(t, int) else pl.multiple_of(t * rows, rows), rows)

    def late(t, i):
        src, dst = ((start, startv), (gmid, gmidv))[i]
        return pltpu.make_async_copy(src.at[rows_at(t)], dst.at[rows_at(t)], tsem.at[2 * t + i])

    def fetch(name, src, dst):
        fetches[name] = pltpu.make_async_copy(src, dst, sem.at[len(fetches)])
        fetches[name].start()

    fetch("normed", normt, normv)
    fetch(0, dq, grads.at[0])
    fetch(1, dk, grads.at[1])
    gtab[...] = jnp.zeros_like(gtab)
    gvec[...] = jnp.zeros_like(gvec)
    if linked:
        place = position()
        z, x, y, c = place
        plans = [scatter_plan(place, *p) for p in places]

        def level(k):
            return remote(esum.at[peer(z, k)], egot.at[k - 1], esend.at[k - 1], erecv.at[k - 1],
                          device(peer(z, k), x, y, c))

        greet(*place)
        lands = [pltpu.make_async_copy(p, land.at[i], lsem.at[i]) for i, p in enumerate(pieces)]
    fetches["normed"].wait()
    for i in range(3):
        fetches[i].wait()
        total = dot(normv[...], grads[i]).astype(BF16)
        if linked:
            full = places[i][0]
            full[...] = total.reshape(full.shape)
            plans[i][0]()
            if i:
                plans[i - 1][1]()
        else:
            gin_o[:, width * i : width * i + width] = total
        if i == 0:
            fetch(2, dv, grads.at[2])
            if linked:
                for copy in lands:
                    copy.start()
            fetch("weights", w_in, weights)
        elif i == 1:
            for t in range(tiles):
                late(t, 0).start()
                late(t, 1).start()
    if linked:
        for copy in lands:
            copy.wait()
        for i in range(4):
            parts = [land[j, i].astype(F32) for j in range(4)]
            esum[i] = (parts[0] + parts[1] + parts[2] + parts[3]).astype(BF16)
        for k in (1, 2, 3):
            level(k).start()
    fetches["weights"].wait()
    if linked:
        plans[2][1]()

    def norm_tile(t, _):
        at = rows_at(t)
        n = sum(dot_nt(grads[i, at, :], weights[i]) for i in range(3))
        late(t, 0).wait()
        late(t, 1).wait()
        xhat, rstd = norm_parts(startv[at, :])
        put_columns(gtokf, at, gmidv[at, :] + norm_back(n, xhat, rstd, vec[1:2, :]))
        gvec[0:1, :] += jnp.sum(n * xhat, axis=0, keepdims=True)
        gvec[1:2, :] += jnp.sum(n, axis=0, keepdims=True)
        return 0

    lax.fori_loop(0, tiles, norm_tile, 0)
    wrap_columns(gtokf, rows)

    def move(t):
        return pltpu.make_async_copy(gtokv.at[rows_at(t)], gtok_o.at[rows_at(t)], tsem.at[2 * tiles + t])

    def back_tile(t, _):
        at = rows_at(t)
        grad = turned(gtokf, rows * t - cuts[0], rows)
        gtokv[at, :] = grad
        move(t).start()
        gtab[...] += dot(token_selector(stamps[:, at], flags[:, at], steps), grad.astype(BF16))
        return 0

    lax.fori_loop(0, tiles, back_tile, 0)
    if linked:
        pack_small(places[3][0], steps, gtab, gvec, gvec2, ghid)
        plans[3][0]()
        plans[0][2]()
        plans[3][1]()
        plans[1][2]()
        plans[2][2]()
        for k in (1, 2, 3):
            level(k).wait_recv()
        gfeed_o[...] = (esum[z].astype(F32) + egot[0].astype(F32)) + (egot[1].astype(F32) + egot[2].astype(F32))
        plans[3][2]()
        for i in range(3):
            plans[i][3](gin_o, width * i)
        plans[3][3](gsmall_o, 0)
        for plan in plans:
            plan[4]()
        for k in (1, 2, 3):
            level(k).wait_send()
    for t in range(tiles):
        move(t).wait()


def pack_small(full, steps, gtab, gvec, gvec2, ghid):
    width = gtab.shape[1]
    groups = steps // 8
    per = width // groups
    sums = [gtab[steps : steps + 1, :], gvec[0:1, :], gvec[1:2, :]]
    sums += [gvec2[i : i + 1, :] for i in range(4)]
    mine = iota((groups, width), 1) // per == iota((groups, width), 0)
    spread = jnp.concatenate([jnp.where(mine, v, 0.0) for v in sums], 0).astype(BF16)
    same = (iota((width, width), 0) % per == iota((width, width), 1) % per).astype(BF16)
    wide = dot(spread, same).reshape(7, groups, width)
    lane = iota((1, width), 1)
    row = jnp.zeros((groups, width), F32)
    for i in range(7):
        row = jnp.where(lane // per == i, wide[i], row)
    hidden = ghid.shape[1]
    part = hidden // groups
    own = iota((groups, hidden), 1) // part == iota((groups, hidden), 0)
    pick = (iota((hidden, width), 0) % part == iota((hidden, width), 1) - 7 * per).astype(BF16)
    row = row + dot(jnp.where(own, ghid[...], 0.0).astype(BF16), pick)
    table = gtab[:steps, :].reshape(groups, 8, width)
    full[...] = pack_block(table, row[:, None, : 2 * SIDE]).astype(BF16).reshape(full.shape)


def leave(cuts, dq, dk, dv, normt, w_in, start, gmid, stamps, flags, vec, gvec2, ghid, steps, pieces, linked):
    count, width = start.shape
    rows = min(TILE, count)
    tiles = count // rows
    lot = lambda *s: pltpu.SemaphoreType.DMA(s)
    anywhere = pl.BlockSpec(memory_space=pl.ANY)
    inside = pl.BlockSpec(memory_space=pltpu.VMEM)
    sums = [jax.ShapeDtypeStruct((steps + 16, width), F32), jax.ShapeDtypeStruct((8, width), F32)]
    if linked:
        more = [jax.ShapeDtypeStruct(s, F32) for s in ((16, 3 * width), (16, width // 2 + SIDE), (144, width))]
        scratch = [pltpu.VMEM(a.shape, F32) for a in sums]
        scratch += [pltpu.VMEM(n + (144, width), BF16) for n in ((4, 4), (4,), (3,))] + [lot(3), lot(3), lot(4)]
        for w in (width, width, width, width // 2 + SIDE):
            scratch += scatter_buffers(16, w) + [lot(SCATTER_SLOTS), lot(SCATTER_SLOTS)]
        compiler = params(collective_id=2, has_side_effects=True)
    else:
        more = [jax.ShapeDtypeStruct((width, 3 * width), BF16)] + sums
        scratch = []
        compiler = params()
    big = lambda d: pltpu.VMEM((count, width), d)
    return pl.pallas_call(
        functools.partial(leave_kernel, linked),
        in_specs=[pl.BlockSpec(memory_space=pltpu.SMEM)] + [anywhere] * 7 + [inside] * 5 + [anywhere] * len(pieces),
        out_specs=[anywhere] + [inside] * len(more),
        out_shape=[jax.ShapeDtypeStruct((count, width), F32)] + more,
        scratch_shapes=scratch + [
            pltpu.VMEM((3, count, width), BF16), pltpu.VMEM((width, count), BF16), big(F32), big(F32),
            pltpu.VMEM((3, width, width), BF16), pltpu.VMEM((width // 128, count + rows, 128), F32), big(F32),
            lot(5), lot(3 * tiles),
        ],
        compiler_params=compiler,
        name="leave",
    )(cuts, dq, dk, dv, normt, w_in, start, gmid, stamps, flags, vec, gvec2, ghid, *pieces)


def unpack_kernel(sizes, gtok, gin, gsmall, gfeed, gtok_o, gin_o, gtab_o, gout_o, gup_o, gdown_o, *refs):
    *vecs, held, there, back = refs
    parts = there.shape[0]
    rows = gtok.shape[0] // parts
    spans = [pl.ds(rows * i, rows) for i in range(parts)]
    reads = [pltpu.make_async_copy(gtok.at[at], held.at[at], there.at[i]) for i, at in enumerate(spans)]
    writes = [pltpu.make_async_copy(held.at[at], gtok_o.at[at], back.at[i]) for i, at in enumerate(spans)]
    for copy in reads:
        copy.start()
    for i in range(parts):
        reads[i].wait()
        writes[i].start()
        if i == 0:
            unpack_rest(sizes, gin, gsmall, gfeed, gin_o, gtab_o, gout_o, gup_o, gdown_o, *vecs)
    for copy in writes:
        copy.wait()


def unpack_rest(sizes, gin, gsmall, gfeed, gin_o, gtab_o, gout_o, gup_o, gdown_o, *vecs):
    width = gtab_o.shape[1]
    half = width // 2
    gin_o[...] = gin[...]
    gtab_o[:, :half] = gsmall[:8, :half]
    gtab_o[:, half:] = gsmall[8:, :half]
    row = jnp.concatenate([gsmall[0:1, half:], gsmall[1:2, half:]], 1)
    gdown_o[...] = gfeed[:64, :]
    for i in range(gup_o.shape[1] // width):
        gup_o[:, width * i : width * (i + 1)] = gfeed[64 + 16 * i : 80 + 16 * i, :]
    gout_o[...] = gfeed[128:144, :]
    at = 0
    for ref, size in zip(vecs, sizes):
        ref[...] = row[:, at : at + size]
        at += size


def unpack(gtok, gin, gsmall, gfeed, hidden, sizes):
    width = gfeed.shape[1]
    shapes = [gtok.shape, gin.shape, (8, width), (16, width), (16, hidden), (64, width)] + [(1, n) for n in sizes]
    anywhere = pl.BlockSpec(memory_space=pl.ANY)
    inside = pl.BlockSpec(memory_space=pltpu.VMEM)
    parts = 8
    return pl.pallas_call(
        functools.partial(unpack_kernel, sizes),
        in_specs=[anywhere] + [inside] * 3,
        out_specs=[anywhere] + [inside] * (len(shapes) - 1),
        out_shape=[jax.ShapeDtypeStruct(s, F32) for s in shapes],
        scratch_shapes=[pltpu.VMEM(gtok.shape, F32), pltpu.SemaphoreType.DMA((parts,)), pltpu.SemaphoreType.DMA((parts,))],
        compiler_params=params(),
        name="unpack",
    )(gtok, gin, gsmall, gfeed)


def exchange_plane(arrays):
    out = [arrays[0]]
    for array, (dx, dy) in zip(arrays[1:], ((1, 0), (0, 1), (1, 1))):
        pairs = [(4 * dp + fs, 4 * (dp ^ dx) + (fs ^ (2 * dy))) for dp in range(8) for fs in range(4)]
        out.append(lax.ppermute(array, AXES, pairs))
    return out


def per_device(fast, tokens, mask_flags, timesteps, segment_ids, mask_embed, time_table, first_gain, first_bias,
               input_proj, output_proj, output_bias, second_gain, second_bias, hidden_weight, hidden_bias,
               down_weight, down_bias, cotangent):
    count, width = tokens.shape
    hidden = hidden_weight.shape[1]
    vectors = (mask_embed, first_gain, first_bias, output_bias, second_gain, second_bias, down_bias)
    segments = segment_ids.reshape(-1)
    stamps, flags = timesteps[None], mask_flags[None]
    if fast:
        lines = [v[None] for v in vectors + (hidden_bias,)]
        sizes = [v.shape[1] for v in lines]
        shards = lines + [time_table, input_proj, output_proj, hidden_weight, down_weight]
        *kept, w_in, w_out, own = enter(tokens, segments, stamps, flags, hidden, shards, None, None)
        w_in, w_out = w_in.reshape(3, width, width), w_out.reshape(width, width)
        steps = time_table.shape[0] * 32
        weights = exchange_plane([own] * 4)
    else:
        whole = lambda a: lax.all_gather(a, AXES, axis=0, tiled=True)
        groups = whole(time_table).reshape(-1, 8, width)
        pieces = jnp.concatenate(
            [whole(v).reshape(groups.shape[0], -1) for v in vectors + (hidden_bias,)], 1
        )
        pieces = jnp.pad(pieces, ((0, 0), (0, 2 * SIDE - pieces.shape[1])))[:, None]
        small = pack_block(groups.astype(F32), pieces.astype(F32)).astype(BF16)
        w_in, w_out = whole(input_proj), whole(output_proj)
        weights = [whole(hidden_weight), whole(down_weight)]
        steps = groups.shape[0] * 8
        kept = enter(tokens, segments, stamps, flags, hidden, None, small, w_in)
        w_in = w_in.reshape(width, 3, width).transpose(1, 0, 2)
    start, normt, packed, mq, mk, vec, hid, cuts = kept

    mixture, lse = attention_forward(packed, cuts, mq, mk, 256, 4)
    out, gmid, dmix, delta, gvec2, ghid, *grads = feed(cuts, start, mixture, cotangent, w_out, vec, hid, weights, fast)
    pieces = exchange_plane(grads) if fast else []
    dq, dk, dv, out = attention_backward(packed, dmix, cuts, mq, mk, lse, delta, out, 256, 4)
    gtok, gin, *rest = leave(
        cuts, dq, dk, dv, normt, w_in, start, gmid, stamps, flags, vec, gvec2, ghid, steps, pieces, fast
    )
    if fast:
        gtok, gin, gtab, gout, gup, gdown, *small = unpack(gtok, gin, rest[0], rest[1], hidden, sizes)
        gmask, gg1, gb1, gob, gg2, gb2, gdb, ghb = [v.reshape(-1) for v in small]
    else:
        total = lambda a: lax.psum_scatter(a.astype(F32), AXES, scatter_dimension=0, tiled=True)
        gtab, gvec1 = rest
        gup, gdown, gout = grads
        gin, gout, gup, gdown = (total(a) for a in (gin, gout, gup, gdown))
        gmask = total(gtab[steps])
        gtab = total(gtab[:steps])
        gg1, gb1, gob, gg2, gb2, gdb, ghb = (
            total(a) for a in (gvec1[0], gvec1[1], gvec2[0], gvec2[1], gvec2[2], gvec2[3], ghid[0])
        )
    return (out, gtok, gmask, gtab, gg1, gb1, gin, gout, gob, gg2, gb2, gup, ghb, gdown, gdb)


def solution(mesh):
    split = P(AXES)
    rows = P(AXES, None)
    fast = tuple(mesh.shape[a] for a in AXES) == (8, 4)
    placed = (rows, split, split, rows, split, rows, split, split, rows, rows, split, split, split, rows, split, rows,
              split, rows)
    return jax.shard_map(
        functools.partial(per_device, fast),
        mesh=mesh,
        in_specs=placed,
        out_specs=(rows, rows, split, rows, split, split, rows, rows, split, split, split, rows, split, rows, split),
        check_vma=False,
    )
```

```python
import functools

import jax
import jax.numpy as jnp
from jax import lax
from jax.experimental import pallas as pl
from jax.experimental.pallas import tpu as pltpu
from jax.sharding import PartitionSpec as P

F32, BF16 = jnp.float32, jnp.bfloat16
HD = 64
SEGMENTS = 4
SCALE = HD ** -0.5
NEG = -1e30
EPSILON = 1e-05
AXES = ("dp", "fsdp")
MESH = pl.DeviceIdType.MESH
VMEM_BYTES = 58 << 20
TILE = 512


def dot(a, b):
    return jnp.dot(a, b, preferred_element_type=F32)


def dot_nt(a, b):
    return lax.dot_general(a, b, (((1,), (1,)), ((), ())), preferred_element_type=F32)


def dot_tn(a, b):
    return lax.dot_general(a, b, (((0,), (0,)), ((), ())), preferred_element_type=F32)


def iota(shape, dim):
    return lax.broadcasted_iota(jnp.int32, shape, dim)


def params(room=VMEM_BYTES, **more):
    return pltpu.CompilerParams(vmem_limit_bytes=room, **more)


def norm_parts(h):
    centered = h - jnp.mean(h, axis=-1, keepdims=True)
    rstd = lax.rsqrt(jnp.mean(centered * centered, axis=-1, keepdims=True) + EPSILON)
    return centered * rstd, rstd


def norm_back(n, xhat, rstd, gain):
    ng = n * gain
    first = jnp.mean(ng, axis=-1, keepdims=True)
    second = jnp.mean(ng * xhat, axis=-1, keepdims=True)
    return rstd * (ng - first - xhat * second)


def position():
    dp, fs = lax.axis_index("dp"), lax.axis_index("fsdp")
    return dp // 2, dp % 2, fs // 2, fs % 2


def device(z, x, y, c):
    return (z * 2 + x, y * 2 + c)


def peer(z, k):
    return lax.rem(z + k, 4)


def greet(z, x, y, c):
    barrier = pltpu.get_barrier_semaphore()
    partners = [device(peer(z, k), x, y, c) for k in (1, 2, 3)]
    partners += [device(z, xs, ys, c) for xs, ys in plane(x, y)[1:]] + [device(z, x, y, 1 - c)]
    for partner in partners:
        pl.semaphore_signal(barrier, inc=1, device_id=partner, device_id_type=MESH)
    pl.semaphore_wait(barrier, len(partners))


def remote(src, dst, send, recv, target):
    return pltpu.make_async_remote_copy(
        src_ref=src, dst_ref=dst, send_sem=send, recv_sem=recv, device_id=target, device_id_type=MESH
    )


def plane(x, y):
    return ((x, y), (1 - x, y), (x, 1 - y), (1 - x, 1 - y))


def gather_plan(place, shard, whole, send, recv, local):
    z, x, y, c = place
    spots = plane(x, y)
    level = lambda k: peer(z, 4 - k)

    def copy(slot):
        if slot < 4 and slot:
            src, dst, to = shard, whole.at[z, x, y, c], device(peer(z, slot), x, y, c)
        elif 4 <= slot < 16:
            k = slot % 4
            dst, to = whole.at[level(k), x, y, c], device(z, *spots[slot // 4], c)
            src = dst if k else shard
        else:
            xs, ys = spots[max(slot - 15, 0)]
            src = dst = whole.at[:, xs, ys, c]
            to = device(z, x, y, 1 - c)
        return remote(src, dst, send.at[slot], recv.at[slot], to)

    keep = pltpu.make_async_copy(shard, whole.at[z, x, y, c], local)

    def begin():
        keep.start()
        for k in (1, 2, 3):
            copy(k).start()

    def spread():
        for k in range(4):
            if k:
                copy(k).wait_recv()
            for kind in (4, 8, 12):
                copy(kind + k).start()
        keep.wait()
        copy(0).start()

    def finish():
        for i in range(3):
            for k in range(4):
                copy(4 + 4 * i + k).wait_recv()
            copy(16 + i).start()

    def ready():
        for slot in (0, 16, 17, 18):
            copy(slot).wait_recv()

    def drain():
        for slot in range(GATHER_SLOTS):
            copy(slot).wait_send()

    return begin, spread, finish, ready, drain


GATHER_SLOTS = 19


def scatter_plan(place, full, own, got, land, last, send, recv):
    z, x, y, c = place
    spots = plane(x, y)

    def copy(slot):
        if slot == 0:
            src, dst, to = full.at[:, :, :, 1 - c], got, device(z, x, y, 1 - c)
        elif slot < 4:
            xs, ys = spots[slot]
            src, dst, to = own.at[:, xs, ys], land.at[slot - 1], device(z, xs, ys, c)
        else:
            k = slot - 3
            src, dst, to = got.at[peer(z, k), 0, 0], last.at[k - 1], device(peer(z, k), x, y, c)
        return remote(src, dst, send.at[slot], recv.at[slot], to)

    def to_sibling():
        copy(0).start()

    def to_plane():
        copy(0).wait_recv()
        for i in range(4):
            own[i] = (full[i, :, :, c].astype(F32) + got[i].astype(F32)).astype(BF16)
        for slot in (1, 2, 3):
            copy(slot).start()

    def to_levels():
        for slot in (1, 2, 3):
            copy(slot).wait_recv()
        for i in range(4):
            parts = [own[i, x, y]] + [land[j, i] for j in range(3)]
            parts = [p.astype(F32) for p in parts]
            got[i, 0, 0] = (parts[0] + parts[1] + parts[2] + parts[3]).astype(BF16)
        for slot in (4, 5, 6):
            copy(slot).start()

    def total(out, at):
        for slot in (4, 5, 6):
            copy(slot).wait_recv()
        rest = last[0].astype(F32) + last[1].astype(F32) + last[2].astype(F32)
        out[:, at : at + rest.shape[1]] = got[z, 0, 0].astype(F32) + rest

    def drain():
        for slot in range(SCATTER_SLOTS):
            copy(slot).wait_send()

    return to_sibling, to_plane, to_levels, total, drain


SCATTER_SLOTS = 7


def scatter_buffers(rows, width):
    return [pltpu.VMEM(s, BF16) for s in (
        (4, 2, 2, 2, rows, width), (4, 2, 2, rows, width), (4, 2, 2, rows, width), (3, 4, rows, width),
        (3, rows, width))]


def find_cuts(seg, length, cuts):
    def first_at_least(s):
        def step(_, span):
            lo, hi = span
            mid = (lo + hi) // 2
            below = seg[jnp.minimum(mid, length - 1)] < s
            live = lo < hi
            return jnp.where(live & below, mid + 1, lo), jnp.where(live & jnp.logical_not(below), mid, hi)

        return lax.fori_loop(0, length.bit_length(), step, (jnp.int32(0), jnp.int32(length)))[0]

    edges = [jnp.int32(0)] + [first_at_least(s) for s in range(1, SEGMENTS)] + [jnp.int32(length)]
    sizes = [edges[i + 1] - edges[i] for i in range(SEGMENTS)]
    roll, most = edges[0], sizes[0]
    for edge, size in zip(edges[1:], sizes[1:]):
        roll = jnp.where(size > most, edge, roll)
        most = jnp.maximum(size, most)
    cuts[0] = roll
    firsts = []
    for i in range(SEGMENTS):
        at = edges[i] - roll
        firsts.append(jnp.where(at < 0, at + length, at))
        cuts[1 + i] = firsts[i]
        cuts[1 + SEGMENTS + i] = sizes[i]
    return roll, firsts, sizes


def turned(ref, first, rows):
    length = ref.shape[1] - rows
    at = jnp.where(first >= length, first - length, first)
    at = jnp.where(at < 0, at + length, at)
    return jnp.concatenate([ref[i, pl.ds(at, rows), :] for i in range(ref.shape[0])], 1)


def put_columns(ref, at, value):
    for i in range(ref.shape[0]):
        ref[i, at, :] = value[:, 128 * i : 128 * i + 128]


def wrap_columns(ref, rows):
    length = ref.shape[1] - rows
    for i in range(ref.shape[0]):
        ref[i, length:, :] = ref[i, :rows, :]


def enter_kernel(linked, seg, tok, stamps, flags, *refs):
    if linked:
        vectors, stamps_table, s_in, s_out, s_up, s_down = refs[:8], *refs[8:13]
        refs = refs[13:]
        (start_o, normt_o, packed_o, mq_o, mk_o, vec_o, hid_o, cuts, win_o, wout_o, feed_o,
         s_small, small, w_in, send, recv, local, fsend, frecv, flocal) = refs[:20]
        refs = refs[20:]
    else:
        small, w_in, start_o, normt_o, packed_o, mq_o, mk_o, vec_o, hid_o, cuts = refs[:10]
        refs = refs[10:]
    tokv, startf, startv, normv, normtv, packv, mqv, mkv, table, moved, tsem = refs
    count, width = tok.shape
    rows = min(TILE, count)
    tiles = count // rows
    fetch = pltpu.make_async_copy(tok, tokv, moved.at[0])
    fetch.start()
    if linked:
        place = position()
        z, x, y, c = place
        greet(*place)
        row = jnp.zeros((1, width), F32)
        at = 0
        for v in vectors:
            size = v.shape[1]
            row = row + dot(v[...], (iota((size, width), 1) == iota((size, width), 0) + at).astype(BF16))
            at += size
        s_small[...] = pack_block(stamps_table[...].astype(F32), row[:, : 2 * SIDE]).astype(BF16)
        plans = [
            gather_plan(place, s, w, send.at[a], recv.at[a], local.at[a])
            for a, (s, w) in enumerate(
                [(s_small, small)]
                + [(s_in.at[:, width * i : width * i + width], w_in.at[i]) for i in range(3)]
                + [(s_out, wout_o)]
            )
        ]
        first, *middle, final = plans
        parts = [(s_down, 0, 64)] + [(s_up.at[:, width * j : width * j + width], 64 + 16 * j, 16) for j in range(4)]

        def feed_copy(j, k):
            src, at, size = parts[j]
            dst = feed_o.at[z, at : at + size, :]
            if k == 0:
                return pltpu.make_async_copy(src, dst, flocal.at[j])
            return remote(src, dst, fsend.at[j, k - 1], frecv.at[j, k - 1], device(peer(z, k), x, y, c))

        feeds = [feed_copy(j, k) for j in range(5) for k in range(4)]
        for plan in plans[:4]:
            plan[0]()
    roll, firsts, sizes = find_cuts(seg, count, cuts)
    if linked:
        for plan in plans[:4]:
            plan[1]()
        final[0]()
        for copy in feeds:
            copy.start()
        first[2]()
        first[3]()
    unpack_small(small[...].reshape((-1,) + small.shape[-2:]), vec_o, hid_o, table)
    fetch.wait()
    moves = []

    def move(src, dst):
        copy = pltpu.make_async_copy(src, dst, moved.at[len(moves) + 1])
        copy.start()
        moves.append(copy)

    def rows_at(t):
        return pl.ds(t * rows if isinstance(t, int) else pl.multiple_of(t * rows, rows), rows)

    def start_tile(t, _):
        at = rows_at(t)
        select = token_selector(stamps[:, at], flags[:, at], table.shape[0] - 16)
        put_columns(startf, at, tokv[at, :].astype(F32) + dot_tn(select, table[...]))
        return 0

    lax.fori_loop(0, tiles, start_tile, 0)
    wrap_columns(startf, rows)
    lane = iota((1, 128), 1)
    lows, highs = jnp.zeros((1, 128), jnp.int32), jnp.zeros((1, 128), jnp.int32)
    for i in range(SEGMENTS):
        lows = jnp.where(lane == i, firsts[i], lows)
        highs = jnp.where(lane == i, firsts[i] + sizes[i], highs)
    if linked:
        final[1]()
    def save(t):
        return pltpu.make_async_copy(startv.at[rows_at(t)], start_o.at[rows_at(t)], tsem.at[t])

    def norm_tile(t, _):
        at = rows_at(t)
        start = turned(startf, roll + rows * t, rows)
        startv[at, :] = start
        save(t).start()
        xhat, _ = norm_parts(start)
        normed = (xhat * vec_o[1:2, :] + vec_o[2:3, :]).astype(BF16)
        normv[at, :] = normed
        normtv[:, at] = jnp.transpose(normed, (1, 0))
        row = iota((rows, 128), 0) + rows * t
        member = (row >= lows) & (row < highs)
        mqv[at, :] = jnp.where(member, 1.0, 0.0).astype(BF16)
        mkv[at, :] = jnp.where(member | (lane >= SEGMENTS), 0.0, NEG).astype(BF16)
        return 0

    lax.fori_loop(0, tiles, norm_tile, 0)
    if linked:
        middle[0][2]()
    move(normtv, normt_o)
    move(mqv, mq_o)
    move(mkv, mk_o)
    for i in range(3):
        cols = slice(width * i, width * i + width)
        if linked:
            middle[i][3]()
            weights = w_in[i].reshape(width, width)
            if i < 2:
                middle[i + 1][2]()
            else:
                final[2]()
        else:
            weights = w_in[:, cols]
        scale = SCALE if i == 0 else 1.0

        def project(t, _):
            at = rows_at(t)
            packv[at, cols] = (dot(normv[at, :], weights) * scale).astype(BF16)
            return 0

        for t in range(tiles):
            project(t, 0)
        move(packv.at[:, cols], packed_o.at[:, cols])
    if linked:
        move(w_in, win_o)
    for copy in moves:
        copy.wait()
    for t in range(tiles):
        save(t).wait()
    if linked:
        final[3]()
        for plan in plans:
            plan[4]()
        for copy in feeds:
            copy.wait()


SIDE = 128


def pack_block(table, row):
    half = table.shape[-1] // 2
    left = jnp.concatenate([table[..., :half], table[..., half:]], -2)
    lines = jnp.concatenate([row[..., :SIDE], row[..., SIDE:]], -2)
    empty = jnp.zeros(left.shape[:-2] + (left.shape[-2] - 2, SIDE), F32)
    return jnp.concatenate([left, jnp.concatenate([lines, empty], -2)], -1)


def unpack_small(flat16, vec_o, hid_o, table):
    devices = flat16.shape[0]
    width = vec_o.shape[1]
    steps = devices * 8
    flat = flat16.astype(F32)
    half = width // 2
    row = jnp.concatenate([flat[:, 0, half:], flat[:, 1, half:]], 1).astype(BF16)
    per = width // devices
    lane = iota(row.shape, 1)
    spread = jnp.concatenate([jnp.where(lane // per == i, row, jnp.zeros_like(row)) for i in range(7)], 0)
    same = (iota((2 * SIDE, width), 0) % per == iota((2 * SIDE, width), 1) % per).astype(BF16)
    wide = dot(spread, same).reshape(7, devices, width)
    mine = (iota((devices, width), 1) // per == iota((devices, width), 0))[None]
    vecs = jnp.sum(jnp.where(mine, wide, 0.0), axis=1)
    vec_o[...] = jnp.concatenate([vecs, jnp.zeros((1, width), F32)], 0)
    hidden = hid_o.shape[1]
    part = hidden // devices
    at = iota((2 * SIDE, hidden), 0) - 7 * per
    pick = (at == iota((2 * SIDE, hidden), 1) % part).astype(BF16)
    own = iota((devices, hidden), 1) // part == iota((devices, hidden), 0)
    hid_o[...] = jnp.sum(jnp.where(own, dot(row, pick), 0.0), axis=0, keepdims=True)
    entries = jnp.concatenate([flat[:, :8, :half], flat[:, 8:, :half]], 2)
    table[:steps, :] = entries.reshape(steps, width).astype(BF16)
    table[steps:, :] = jnp.where(iota((16, width), 0) == 0, vecs[0:1], 0.0).astype(BF16)


def token_selector(stamps, flags, steps):
    rows = stamps.shape[1]
    chosen = (stamps == iota((steps, rows), 0)).astype(F32)
    flagged = jnp.where(iota((16, rows), 0) == 0, flags.astype(F32), 0.0)
    return jnp.concatenate([chosen, flagged], 0).astype(BF16)


def enter(tokens, segments, stamps, flags, hidden, shards, small, w_in):
    count, width = tokens.shape
    linked = shards is not None
    rows = min(TILE, count)
    tiles = count // rows
    anywhere = pl.BlockSpec(memory_space=pl.ANY)
    inside = pl.BlockSpec(memory_space=pltpu.VMEM)
    scalars = pl.BlockSpec(memory_space=pltpu.SMEM)
    lot = lambda *s: pltpu.SemaphoreType.DMA(s)
    big = lambda w, d: pltpu.VMEM((count, w), d)
    full = lambda a: (4, 2, 2, 2) + a
    outs = [
        jax.ShapeDtypeStruct((count, width), F32),
        jax.ShapeDtypeStruct((width, count), BF16),
        jax.ShapeDtypeStruct((count, 3 * width), BF16),
        jax.ShapeDtypeStruct((count, 128), BF16),
        jax.ShapeDtypeStruct((count, 128), BF16),
        jax.ShapeDtypeStruct((8, width), F32),
        jax.ShapeDtypeStruct((1, hidden), F32),
        jax.ShapeDtypeStruct((16,), jnp.int32),
    ]
    out_specs = [anywhere] * 5 + [inside] * 2 + [scalars]
    if linked:
        *vectors, stamps_table, s_in, s_out, s_up, s_down = shards
        operands = shards
        in_specs = [inside] * 9 + [anywhere] * 4
        outs += [
            jax.ShapeDtypeStruct((3,) + full(s_out.shape), BF16),
            jax.ShapeDtypeStruct(full(s_out.shape), BF16),
            jax.ShapeDtypeStruct((4, s_down.shape[0] + 64, width), BF16),
        ]
        out_specs += [anywhere] * 3
        scratch = [
            pltpu.VMEM((16, width // 2 + SIDE), BF16), pltpu.VMEM(full((16, width // 2 + SIDE)), BF16),
            pltpu.VMEM((3,) + full(s_out.shape), BF16),
            lot(5, GATHER_SLOTS), lot(5, GATHER_SLOTS), lot(5), lot(5, 3), lot(5, 3), lot(5),
        ]
        steps = 256
        compiler = params(collective_id=0, has_side_effects=True)
    else:
        operands, in_specs, scratch = [small, w_in], [inside] * 2, []
        steps = small.shape[0] * 8
        compiler = params()
    outs = pl.pallas_call(
        functools.partial(enter_kernel, linked),
        in_specs=[scalars, anywhere, inside, inside] + in_specs,
        out_specs=out_specs,
        out_shape=outs,
        scratch_shapes=scratch + [
            big(width, BF16), pltpu.VMEM((width // 128, count + rows, 128), F32), big(width, F32), big(width, BF16),
            pltpu.VMEM((width, count), BF16), big(3 * width, BF16), big(128, BF16), big(128, BF16),
            pltpu.VMEM((steps + 16, width), BF16), lot(16), lot(tiles),
        ],
        compiler_params=compiler,
        name="enter",
    )(segments, tokens, stamps, flags, *operands)
    return list(outs)


def key_range(cuts, row, rows):
    lo, hi = jnp.int32(1 << 20), jnp.int32(0)
    for i in range(SEGMENTS):
        first, size = cuts[1 + i], cuts[1 + SEGMENTS + i]
        meets = (size > 0) & (first < row + rows) & (first + size > row)
        lo = jnp.where(meets, jnp.minimum(lo, first), lo)
        hi = jnp.where(meets, jnp.maximum(hi, first + size), hi)
    return lo, hi


def list_tiles(cuts, length, tile, qi, ki):
    blank = length // tile

    def one(t, n):
        lo, hi = key_range(cuts, t * tile, tile)

        def put(j, n):
            qi[n], ki[n] = t, j
            return n + 1

        return lax.fori_loop(lo // tile, (hi + tile - 1) // tile, put, n)

    n = lax.fori_loop(0, blank, one, jnp.int32(1))
    for i in range(2):
        qi[n + i], ki[n + i] = jnp.int32(blank), jnp.int32(blank)
    return n // 2


def spots(qi, ki, i, tile, length):
    q, k = pl.multiple_of(qi[i] * tile, tile), pl.multiple_of(ki[i] * tile, tile)
    q_in, k_in = (pl.multiple_of(jnp.where(v >= length, 0, v), tile) for v in (q, k))
    return pl.ds(q_in, tile), pl.ds(k_in, tile), pl.ds(q, tile), pl.ds(k, tile)


def head_masks():
    first = iota((1, 128), 1) < HD
    return [jnp.where(first == (h == 0), 1.0, 0.0).astype(BF16) for h in range(2)]


def fwd_kernel(length, tile, npair, cuts, q_ref, k_ref, v_ref, mq_ref, mk_ref, o_ref, lse_ref,
               vt, acc, top, alpha, ps, qi, ki):
    g = pl.program_id(0)
    heads = 2 * npair
    only = head_masks()
    ones = jnp.ones((16, tile), BF16)
    count = list_tiles(cuts, length, tile, qi, ki)
    vt[...] = jnp.transpose(v_ref[...], (1, 0))
    acc[...] = jnp.zeros_like(acc)
    top[...] = jnp.full_like(top, -3e38)

    def scan(i, slot, hs):
        q_in, k_in, q, _ = spots(qi, ki, i, tile, length)
        for h in hs:
            cols = slice(128 * (h // 2), 128 * (h // 2) + 128)
            s = dot_nt(jnp.concatenate([k_ref[k_in, cols], mk_ref[k_in, :]], 1),
                       jnp.concatenate([q_ref[q_in, cols] * only[h % 2], mq_ref[q_in, :]], 1))
            old = top[h : h + 1, q]
            new = jnp.maximum(old, jnp.max(s, axis=0, keepdims=True))
            top[h : h + 1, q] = new
            alpha[slot, h : h + 1] = jnp.exp(old - new)
            ps[slot, h] = jnp.exp(s - new).astype(BF16)

    def mix(i, slot, hs):
        _, k_in, q, _ = spots(qi, ki, i, tile, length)
        for h in hs:
            values = jnp.concatenate([vt[HD * h : HD * h + HD, k_in], ones], 0)
            acc[h, :, q] = acc[h, :, q] * alpha[slot, h : h + 1] + dot(values, ps[slot, h])

    def step(m, _):
        def both(a, sa, b, sb):
            for h in range(heads):
                mix(a, sa, [h])
                scan(b, sb, [h])

        both(2 * m + 1, 0, 2 * m + 2, 1)
        both(2 * m + 2, 1, 2 * m + 3, 0)
        return 0

    scan(1, 0, range(heads))
    lax.fori_loop(0, count, step, 0)
    for i in range(npair):
        both = []
        for h in (2 * i, 2 * i + 1):
            total = acc[h, HD : HD + 1, :length]
            both.append(acc[h, :HD, :length] / total)
            lse_ref[pl.ds(heads * g + h, 1), :] = top[h : h + 1, :length] + jnp.log(total)
        o_ref[:, 128 * i : 128 * i + 128] = jnp.transpose(jnp.concatenate(both, 0), (1, 0)).astype(BF16)


def attention_forward(packed, cuts, mq, mk, tile, npair):
    length = packed.shape[0]
    steps = 4 // npair
    w, heads = 128 * npair, 2 * npair
    most = (length // tile) ** 2 + 8
    col = lambda o: pl.BlockSpec((length, w), lambda g, s: (0, g + o * steps))
    whole = pl.BlockSpec((length, 128), lambda g, s: (0, 0))
    return pl.pallas_call(
        functools.partial(fwd_kernel, length, tile, npair),
        grid_spec=pltpu.PrefetchScalarGridSpec(
            num_scalar_prefetch=1, grid=(steps,),
            in_specs=[col(0), col(1), col(2), whole, whole],
            out_specs=[col(0), pl.BlockSpec((8, length), lambda g, s: (0, 0))],
            scratch_shapes=[
                pltpu.VMEM((w, length), BF16),
                pltpu.VMEM((heads, HD + 16, length + tile), F32),
                pltpu.VMEM((8, length + tile), F32),
                pltpu.VMEM((2, 8, tile), F32),
                pltpu.VMEM((2, heads, tile, tile), BF16),
                pltpu.SMEM((most,), jnp.int32),
                pltpu.SMEM((most,), jnp.int32),
            ]),
        out_shape=[jax.ShapeDtypeStruct((length, 512), BF16), jax.ShapeDtypeStruct((8, length), F32)],
        compiler_params=params(63 << 20),
        name="attend_forward",
    )(cuts, packed, packed, packed, mq, mk)


def bwd_kernel(length, tile, npair, cuts, q_ref, k_ref, v_ref, do_ref, mq_ref, mk_ref, lse_ref, delta_ref,
               out_ref, dq_ref, dk_ref, dv_ref, out_again, kt, dk, dv, dqt, ps, dss, qi, ki):
    g = pl.program_id(0)
    heads = 2 * npair
    out_again[...] = out_ref[...]
    only = head_masks()
    count = list_tiles(cuts, length, tile, qi, ki)
    kt[...] = jnp.transpose(k_ref[...], (1, 0))
    for ref in (dk, dv, dqt):
        ref[...] = jnp.zeros_like(ref)

    def scan(i, slot):
        q_in, k_in, _, _ = spots(qi, ki, i, tile, length)
        for h in range(heads):
            at = slice(128 * (h // 2), 128 * (h // 2) + 128)
            lse = lse_ref[pl.ds(heads * g + h, 1), q_in]
            delta = delta_ref[pl.ds(heads * g + h, 1), q_in]
            s = dot_nt(jnp.concatenate([k_ref[k_in, at], mk_ref[k_in, :]], 1),
                       jnp.concatenate([q_ref[q_in, at] * only[h % 2], mq_ref[q_in, :]], 1))
            p = jnp.exp(s - lse)
            dp = dot_nt(v_ref[k_in, at], do_ref[q_in, at] * only[h % 2])
            cols = slice(tile * (h % 2), tile * (h % 2) + tile)
            ps[slot, h // 2, :, cols] = p.astype(BF16)
            dss[slot, h // 2, :, cols] = (p * (dp - delta)).astype(BF16)

    def mix(i, slot):
        q_in, k_in, q, k = spots(qi, ki, i, tile, length)
        for i in range(npair):
            at = slice(128 * i, 128 * i + 128)
            part = do_ref[q_in, at]
            dv[i, k, :] += dot(ps[slot, i], jnp.concatenate([part * only[0], part * only[1]], 0))
            part = q_ref[q_in, at]
            dk[i, k, :] += dot(dss[slot, i], jnp.concatenate([part * only[0], part * only[1]], 0))
            for h in (2 * i, 2 * i + 1):
                rows = slice(HD * h, HD * h + HD)
                cols = slice(tile * (h % 2), tile * (h % 2) + tile)
                dqt[rows, q] += dot(kt[rows, k_in], dss[slot, i, :, cols])

    def step(m, _):
        scan(2 * m + 2, 1)
        mix(2 * m + 1, 0)
        scan(2 * m + 3, 0)
        mix(2 * m + 2, 1)
        return 0

    scan(1, 0)
    lax.fori_loop(0, count, step, 0)
    for i in range(npair):
        cols = slice(128 * i, 128 * i + 128)
        dk_ref[:, cols] = dk[i, :length].astype(BF16)
        dv_ref[:, cols] = dv[i, :length].astype(BF16)
        dq_ref[:, cols] = jnp.transpose(dqt[cols, :length] * SCALE, (1, 0)).astype(BF16)


def attention_backward(packed, dmix, cuts, mq, mk, lse, delta, out, tile, npair):
    length = packed.shape[0]
    steps = 4 // npair
    w, heads = 128 * npair, 2 * npair
    most = (length // tile) ** 2 + 8
    col = lambda o: pl.BlockSpec((length, w), lambda g, s: (0, g + o * steps))
    whole = pl.BlockSpec((length, 128), lambda g, s: (0, 0))
    rowspec = pl.BlockSpec((8, length), lambda g, s: (0, 0))
    return pl.pallas_call(
        functools.partial(bwd_kernel, length, tile, npair),
        grid_spec=pltpu.PrefetchScalarGridSpec(
            num_scalar_prefetch=1, grid=(steps,),
            in_specs=[col(0), col(1), col(2), col(0), whole, whole, rowspec, rowspec, col(0)],
            out_specs=[col(0)] * 4,
            scratch_shapes=[
                pltpu.VMEM((w, length), BF16),
                pltpu.VMEM((npair, length + tile, 128), F32),
                pltpu.VMEM((npair, length + tile, 128), F32),
                pltpu.VMEM((w, length + tile), F32),
                pltpu.VMEM((2, npair, tile, 2 * tile), BF16),
                pltpu.VMEM((2, npair, tile, 2 * tile), BF16),
                pltpu.SMEM((most,), jnp.int32),
                pltpu.SMEM((most,), jnp.int32),
            ]),
        out_shape=[jax.ShapeDtypeStruct((length, 512), BF16)] * 3 + [jax.ShapeDtypeStruct(out.shape, out.dtype)],
        compiler_params=params(63 << 20),
        name="attend_backward",
    )(cuts, packed, packed, packed, dmix, mq, mk, lse, delta, out)


def gelu_parts(v):
    phi = 0.5 * lax.erf(v * 0.7071067811865476) + 0.5
    return v * phi, phi + v * jnp.exp2(v * v * -0.7213475204444817 - 1.3257480647361593)


def feed_kernel(linked, rows, f, cuts, start, mix, cot, w_out, vec, hid, *refs):
    if linked:
        lands = refs[:4]
        out_o, gmid_o, dmix_o, delta_o, gvec_o, ghid_o = refs[4:10]
        leaves = refs[10:14]
        refs = refs[14:]
    else:
        up_all, down_all = refs[:2]
        out_o, gmid_o, dmix_o, delta_o, gvec_o, ghid_o, gup_o, gdown_o, gout_o = refs[2:11]
        refs = refs[11:]
    (mid, res, gn2, n2, n2t, br, brt, mixv, projv, act0, act1, gpre0, gpre1, gup, gdt, gout, cotf, rsv,
     csem, tsem, osem) = refs[:21]
    count, width = mid.shape
    hidden = gup.shape[1]
    tiles, chunks = count // rows, hidden // f
    half = tiles // 2
    roll = cuts[0]
    spans = [slice(rows * t, rows * t + rows) for t in range(tiles)]
    loads = [pltpu.make_async_copy(w_out, projv, tsem.at[2 * tiles])]
    for t, at in enumerate(spans):
        pltpu.make_async_copy(mix.at[at], mixv.at[at], tsem.at[2 * t]).start()
        pltpu.make_async_copy(start.at[at], mid.at[at], tsem.at[2 * t + 1]).start()
    for i in range(width // 128):
        cols = pl.ds(128 * i, 128)
        loads.append(pltpu.make_async_copy(cot.at[:, cols], cotf.at[i, pl.ds(0, count), :], csem.at[i, 0]))
        loads.append(pltpu.make_async_copy(cot.at[pl.ds(0, rows), cols], cotf.at[i, pl.ds(count, rows), :], csem.at[i, 1]))
    for copy in loads:
        copy.start()

    def rows_at(t):
        return pl.ds(t * rows if isinstance(t, int) else pl.multiple_of(t * rows, rows), rows)

    if linked:
        up, down, sent, kept, got, lsem, lsend, lrecv, esend, erecv, eout = refs[21:]
        place = position()
        z, x, y, c = place
        sibling = device(z, x, y, 1 - c)

        def arrive(i, j, kind):
            xs, ys = plane(x, y)[i]
            if j == 0:
                src, dst = lands[i].at[:, :64, :], down.at[:, xs, ys, c]
            else:
                src = lands[i].at[:, 48 + 16 * j : 64 + 16 * j, :]
                dst = up.at[:, xs, ys, c, :, width * (j - 1) : width * j]
            if kind == 0:
                return pltpu.make_async_copy(src, dst, lsem.at[i, j])
            return remote(src, dst, lsend.at[i, j], lrecv.at[i, j], sibling)

        arrivals = [arrive(i, j, kind) for i in range(4) for j in range(5) for kind in range(2)]

        def exchange(j):
            at = slice(0, 128) if j == 0 else slice(128, 144)
            return remote(sent.at[:, :, :, at, :], got.at[:, :, :, at, :], esend.at[j], erecv.at[j], sibling)

        def leave(i):
            xs, ys = plane(x, y)[i]
            return pltpu.make_async_copy(got.at[:, xs, ys], leaves[i], eout.at[i])

        barrier = pltpu.get_barrier_semaphore()
        pl.semaphore_signal(barrier, inc=1, device_id=sibling, device_id_type=MESH)
        pl.semaphore_wait(barrier, 1)
        for copy in arrivals:
            copy.start()

    def cols_at(ch):
        return pl.ds(pl.multiple_of(ch * f, f), f)

    def up_chunk(ch):
        if linked:
            return up[:, :, :, :, :, cols_at(ch)].reshape(width, f)
        return up_all[:, cols_at(ch)]

    def down_chunk(ch):
        if linked:
            return down[ch].reshape(f, width)
        return down_all[cols_at(ch), :]

    for ref in (act1, gpre1, gup, gdt, gn2, gout, gvec_o):
        ref[...] = jnp.zeros_like(ref)
    loads[0].wait()

    def load_tile(t, i):
        at = rows_at(t)
        if i == 0:
            return pltpu.make_async_copy(mix.at[at], mixv.at[at], tsem.at[2 * t])
        return pltpu.make_async_copy(start.at[at], mid.at[at], tsem.at[2 * t + 1])

    def middle_tile(t, _):
        at = rows_at(t)
        load_tile(t, 0).wait()
        load_tile(t, 1).wait()
        middle = mid[at, :] + dot(mixv[at, :], projv[...]) + vec[3:4, :]
        put_columns(res, at, middle + vec[6:7, :])
        xhat, rstd = norm_parts(middle)
        mid[at, :] = xhat
        rsv[at, :] = jnp.broadcast_to(rstd, (rows, 128))
        normed = (xhat * vec[4:5, :] + vec[5:6, :]).astype(BF16)
        n2[at, :] = normed
        n2t[:width, at] = jnp.transpose(normed, (1, 0))
        n2t[width:, at] = jnp.ones((16, rows), BF16)
        return 0

    lax.fori_loop(0, tiles, middle_tile, 0)
    for copy in loads[1:]:
        copy.wait()

    def branch_tile(t, _):
        at = rows_at(t)
        branch = turned(cotf, roll + rows * t, rows).astype(BF16)
        br[at, :] = branch
        brt[:, at] = jnp.transpose(branch, (1, 0))
        gvec_o[3:4, :] += jnp.sum(branch.astype(F32), axis=0, keepdims=True)
        return 0

    lax.fori_loop(0, tiles, branch_tile, 0)
    if linked:
        for copy in arrivals:
            copy.wait()

    def inner(ch, t, act, gpre):
        cols, at = cols_at(ch), rows_at(t)
        pre = dot(n2[at, :], up_chunk(ch)) + hid[:, cols]
        grad = dot_nt(br[at, :], down_chunk(ch))
        value, slope = gelu_parts(pre)
        act[...] = value.astype(BF16)
        low = (grad * slope).astype(BF16)
        gpre[...] = low

    def outer(ch, t, act, gpre):
        cols, at = cols_at(ch), rows_at(t)
        a, g = act[...], gpre[...]
        more = dot(a, down_chunk(ch))
        for i in range(width // 128):
            res[i, at, :] += more[:, 128 * i : 128 * i + 128]
        gn2[at, :] += dot_nt(g, up_chunk(ch))
        gup[:, cols] += dot(n2t[:, at], g)
        gdt[:, cols] += dot(brt[:, at], a)

    def step(b, _):
        before = jnp.maximum(b - 1, 0)
        ch, t = b // half, 2 * (b % half)
        outer(before // half, 2 * (before % half) + 1, act1, gpre1)
        inner(ch, t, act0, gpre0)
        outer(ch, t, act0, gpre0)
        inner(ch, t + 1, act1, gpre1)
        return 0

    lax.fori_loop(0, chunks * half, step, 0)
    outer(chunks - 1, tiles - 1, act1, gpre1)
    wrap_columns(res, rows)
    ghid_o[...] = gup[width : width + 1, :]
    if linked:
        for i in range(4):
            block = jnp.transpose(gdt[:, 512 * i : 512 * i + 512], (1, 0)).reshape(2, 2, 2, 64, width)
            first, second = block[:, :, 0], block[:, :, 1]
            kept[i, :, :, :64, :] = jnp.where(c == 0, first, second).astype(BF16)
            sent[i, :, :, :64, :] = jnp.where(c == 0, second, first).astype(BF16)
            cols = slice(width * i, width * i + width)
            block = gup[:width, cols].reshape(4, 2, 2, 2, 16, width)
            first, second = block[:, :, :, 0], block[:, :, :, 1]
            at = slice(64 + 16 * i, 80 + 16 * i)
            kept[:, :, :, at, :] = jnp.where(c == 0, first, second).astype(BF16)
            sent[:, :, :, at, :] = jnp.where(c == 0, second, first).astype(BF16)
        exchange(0).start()
    else:
        for i in range(chunks):
            gup_o[:, i * f : (i + 1) * f] = gup[:width, i * f : (i + 1) * f].astype(BF16)
            gdown_o[i * f : (i + 1) * f, :] = jnp.transpose(gdt[:, i * f : (i + 1) * f], (1, 0)).astype(BF16)
    heads = (iota((16, width), 1) // HD == iota((16, width), 0)).astype(BF16)

    def move(t, i):
        at = rows_at(t)
        src, dst = ((n2, out_o), (gn2, gmid_o), (br, dmix_o))[i]
        return pltpu.make_async_copy(src.at[at], dst.at[at], osem.at[3 * t + i])

    def last_tile(t, _):
        at = rows_at(t)
        n2[at, :] = turned(res, rows * t - roll, rows).astype(BF16)
        move(t, 0).start()
        xhat, rstd = mid[at, :], jnp.concatenate([rsv[at, :]] * (width // 128), 1)
        n = gn2[at, :]
        grad = turned(cotf, roll + rows * t, rows) + norm_back(n, xhat, rstd, vec[4:5, :])
        gn2[at, :] = grad
        move(t, 1).start()
        low = grad.astype(BF16)
        for i, term in enumerate((low.astype(F32), n * xhat, n)):
            gvec_o[i : i + 1, :] += jnp.sum(term, axis=0, keepdims=True)
        mixed = mixv[at, :]
        gout[...] += dot_tn(mixed, low)
        dmix = dot_nt(low, projv[...]).astype(BF16)
        br[at, :] = dmix
        move(t, 2).start()
        prod = dmix.astype(F32) * mixed.astype(F32)
        high = prod.astype(BF16)
        rest = (prod - high.astype(F32)).astype(BF16)
        delta_o[:, at] = (dot_nt(heads, high) + dot_nt(heads, rest))[:8]
        return 0

    for t in range(tiles):
        last_tile(t, 0)
    if linked:
        block = gout[...].reshape(4, 2, 2, 2, 16, width)
        first, second = block[:, :, :, 0], block[:, :, :, 1]
        kept[:, :, :, 128:, :] = jnp.where(c == 0, first, second).astype(BF16)
        sent[:, :, :, 128:, :] = jnp.where(c == 0, second, first).astype(BF16)
        exchange(1).start()
        exchange(0).wait()
        exchange(1).wait()
        for i in range(4):
            got[i] = (got[i].astype(F32) + kept[i].astype(F32)).astype(BF16)
        for i in range(4):
            leave(i).start()
        for i in range(4):
            leave(i).wait()
    else:
        gout_o[...] = gout[...].astype(BF16)
    for t in range(tiles):
        for i in range(3):
            move(t, i).wait()


def feed(cuts, start, mixture, cotangent, w_out, vec, hid, weights, linked):
    count, width = start.shape
    hidden = hid.shape[1]
    rows = min(TILE, count)
    f = min(512, hidden)
    tiles = count // rows
    anywhere = pl.BlockSpec(memory_space=pl.ANY)
    inside = pl.BlockSpec(memory_space=pltpu.VMEM)
    big = lambda d: pltpu.VMEM((count, width), d)
    flat = lambda more=0: pltpu.VMEM((width + more, count), BF16)
    turning = pltpu.VMEM((width // 128, count + rows, 128), F32)
    lot = lambda *s: pltpu.SemaphoreType.DMA(s)
    scratch = (
        [big(F32), turning, big(F32), big(BF16), flat(16), big(BF16), flat(), big(BF16), pltpu.VMEM((width, width), BF16)]
        + [pltpu.VMEM((rows, f), BF16)] * 4
        + [pltpu.VMEM((width + 16, hidden), F32), pltpu.VMEM((width, hidden), F32)]
        + [pltpu.VMEM((width, width), F32), turning, pltpu.VMEM((count, 128), F32)]
        + [lot(width // 128, 2), lot(2 * tiles + 1), lot(3 * tiles)]
    )
    common = [
        jax.ShapeDtypeStruct((count, width), BF16),
        jax.ShapeDtypeStruct((count, width), F32),
        jax.ShapeDtypeStruct((count, width), BF16),
        jax.ShapeDtypeStruct((8, count), F32),
        jax.ShapeDtypeStruct((8, width), F32),
        jax.ShapeDtypeStruct((1, hidden), F32),
    ]
    if linked:
        weight_specs = [anywhere] * 4
        more = [jax.ShapeDtypeStruct((4, 144, width), BF16)] * 4
        more_specs = [anywhere] * 4
        scratch += [
            pltpu.VMEM((4, 2, 2, 2, 16, hidden), BF16), pltpu.VMEM((4, 2, 2, 2, 64, width), BF16),
        ] + [pltpu.VMEM((4, 2, 2, 144, width), BF16)] * 3 + [lot(4, 5), lot(4, 5), lot(4, 5), lot(2), lot(2), lot(4)]
        compiler = params(60 << 20, collective_id=1, has_side_effects=True)
    else:
        weight_specs = [inside] * 2
        more = [jax.ShapeDtypeStruct(s, BF16) for s in ((width, hidden), (hidden, width), (width, width))]
        more_specs = [inside] * 3
        compiler = params()
    return pl.pallas_call(
        functools.partial(feed_kernel, linked, rows, f),
        in_specs=[pl.BlockSpec(memory_space=pltpu.SMEM)] + [anywhere] * 4 + [inside] * 2 + weight_specs,
        out_specs=[anywhere] * 3 + [inside] * 3 + more_specs,
        out_shape=common + more,
        scratch_shapes=scratch,
        compiler_params=compiler,
        name="feed_forward",
    )(cuts, start, mixture, cotangent, w_out, vec, hid, *weights)


def in_pairs(count, body):
    def two(m, _):
        body(2 * m, 0)
        return body(2 * m + 1, 0)

    lax.fori_loop(0, count // 2, two, 0)
    if count % 2:
        body(count - 1, 0)


def leave_kernel(linked, cuts, dq, dk, dv, normt, w_in, start, gmid, stamps, flags, vec, gvec2, ghid, *refs):
    if linked:
        pieces = refs[:4]
        gtok_o, gin_o, gsmall_o, gfeed_o, gtab, gvec, land, esum, egot, esend, erecv, lsem = refs[4:16]
        places = [refs[16 + 7 * i : 23 + 7 * i] for i in range(4)]
        refs = refs[44:]
    else:
        gtok_o, gin_o, gtab, gvec = refs[:4]
        refs = refs[4:]
    grads, normv, startv, gmidv, weights, gtokf, gtokv, sem, tsem = refs
    count, width = start.shape
    rows = min(TILE, count)
    tiles = count // rows
    steps = gtab.shape[0] - 16
    fetches = {}

    def rows_at(t):
        return pl.ds(t * rows if isinstance(t, int) else pl.multiple_of(t * rows, rows), rows)

    def late(t, i):
        src, dst = ((start, startv), (gmid, gmidv))[i]
        return pltpu.make_async_copy(src.at[rows_at(t)], dst.at[rows_at(t)], tsem.at[2 * t + i])

    def fetch(name, src, dst):
        fetches[name] = pltpu.make_async_copy(src, dst, sem.at[len(fetches)])
        fetches[name].start()

    fetch("normed", normt, normv)
    fetch(0, dq, grads.at[0])
    fetch(1, dk, grads.at[1])
    gtab[...] = jnp.zeros_like(gtab)
    gvec[...] = jnp.zeros_like(gvec)
    if linked:
        place = position()
        z, x, y, c = place
        plans = [scatter_plan(place, *p) for p in places]

        def level(k):
            return remote(esum.at[peer(z, k)], egot.at[k - 1], esend.at[k - 1], erecv.at[k - 1],
                          device(peer(z, k), x, y, c))

        greet(*place)
        lands = [pltpu.make_async_copy(p, land.at[i], lsem.at[i]) for i, p in enumerate(pieces)]
        for copy in lands:
            copy.start()
    fetches["normed"].wait()
    for i in range(3):
        fetches[i].wait()
        total = dot(normv[...], grads[i]).astype(BF16)
        if linked:
            full = places[i][0]
            full[...] = total.reshape(full.shape)
            plans[i][0]()
            if i:
                plans[i - 1][1]()
        else:
            gin_o[:, width * i : width * i + width] = total
        if i == 0:
            fetch(2, dv, grads.at[2])
            fetch("weights", w_in, weights)
            if linked:
                for copy in lands:
                    copy.wait()
                for j in range(4):
                    parts = [land[k, j].astype(F32) for k in range(4)]
                    esum[j] = (parts[0] + parts[1] + parts[2] + parts[3]).astype(BF16)
                for k in (1, 2, 3):
                    level(k).start()
        elif i == 1:
            for t in range(tiles):
                late(t, 0).start()
                late(t, 1).start()
    fetches["weights"].wait()
    if linked:
        plans[2][1]()

    def norm_tile(t, _):
        at = rows_at(t)
        n = sum(dot_nt(grads[i, at, :], weights[i]) for i in range(3))
        late(t, 0).wait()
        late(t, 1).wait()
        xhat, rstd = norm_parts(startv[at, :])
        put_columns(gtokf, at, gmidv[at, :] + norm_back(n, xhat, rstd, vec[1:2, :]))
        gvec[0:1, :] += jnp.sum(n * xhat, axis=0, keepdims=True)
        gvec[1:2, :] += jnp.sum(n, axis=0, keepdims=True)
        return 0

    in_pairs(tiles, norm_tile)
    wrap_columns(gtokf, rows)

    def move(t):
        return pltpu.make_async_copy(gtokv.at[rows_at(t)], gtok_o.at[rows_at(t)], tsem.at[2 * tiles + t])

    def back_tile(t, _):
        at = rows_at(t)
        grad = turned(gtokf, rows * t - cuts[0], rows)
        gtokv[at, :] = grad
        move(t).start()
        gtab[...] += dot(token_selector(stamps[:, at], flags[:, at], steps), grad.astype(BF16))
        return 0

    in_pairs(tiles, back_tile)
    if linked:
        pack_small(places[3][0], steps, gtab, gvec, gvec2, ghid)
        plans[3][0]()
        plans[0][2]()
        plans[3][1]()
        plans[1][2]()
        plans[2][2]()
        for k in (1, 2, 3):
            level(k).wait_recv()
        gfeed_o[...] = (esum[z].astype(F32) + egot[0].astype(F32)) + (egot[1].astype(F32) + egot[2].astype(F32))
        plans[3][2]()
        for i in range(3):
            plans[i][3](gin_o, width * i)
        plans[3][3](gsmall_o, 0)
        for plan in plans:
            plan[4]()
        for k in (1, 2, 3):
            level(k).wait_send()
    for t in range(tiles):
        move(t).wait()


def pack_small(full, steps, gtab, gvec, gvec2, ghid):
    width = gtab.shape[1]
    groups = steps // 8
    per = width // groups
    sums = [gtab[steps : steps + 1, :], gvec[0:1, :], gvec[1:2, :]]
    sums += [gvec2[i : i + 1, :] for i in range(4)]
    mine = iota((groups, width), 1) // per == iota((groups, width), 0)
    spread = jnp.concatenate([jnp.where(mine, v, 0.0) for v in sums], 0).astype(BF16)
    same = (iota((width, width), 0) % per == iota((width, width), 1) % per).astype(BF16)
    wide = dot(spread, same).reshape(7, groups, width)
    lane = iota((1, width), 1)
    row = jnp.zeros((groups, width), F32)
    for i in range(7):
        row = jnp.where(lane // per == i, wide[i], row)
    hidden = ghid.shape[1]
    part = hidden // groups
    own = iota((groups, hidden), 1) // part == iota((groups, hidden), 0)
    pick = (iota((hidden, width), 0) % part == iota((hidden, width), 1) - 7 * per).astype(BF16)
    row = row + dot(jnp.where(own, ghid[...], 0.0).astype(BF16), pick)
    table = gtab[:steps, :].reshape(groups, 8, width)
    full[...] = pack_block(table, row[:, None, : 2 * SIDE]).astype(BF16).reshape(full.shape)


def leave(cuts, dq, dk, dv, normt, w_in, start, gmid, stamps, flags, vec, gvec2, ghid, steps, pieces, linked):
    count, width = start.shape
    rows = min(TILE, count)
    tiles = count // rows
    lot = lambda *s: pltpu.SemaphoreType.DMA(s)
    anywhere = pl.BlockSpec(memory_space=pl.ANY)
    inside = pl.BlockSpec(memory_space=pltpu.VMEM)
    sums = [jax.ShapeDtypeStruct((steps + 16, width), F32), jax.ShapeDtypeStruct((8, width), F32)]
    if linked:
        more = [jax.ShapeDtypeStruct(s, F32) for s in ((16, 3 * width), (16, width // 2 + SIDE), (144, width))]
        scratch = [pltpu.VMEM(a.shape, F32) for a in sums]
        scratch += [pltpu.VMEM(n + (144, width), BF16) for n in ((4, 4), (4,), (3,))] + [lot(3), lot(3), lot(4)]
        for w in (width, width, width, width // 2 + SIDE):
            scratch += scatter_buffers(16, w) + [lot(SCATTER_SLOTS), lot(SCATTER_SLOTS)]
        compiler = params(collective_id=2, has_side_effects=True)
    else:
        more = [jax.ShapeDtypeStruct((width, 3 * width), BF16)] + sums
        scratch = []
        compiler = params()
    big = lambda d: pltpu.VMEM((count, width), d)
    return pl.pallas_call(
        functools.partial(leave_kernel, linked),
        in_specs=[pl.BlockSpec(memory_space=pltpu.SMEM)] + [anywhere] * 7 + [inside] * 5 + [anywhere] * len(pieces),
        out_specs=[anywhere] + [inside] * len(more),
        out_shape=[jax.ShapeDtypeStruct((count, width), F32)] + more,
        scratch_shapes=scratch + [
            pltpu.VMEM((3, count, width), BF16), pltpu.VMEM((width, count), BF16), big(F32), big(F32),
            pltpu.VMEM((3, width, width), BF16), pltpu.VMEM((width // 128, count + rows, 128), F32), big(F32),
            lot(5), lot(3 * tiles),
        ],
        compiler_params=compiler,
        name="leave",
    )(cuts, dq, dk, dv, normt, w_in, start, gmid, stamps, flags, vec, gvec2, ghid, *pieces)


def unpack_kernel(sizes, gtok, gin, gsmall, gfeed, gtok_o, gin_o, gtab_o, gout_o, gup_o, gdown_o, *refs):
    *vecs, held, there, back = refs
    parts = there.shape[0]
    rows = gtok.shape[0] // parts
    spans = [pl.ds(rows * i, rows) for i in range(parts)]
    reads = [pltpu.make_async_copy(gtok.at[at], held.at[at], there.at[i]) for i, at in enumerate(spans)]
    writes = [pltpu.make_async_copy(held.at[at], gtok_o.at[at], back.at[i]) for i, at in enumerate(spans)]
    for copy in reads:
        copy.start()
    for i in range(parts):
        reads[i].wait()
        writes[i].start()
        if i == 0:
            unpack_rest(sizes, gin, gsmall, gfeed, gin_o, gtab_o, gout_o, gup_o, gdown_o, *vecs)
    for copy in writes:
        copy.wait()


def unpack_rest(sizes, gin, gsmall, gfeed, gin_o, gtab_o, gout_o, gup_o, gdown_o, *vecs):
    width = gtab_o.shape[1]
    half = width // 2
    gin_o[...] = gin[...]
    gtab_o[:, :half] = gsmall[:8, :half]
    gtab_o[:, half:] = gsmall[8:, :half]
    row = jnp.concatenate([gsmall[0:1, half:], gsmall[1:2, half:]], 1)
    gdown_o[...] = gfeed[:64, :]
    for i in range(gup_o.shape[1] // width):
        gup_o[:, width * i : width * (i + 1)] = gfeed[64 + 16 * i : 80 + 16 * i, :]
    gout_o[...] = gfeed[128:144, :]
    at = 0
    for ref, size in zip(vecs, sizes):
        ref[...] = row[:, at : at + size]
        at += size


def unpack(gtok, gin, gsmall, gfeed, hidden, sizes):
    width = gfeed.shape[1]
    shapes = [gtok.shape, gin.shape, (8, width), (16, width), (16, hidden), (64, width)] + [(1, n) for n in sizes]
    anywhere = pl.BlockSpec(memory_space=pl.ANY)
    inside = pl.BlockSpec(memory_space=pltpu.VMEM)
    parts = 8
    return pl.pallas_call(
        functools.partial(unpack_kernel, sizes),
        in_specs=[anywhere] + [inside] * 3,
        out_specs=[anywhere] + [inside] * (len(shapes) - 1),
        out_shape=[jax.ShapeDtypeStruct(s, F32) for s in shapes],
        scratch_shapes=[pltpu.VMEM(gtok.shape, F32), pltpu.SemaphoreType.DMA((parts,)), pltpu.SemaphoreType.DMA((parts,))],
        compiler_params=params(),
        name="unpack",
    )(gtok, gin, gsmall, gfeed)


def exchange_plane(arrays):
    out = [arrays[0]]
    for array, (dx, dy) in zip(arrays[1:], ((1, 0), (0, 1), (1, 1))):
        pairs = [(4 * dp + fs, 4 * (dp ^ dx) + (fs ^ (2 * dy))) for dp in range(8) for fs in range(4)]
        out.append(lax.ppermute(array, AXES, pairs))
    return out


def per_device(fast, tokens, mask_flags, timesteps, segment_ids, mask_embed, time_table, first_gain, first_bias,
               input_proj, output_proj, output_bias, second_gain, second_bias, hidden_weight, hidden_bias,
               down_weight, down_bias, cotangent):
    count, width = tokens.shape
    hidden = hidden_weight.shape[1]
    vectors = (mask_embed, first_gain, first_bias, output_bias, second_gain, second_bias, down_bias)
    segments = segment_ids.reshape(-1)
    stamps, flags = timesteps[None], mask_flags[None]
    if fast:
        lines = [v[None] for v in vectors + (hidden_bias,)]
        sizes = [v.shape[1] for v in lines]
        shards = lines + [time_table, input_proj, output_proj, hidden_weight, down_weight]
        *kept, w_in, w_out, own = enter(tokens, segments, stamps, flags, hidden, shards, None, None)
        w_in, w_out = w_in.reshape(3, width, width), w_out.reshape(width, width)
        steps = time_table.shape[0] * 32
        weights = exchange_plane([own] * 4)
    else:
        whole = lambda a: lax.all_gather(a, AXES, axis=0, tiled=True)
        groups = whole(time_table).reshape(-1, 8, width)
        pieces = jnp.concatenate(
            [whole(v).reshape(groups.shape[0], -1) for v in vectors + (hidden_bias,)], 1
        )
        pieces = jnp.pad(pieces, ((0, 0), (0, 2 * SIDE - pieces.shape[1])))[:, None]
        small = pack_block(groups.astype(F32), pieces.astype(F32)).astype(BF16)
        w_in, w_out = whole(input_proj), whole(output_proj)
        weights = [whole(hidden_weight), whole(down_weight)]
        steps = groups.shape[0] * 8
        kept = enter(tokens, segments, stamps, flags, hidden, None, small, w_in)
        w_in = w_in.reshape(width, 3, width).transpose(1, 0, 2)
    start, normt, packed, mq, mk, vec, hid, cuts = kept

    mixture, lse = attention_forward(packed, cuts, mq, mk, 256, 4)
    out, gmid, dmix, delta, gvec2, ghid, *grads = feed(cuts, start, mixture, cotangent, w_out, vec, hid, weights, fast)
    pieces = exchange_plane(grads) if fast else []
    dq, dk, dv, out = attention_backward(packed, dmix, cuts, mq, mk, lse, delta, out, 256, 4)
    gtok, gin, *rest = leave(
        cuts, dq, dk, dv, normt, w_in, start, gmid, stamps, flags, vec, gvec2, ghid, steps, pieces, fast
    )
    if fast:
        gtok, gin, gtab, gout, gup, gdown, *small = unpack(gtok, gin, rest[0], rest[1], hidden, sizes)
        gmask, gg1, gb1, gob, gg2, gb2, gdb, ghb = [v.reshape(-1) for v in small]
    else:
        total = lambda a: lax.psum_scatter(a.astype(F32), AXES, scatter_dimension=0, tiled=True)
        gtab, gvec1 = rest
        gup, gdown, gout = grads
        gin, gout, gup, gdown = (total(a) for a in (gin, gout, gup, gdown))
        gmask = total(gtab[steps])
        gtab = total(gtab[:steps])
        gg1, gb1, gob, gg2, gb2, gdb, ghb = (
            total(a) for a in (gvec1[0], gvec1[1], gvec2[0], gvec2[1], gvec2[2], gvec2[3], ghid[0])
        )
    return (out, gtok, gmask, gtab, gg1, gb1, gin, gout, gob, gg2, gb2, gup, ghb, gdown, gdb)


def solution(mesh):
    split = P(AXES)
    rows = P(AXES, None)
    fast = tuple(mesh.shape[a] for a in AXES) == (8, 4)
    placed = (rows, split, split, rows, split, rows, split, split, rows, rows, split, split, split, rows, split, rows,
              split, rows)
    return jax.shard_map(
        functools.partial(per_device, fast),
        mesh=mesh,
        in_specs=placed,
        out_specs=(rows, rows, split, rows, split, split, rows, rows, split, split, split, rows, split, rows, split),
        check_vma=False,
    )
```
